32 devices in a mesh: clip: 2 (over y), fp: 4 (over z), tp: 4 (over x, core).
Axes of the slice: x: 2, y: 2, z: 4, core: 2. Of those that a mesh axis runs over, the one named last changes fastest.
Arguments:
- inputs: bfloat16 [2, 8, 16, 192, 768], P(None, 'clip', 'fp', 'tp'), may hold values from -6 to 6
- cotangent: bfloat16 [2, 8, 16, 192, 768], P(None, 'clip', 'fp', 'tp'), may hold values from -6 to 6
- qkv_weight: bfloat16 [2, 3, 768, 768], P(None, None, ('clip', 'fp'), 'tp'), may hold values from -0.21875 to 0.21875
- out_spatial: bfloat16 [768, 768], P('tp', ('clip', 'fp')), may hold values from -1.5 to 1.5
- out_temporal: bfloat16 [768, 768], P('tp', ('clip', 'fp')), may hold values from -0.4375 to 0.4375
- mlp_in: bfloat16 [768, 3072], P(('clip', 'fp'), 'tp'), may hold values from -0.21875 to 0.21875
- mlp_out: bfloat16 [3072, 768], P('tp', ('clip', 'fp')), may hold values from -0.15625 to 0.15625
- ln_gain: bfloat16 [3, 768], P(None, ('clip', 'fp')), may hold values from 0.5 to 1.5
- ln_bias: bfloat16 [3, 768], P(None, ('clip', 'fp')), may hold values from -2 to 2
Outputs:
- activations: bfloat16 [2, 8, 16, 192, 768], P(None, 'clip', 'fp', 'tp')
- input_grad: float32 [2, 8, 16, 192, 768], P(None, 'clip', 'fp', 'tp')
- qkv_grad: float32 [2, 3, 768, 768], P(None, None, ('clip', 'fp'), 'tp')
- out_spatial_grad: float32 [768, 768], P('tp', ('clip', 'fp'))
- out_temporal_grad: float32 [768, 768], P('tp', ('clip', 'fp'))
- mlp_in_grad: float32 [768, 3072], P(('clip', 'fp'), 'tp')
- mlp_out_grad: float32 [3072, 768], P('tp', ('clip', 'fp'))
- ln_gain_grad: float32 [3, 768], P(None, ('clip', 'fp'))
- ln_bias_grad: float32 [3, 768], P(None, ('clip', 'fp'))
The draws below stay inside these ranges and needn't reach their ends.
All inputs are finite; a program needn't handle non-finite values.
Results may differ from the reference program's by a relative error of at most 0.014.
Values may be sent and summed in bfloat16 or wider, within the bound.
A program may use at most 320 MiB of HBM per device.

```python
from functools import partial
import jax
import jax.numpy as jnp
from jax import lax

D = 768
HEADS = 12
HD = 64
FF = 3072
FRAMES = 16
PLACES = 192
MICRO = 2
CLIPS = 8


def block_scale(own_key, extent, shards, low, top_value):
    factor_of = 1.0
    for axis_at, shards_of in shards:
        steps = jax.random.uniform(jax.random.fold_in(jax.random.fold_in(own_key, 6), axis_at), (shards_of,), jnp.float32, low / len(shards), top_value / len(shards))
        factor_of = factor_of * jnp.repeat(jnp.exp(steps), extent[axis_at] // shards_of).reshape((-1,) + (1,) * (len(extent) - 1 - axis_at))
    return factor_of


def normal_values(rng, dims, scale, most, cuts=(), held_as=jnp.bfloat16):
    level = block_scale(rng, dims, cuts, -0.22, 0.18) if cuts else 1.0
    values = jax.random.normal(rng, dims, jnp.float32) * scale * level
    return jnp.minimum(jnp.maximum(values, -most), most).astype(held_as)


def setup_inputs(seed: int = 0) -> dict:
    seeds = jax.random.split(jax.random.key(seed), 10)
    return {
        "inputs": normal_values(seeds[0], (MICRO, CLIPS, FRAMES, PLACES, D), 1.0, 6.0, ((1, 2), (2, 4), (3, 4))),
        "cotangent": normal_values(seeds[1], (MICRO, CLIPS, FRAMES, PLACES, D), 1.0, 6.0, ((1, 2), (2, 4), (3, 4))),
        "qkv_weight": normal_values(seeds[2], (2, 3, D, HEADS * HD), D ** -0.5, 0.21875, ((2, 8), (3, 4))),
        "out_spatial": normal_values(seeds[3], (HEADS * HD, D), (HEADS * HD * 4 // PLACES) ** -0.5, 1.5, ((0, 4), (1, 8))),
        "out_temporal": normal_values(seeds[4], (HEADS * HD, D), (HEADS * HD * 4 // FRAMES) ** -0.5, 0.4375, ((0, 4), (1, 8))),
        "mlp_in": normal_values(seeds[5], (D, FF), D ** -0.5, 0.21875, ((0, 8), (1, 4))),
        "mlp_out": normal_values(seeds[6], (FF, D), (FF // 2) ** -0.5, 0.15625, ((0, 4), (1, 8))),
        "ln_gain": jnp.clip(1.0 + 0.1 * jax.random.normal(seeds[7], (3, D), jnp.float32), 0.5, 1.5).astype(jnp.bfloat16),
        "ln_bias": normal_values(seeds[8], (3, D), 0.3, 2.0, ((1, 8),)),
    }


epsilon = 1e-06
highest = lax.Precision.HIGHEST
space_forms = ('cfphe,cfqhe->cfhpq', 'cfhpq,cfqhe->cfphe', 'cfhpq,cfphe->cfqhe')
time_forms = ('cfphe,cgphe->cphfg', 'cphfg,cgphe->cfphe', 'cphfg,cfphe->cgphe')

@jax.custom_vjp
def low(v):
    return lax.optimization_barrier(v.astype(jnp.bfloat16)).astype(jnp.float32)

@jax.custom_vjp
def low_back(v):
    return v

def low_keep(v):
    return (low(v), None)

def low_pass(kept, grad):
    return (grad,)

def back_keep(v):
    return (v, None)

def back_low(kept, grad):
    return (low(grad),)
low.defvjp(low_keep, low_pass)
low_back.defvjp(back_keep, back_low)

def round_both(value):
    return low(low_back(value))

def layer_norm(values, norm_gain, norm_shift):
    centre = values - lax.optimization_barrier(jnp.mean(values, axis=-1, keepdims=True))
    spread = lax.optimization_barrier(jnp.mean(centre * centre, axis=-1, keepdims=True))
    return centre * lax.rsqrt(spread + epsilon) * norm_gain + norm_shift

def attention(normed, qkv_full, out_weight, einsum_forms):
    qkv_all = round_both(jnp.einsum('cfpd,ide->icfpe', normed, qkv_full, precision=highest))
    qkv_all = qkv_all.reshape(qkv_all.shape[:-1] + (HEADS, HD))
    scores = low_back(jnp.einsum(einsum_forms[0], qkv_all[0], qkv_all[1], precision=highest)) * HD ** (-0.5)
    weights = low(jax.nn.softmax(scores, axis=-1))
    mixed_heads = round_both(jnp.einsum(einsum_forms[1], weights, qkv_all[2], precision=highest))
    mixed_heads = mixed_heads.reshape(mixed_heads.shape[:-2] + (HEADS * HD,))
    return low_back(jnp.einsum('cfpe,ed->cfpd', mixed_heads, out_weight, precision=highest))

def clip_layer(one_clip, params):
    qkv_full, out_space, out_time, weight_in, weight_out, norm_gains, norm_shifts = params
    layer_input = one_clip[None]
    after_space = layer_input + attention(low(layer_norm(layer_input, norm_gains[0], norm_shifts[0])), qkv_full[0], out_space, space_forms)
    after_time = after_space + attention(low(layer_norm(after_space, norm_gains[1], norm_shifts[1])), qkv_full[1], out_time, time_forms)
    normed_mlp = low(layer_norm(after_time, norm_gains[2], norm_shifts[2]))
    hidden_pre = low_back(jnp.einsum('cfpd,de->cfpe', normed_mlp, weight_in, precision=highest))
    hidden = low(jax.nn.gelu(hidden_pre, approximate=False))
    result = after_time + low_back(jnp.einsum('cfpe,ed->cfpd', hidden, weight_out, precision=highest))
    return result[0]

def forward(inputs_wide, params):
    clip_rows = inputs_wide.reshape((-1,) + inputs_wide.shape[2:])
    results = lax.map(jax.checkpoint(partial(clip_layer, params=params)), clip_rows)
    return results.reshape(inputs_wide.shape)

def reference(inputs, cotangent, qkv_weight, out_spatial, out_temporal, mlp_in, mlp_out, ln_gain, ln_bias):
    params = (qkv_weight.astype(jnp.float32), out_spatial.astype(jnp.float32), out_temporal.astype(jnp.float32), mlp_in.astype(jnp.float32), mlp_out.astype(jnp.float32), ln_gain.astype(jnp.float32), ln_bias.astype(jnp.float32))
    result, pullback = jax.vjp(forward, inputs.astype(jnp.float32), params)
    grad_input, grad_params = pullback(cotangent.astype(jnp.float32))
    return (result.astype(jnp.bfloat16), grad_input, grad_params[0], grad_params[1], grad_params[2], grad_params[3], grad_params[4], grad_params[5], grad_params[6])
```

```python
from functools import partial

import jax
import jax.numpy as jnp
from jax import lax
from jax.experimental import pallas as pl
from jax.experimental.pallas import tpu as pltpu
from jax.sharding import PartitionSpec as P

HD = 64
GROUP = 4
WIDE = GROUP * HD
EPS = 1e-06
BF = jnp.bfloat16
F32 = jnp.float32
MIB = 1024 * 1024

NN = (((1,), (0,)), ((), ()))
NT = (((1,), (1,)), ((), ()))
TN = (((0,), (0,)), ((), ()))


def dot(a, b, dims):
    return lax.dot_general(a, b, dims, preferred_element_type=F32)


def normalise(values):
    centre = values - jnp.mean(values, axis=-1, keepdims=True)
    spread = jnp.mean(centre * centre, axis=-1, keepdims=True)
    rate = lax.rsqrt(spread + EPS)
    return centre * rate, rate


def norm_back(upstream, gain, unit, rate):
    weighted = upstream * gain
    inner = jnp.mean(weighted * unit, axis=-1, keepdims=True)
    return rate * (weighted - jnp.mean(weighted, axis=-1, keepdims=True) - unit * inner)


def head_masks(scale):
    lanes = lax.broadcasted_iota(jnp.int32, (1, WIDE), 1) // HD
    return [jnp.where(lanes == h, scale, 0.0).astype(BF) for h in range(GROUP)]


def spread_heads(block, masks):
    return jnp.concatenate([block * mask for mask in masks], axis=0)


def gather_heads(stacked, rows):
    lanes = lax.broadcasted_iota(jnp.int32, (1, WIDE), 1) // HD
    total = stacked[:rows]
    for h in range(1, GROUP):
        total = jnp.where(lanes == h, stacked[h * rows : (h + 1) * rows], total)
    return total


def attend(queries, keys, values, bias):
    rows = queries.shape[0]
    scores = dot(keys, spread_heads(queries, head_masks(HD**-0.5)), NT)
    if bias is not None:
        scores = scores + bias
    top = jnp.max(scores, axis=0, keepdims=True)
    exponent = jnp.exp(scores - top)
    totals = jnp.sum(exponent, axis=0, keepdims=True)
    weights = (exponent * (1.0 / totals)).astype(BF)
    mixed = gather_heads(dot(weights, values, TN), rows).astype(BF)
    return mixed, top + jnp.log(totals)


def attend_back(queries, keys, values, upstream, logsum, bias):
    rows = queries.shape[0]
    spread_q = spread_heads(queries, head_masks(HD**-0.5))
    spread_g = spread_heads(upstream, head_masks(1.0))
    scores = dot(keys, spread_q, NT)
    if bias is not None:
        scores = scores + bias
    probs = jnp.exp(scores - logsum)
    grad_probs = dot(values, spread_g, NT)
    inner = jnp.sum(probs * grad_probs, axis=0, keepdims=True)
    grad_scores = (probs * (grad_probs - inner)).astype(BF)
    grad_values = dot(probs.astype(BF), spread_g, NN)
    grad_keys = dot(grad_scores, spread_q, NN)
    grad_queries = gather_heads(dot(grad_scores, keys, TN), rows) * HD**-0.5
    return grad_queries.astype(BF), grad_keys.astype(BF), grad_values.astype(BF)


def gelu_parts(pre):
    size = jnp.abs(pre) * (0.5**0.5)
    t = 1.0 / (1.0 + 0.3275911 * size)
    bell = jnp.exp(-size * size)
    poly = t * (
        0.254829592
        + t * (-0.284496736 + t * (1.421413741 + t * (-1.453152027 + t * 1.061405429)))
    )
    tail = 0.5 * poly * bell
    return jnp.where(pre >= 0, 1.0 - tail, tail), bell * 0.3989422804014327


def space_forward_kernel(n_in, n_out, at_ref, *refs):
    pieces = refs[:n_in]
    qkv_w, out_w, norm = refs[n_in : n_in + 3]
    outs = refs[n_in + 3 : n_in + 3 + n_out]
    qkv_out, mixed_out, logsum_out, held = refs[n_in + 3 + n_out :]
    width = out_w.shape[1]
    x = jnp.concatenate([piece[0] for piece in pieces], axis=0).astype(F32)
    unit, _ = normalise(x)
    normed = (unit * norm[0:1] + norm[1:2]).astype(BF)
    qkv_out[0] = dot(normed, qkv_w[...], NN).astype(BF)
    for g in range(width // WIDE):
        at = g * WIDE
        mixed, logsum = attend(
            qkv_out[0, :, at : at + WIDE],
            qkv_out[0, :, width + at : width + at + WIDE],
            qkv_out[0, :, 2 * width + at : 2 * width + at + WIDE],
            None,
        )
        mixed_out[0, :, at : at + WIDE] = mixed
        logsum_out[0, g : g + 1] = logsum
    held[...] = x + dot(mixed_out[0], out_w[...], NT)
    rows = outs[0].shape[1]
    for r, out in enumerate(outs):
        start = pl.multiple_of((at_ref[0] ^ r) * rows, 8)
        out[0] = held[pl.ds(start, rows), :].astype(BF)


def space_forward(pieces, qkv_w, out_w, norm, at, n_out):
    frames, rows, width = pieces[0].shape
    places = rows * len(pieces)
    groups = width // WIDE
    whole = pl.BlockSpec(memory_space=pltpu.VMEM)
    frame = lambda *dims: pl.BlockSpec((1,) + dims, lambda f, at: (f,) + (0,) * len(dims))
    return pl.pallas_call(
        partial(space_forward_kernel, len(pieces), n_out),
        grid_spec=pltpu.PrefetchScalarGridSpec(
            num_scalar_prefetch=1,
            grid=(frames,),
            in_specs=[frame(rows, width)] * len(pieces) + [whole] * 3,
            out_specs=[frame(places // n_out, width)] * n_out
            + [frame(places, 3 * width), frame(places, width), frame(groups, GROUP * places)],
            scratch_shapes=[pltpu.VMEM((places, width), F32)],
        ),
        out_shape=[jax.ShapeDtypeStruct((frames, places // n_out, width), BF)] * n_out
        + [
            jax.ShapeDtypeStruct((frames, places, 3 * width), BF),
            jax.ShapeDtypeStruct((frames, places, width), BF),
            jax.ShapeDtypeStruct((frames, groups, GROUP * places), F32),
        ],
        compiler_params=pltpu.CompilerParams(vmem_limit_bytes=48 * MIB),
        cost_estimate=pl.CostEstimate(
            flops=2 * frames * places * width * 5 * width,
            bytes_accessed=frames * places * width * 16,
            transcendentals=0,
        ),
    )(at, *pieces, qkv_w, out_w, norm)


def store_columns(out, kinds, n_parts):
    width = kinds[0].shape[1]
    span = width // n_parts
    for t in range(n_parts):
        for i, kind in enumerate(kinds):
            start = (t * len(kinds) + i) * span
            out[:, start : start + span] = kind[:, t * span : (t + 1) * span]


def space_backward_kernel(n_in, n_grad, at_ref, *refs):
    pieces = refs[:n_in]
    grads = refs[n_in : n_in + n_grad]
    qkv_in, mixed_in, logsum_in, qkv_w, out_w, norm = refs[n_in + n_grad : n_in + n_grad + 6]
    rest = refs[n_in + n_grad + 6 :]
    outs = rest[:n_in]
    normed_out, grad_out, columns, norm_out, held, dqkv = rest[n_in:]
    width = out_w.shape[1]
    rows = grads[0].shape[1]
    for r, grad in enumerate(grads):
        start = pl.multiple_of((at_ref[0] ^ r) * rows, 8)
        held[pl.ds(start, rows), :] = grad[0].astype(F32)
    x = jnp.concatenate([piece[0] for piece in pieces], axis=0).astype(F32)
    unit, rate = normalise(x)
    normed_out[0] = (unit * norm[0:1] + norm[1:2]).astype(BF)
    low = held[...].astype(BF)
    grad_out[0] = low
    grad_mixed = dot(low, out_w[...], NN).astype(BF)
    for g in range(width // WIDE):
        at = g * WIDE
        parts = attend_back(
            qkv_in[0, :, at : at + WIDE],
            qkv_in[0, :, width + at : width + at + WIDE],
            qkv_in[0, :, 2 * width + at : 2 * width + at + WIDE],
            grad_mixed[:, at : at + WIDE],
            logsum_in[0, g : g + 1],
            None,
        )
        for i, part in enumerate(parts):
            dqkv[:, i * width + at : i * width + at + WIDE] = part
    store_columns(
        columns.at[0],
        [dqkv[:, i * width : (i + 1) * width] for i in range(3)] + [mixed_in[0]],
        n_in,
    )
    grad_normed = dot(dqkv[...], qkv_w[...], NT)

    @pl.when(pl.program_id(0) == 0)
    def _():
        norm_out[...] = jnp.zeros_like(norm_out)

    norm_out[0:1] += jnp.sum(grad_normed * unit, axis=0, keepdims=True)
    norm_out[1:2] += jnp.sum(grad_normed, axis=0, keepdims=True)
    total = held[...] + norm_back(grad_normed, norm[0:1], unit, rate)
    rows = outs[0].shape[1]
    for s, out in enumerate(outs):
        out[0] = total[s * rows : (s + 1) * rows].astype(BF)


def space_backward(pieces, grads, qkv, mixed, logsum, qkv_w, out_w, norm, at):
    frames, rows, width = pieces[0].shape
    places = rows * len(pieces)
    groups = width // WIDE
    n_grad = len(grads)
    whole = pl.BlockSpec(memory_space=pltpu.VMEM)
    frame = lambda *dims: pl.BlockSpec((1,) + dims, lambda f, at: (f,) + (0,) * len(dims))
    return pl.pallas_call(
        partial(space_backward_kernel, len(pieces), n_grad),
        grid_spec=pltpu.PrefetchScalarGridSpec(
            num_scalar_prefetch=1,
            grid=(frames,),
            in_specs=[frame(rows, width)] * len(pieces)
            + [frame(places // n_grad, width)] * n_grad
            + [frame(places, 3 * width), frame(places, width), frame(groups, GROUP * places)]
            + [whole] * 3,
            out_specs=[frame(rows, width)] * len(pieces)
            + [frame(places, width), frame(places, width), frame(places, 4 * width)]
            + [pl.BlockSpec((2, width), lambda f, at: (0, 0))],
            scratch_shapes=[
                pltpu.VMEM((places, width), F32),
                pltpu.VMEM((places, 3 * width), BF),
            ],
        ),
        out_shape=[jax.ShapeDtypeStruct((frames, rows, width), BF)] * len(pieces)
        + [
            jax.ShapeDtypeStruct((frames, places, width), BF),
            jax.ShapeDtypeStruct((frames, places, width), BF),
            jax.ShapeDtypeStruct((frames, places, 4 * width), BF),
            jax.ShapeDtypeStruct((2, width), F32),
        ],
        compiler_params=pltpu.CompilerParams(vmem_limit_bytes=48 * MIB),
        cost_estimate=pl.CostEstimate(
            flops=2 * frames * places * width * 7 * width,
            bytes_accessed=frames * places * width * 24,
            transcendentals=0,
        ),
    )(at, *pieces, *grads, qkv, mixed, logsum, qkv_w, out_w, norm)


def time_kernel(n_in, n_parts, sub, *refs):
    pieces = refs[:n_in]
    cots = refs[n_in : 2 * n_in]
    qkv_w, out_w, in_w, unit_w, norm = refs[2 * n_in : 2 * n_in + 5]
    rest = refs[2 * n_in + 5 :]
    results = rest[:n_in]
    grads = rest[n_in : 2 * n_in]
    (
        normed_time,
        columns,
        grad_time,
        normed_mlp,
        grad_pre,
        hidden,
        grad_result,
        norm_out,
        qkv,
        dqkv,
        mixed,
        probs_logsum,
    ) = rest[2 * n_in :]
    width = out_w.shape[1]
    frames, places = pieces[0].shape[:2]
    all_frames = frames * n_in
    rows = all_frames * sub
    parts = places // sub

    def tokens(blocks):
        joined = jnp.concatenate([b[...] for b in blocks], axis=0).astype(F32)
        return jnp.concatenate(
            [joined[:, j * sub : (j + 1) * sub, :].reshape(rows, width) for j in range(parts)],
            axis=0,
        )

    def scatter(values, outs):
        grid = jnp.concatenate(
            [
                values[j * rows : (j + 1) * rows].reshape(all_frames, sub, width)
                for j in range(parts)
            ],
            axis=1,
        ).astype(BF)
        for r, out in enumerate(outs):
            out[...] = grid[r * frames : (r + 1) * frames]

    key_place = lax.broadcasted_iota(jnp.int32, (rows, GROUP * rows), 0) % sub
    query_place = lax.broadcasted_iota(jnp.int32, (rows, GROUP * rows), 1) % sub
    bias = jnp.where(key_place == query_place, 0.0, -1e30)

    after_space = tokens(pieces)
    unit, rate = normalise(after_space)
    normed_time[...] = (unit * norm[2:3] + norm[3:4]).astype(BF)
    qkv[...] = dot(normed_time[...], qkv_w[...], NN).astype(BF)
    groups = width // WIDE
    for j in range(parts):
        at_rows = slice(j * rows, (j + 1) * rows)
        for g in range(groups):
            at = g * WIDE
            out, logsum = attend(
                qkv[at_rows, at : at + WIDE],
                qkv[at_rows, width + at : width + at + WIDE],
                qkv[at_rows, 2 * width + at : 2 * width + at + WIDE],
                bias,
            )
            mixed[at_rows, at : at + WIDE] = out
            probs_logsum[j * groups + g : j * groups + g + 1] = logsum
    after_time = after_space + dot(mixed[...], out_w[...], NT)
    unit2, rate2 = normalise(after_time)
    normed_mlp[...] = (unit2 * norm[4:5] + norm[5:6]).astype(BF)
    cot = tokens(cots)
    grad_result[...] = cot.astype(BF)
    result = after_time
    grad_normed = None
    for c in range(in_w.shape[0]):
        cols = slice(c * in_w.shape[2], (c + 1) * in_w.shape[2])
        pre = dot(normed_mlp[...], in_w[c], NN)
        below, density = gelu_parts(pre)
        hidden[:, cols] = (pre * below).astype(BF)
        result = result + dot(hidden[:, cols], unit_w[c], NT)
        grad_hidden = dot(grad_result[...], unit_w[c], NN)
        grad_pre[:, cols] = (grad_hidden * (below + pre * density)).astype(BF)
        term = dot(grad_pre[:, cols], in_w[c], NT)
        grad_normed = term if c == 0 else grad_normed + term
    scatter(result, results)

    @pl.when(pl.program_id(0) == 0)
    def _():
        norm_out[...] = jnp.zeros_like(norm_out)

    norm_out[2:3] += jnp.sum(grad_normed * unit2, axis=0, keepdims=True)
    norm_out[3:4] += jnp.sum(grad_normed, axis=0, keepdims=True)
    grad_after = cot + norm_back(grad_normed, norm[4:5], unit2, rate2)
    grad_time[...] = grad_after.astype(BF)
    grad_mixed = dot(grad_time[...], out_w[...], NN).astype(BF)
    for j in range(parts):
        at_rows = slice(j * rows, (j + 1) * rows)
        for g in range(groups):
            at = g * WIDE
            back = attend_back(
                qkv[at_rows, at : at + WIDE],
                qkv[at_rows, width + at : width + at + WIDE],
                qkv[at_rows, 2 * width + at : 2 * width + at + WIDE],
                grad_mixed[at_rows, at : at + WIDE],
                probs_logsum[j * groups + g : j * groups + g + 1],
                bias,
            )
            for i, part in enumerate(back):
                dqkv[at_rows, i * width + at : i * width + at + WIDE] = part
    store_columns(
        columns,
        [dqkv[:, i * width : (i + 1) * width] for i in range(3)] + [mixed[...]],
        n_parts,
    )
    grad_normed = dot(dqkv[...], qkv_w[...], NT)
    norm_out[0:1] += jnp.sum(grad_normed * unit, axis=0, keepdims=True)
    norm_out[1:2] += jnp.sum(grad_normed, axis=0, keepdims=True)
    scatter(grad_after + norm_back(grad_normed, norm[2:3], unit, rate), grads)


def time_layer(pieces, cots, qkv_w, out_w, in_w, unit_w, norm):
    frames, places, width = pieces[0].shape
    n_in = len(pieces)
    block = 16 if places % 16 == 0 else 8
    sub = 8
    tokens = frames * n_in * block
    count = frames * n_in * places
    hidden = in_w.shape[0] * in_w.shape[2]
    whole = pl.BlockSpec(memory_space=pltpu.VMEM)
    piece = pl.BlockSpec((frames, block, width), lambda b: (0, b, 0))
    row = lambda cols: pl.BlockSpec((tokens, cols), lambda b: (b, 0))
    kept = [width, 4 * width, width, width, hidden, hidden, width]
    return pl.pallas_call(
        partial(time_kernel, n_in, in_w.shape[0], sub),
        grid=(places // block,),
        in_specs=[piece] * (2 * n_in) + [whole] * 5,
        out_specs=[piece] * (2 * n_in)
        + [row(cols) for cols in kept]
        + [pl.BlockSpec((4, width), lambda b: (0, 0))],
        out_shape=[jax.ShapeDtypeStruct((frames, places, width), BF)] * (2 * n_in)
        + [jax.ShapeDtypeStruct((count, cols), BF) for cols in kept]
        + [jax.ShapeDtypeStruct((4, width), F32)],
        scratch_shapes=[
            pltpu.VMEM((tokens, 3 * width), BF),
            pltpu.VMEM((tokens, 3 * width), BF),
            pltpu.VMEM((tokens, width), BF),
            pltpu.VMEM((8 * (block // sub), GROUP * frames * n_in * sub), F32),
        ],
        compiler_params=pltpu.CompilerParams(vmem_limit_bytes=60 * MIB),
        cost_estimate=pl.CostEstimate(
            flops=2 * count * width * 2 * (4 * width + 2 * hidden),
            bytes_accessed=count * 26000,
            transcendentals=0,
        ),
    )(*pieces, *cots, qkv_w, out_w, in_w, unit_w, norm)


MESH = pl.DeviceIdType.MESH
STEP = 192


def blocks(count, body):
    lax.fori_loop(
        0, count // STEP, lambda i, _: body(pl.ds(pl.multiple_of(i * STEP, STEP), STEP)), None
    )


def reduce_kernel(kinds, n_sets, n_tail, *refs):
    n_chunks = len(kinds)
    refs = list(refs)

    def take(count):
        got = refs[:count]
        del refs[:count]
        return got

    lefts = [[take(n_sets) for _ in range(2 if kind[0] else 1)] for kind in kinds]
    rights = [take(n_sets) for _ in kinds]
    tails = take(n_tail)
    (out,) = take(1)
    tail_out = take(1)[0] if n_tail else None
    turned = [take(len(left)) for left in lefts]
    (stage, tile_in, sent, got1, held, got2, got3, total, got4) = take(9)
    (stage_sem, tile_sem, s1, r1, s2, r2, s3, r3, s4, r4) = take(10)
    if n_tail:
        (tail_sum, tail_got, tail_s, tail_r) = take(4)

    my_tp, my_y, my_z = lax.axis_index("tp"), lax.axis_index("clip"), lax.axis_index("fp")
    core, x = lax.rem(my_tp, 2), my_tp // 2
    n_z = lax.axis_size("fp")
    to_core = {"tp": my_tp ^ 1}
    to_x = {"tp": my_tp ^ 2}
    to_y = {"clip": my_y ^ 1}
    to_z = [{"fp": my_z ^ r} for r in range(1, n_z)]
    peers = [to_core, to_x, to_y] + to_z
    barrier = pltpu.get_barrier_semaphore()
    for peer in peers:
        pl.semaphore_signal(barrier, inc=1, device_id=peer, device_id_type=MESH)

    depth = held.shape[2]
    cols = held.shape[3]
    half = depth // 2
    own = depth // (2 * n_z)
    rows_set = tile_in.shape[1] // n_sets
    parts = [(1 - x) * 2 + 1 - core, x * 2 + 1 - core, (1 - x) * 2 + core, x * 2 + core]
    tiles = [(j, p) for j in range(n_chunks) for p in (0, 1)]
    tiles += [(j, p) for j in range(n_chunks) for p in (2, 3)]

    def fetch(index):
        j, p = tiles[index]
        return [
            pltpu.make_async_copy(
                rights[j][m].at[:, pl.ds(pl.multiple_of(parts[p] * cols, 128), cols)],
                tile_in.at[index % 2, pl.ds(m * rows_set, rows_set)],
                tile_sem.at[index % 2, m],
            )
            for m in range(n_sets)
        ]

    for copy in fetch(0):
        copy.start()
    lhs = [(j, i, m) for j in range(n_chunks) for i in range(len(lefts[j])) for m in range(n_sets)]

    def fetch_left(index):
        j, i, m = lhs[index]
        return pltpu.make_async_copy(
            lefts[j][i][m], stage.at[index % 2], stage_sem.at[index % 2]
        )

    def turn(chunk):
        for index, (j, i, m) in enumerate(lhs):
            if j != chunk:
                continue
            fetch_left(index).wait()
            if index + 1 < len(lhs):
                fetch_left(index + 1).start()

            turned[j][i][:, m * rows_set : (m + 1) * rows_set] = stage[index % 2].T

    def remote(src, dst, send, recv, peer):
        return pltpu.make_async_remote_copy(
            src_ref=src, dst_ref=dst, send_sem=send, recv_sem=recv, device_id=peer,
            device_id_type=MESH,
        )

    def first(j, p):
        return remote(sent.at[j, p], got1.at[j, p], s1.at[j, p], r1.at[j, p], to_core)

    def second(j, p):
        if kinds[j][1]:
            src = held.at[j, p, pl.ds(pl.multiple_of((1 - my_y) * half, 16), half)]
            dst = got2.at[j, pl.ds(p * half, half)]
            return remote(src, dst, s2.at[j, p], r2.at[j, p], to_y)
        return remote(held.at[j, 0], got2.at[j], s2.at[j, 0], r2.at[j, 0], to_x)

    def third(j):
        if kinds[j][1]:
            src = held.at[j, 0, pl.ds(pl.multiple_of(my_y * half, 16), half)]
            return remote(src, got3.at[j], s3.at[j], r3.at[j], to_x)
        src = held.at[j, 1, pl.ds(pl.multiple_of((1 - my_y) * half, 16), half)]
        return remote(src, got3.at[j], s3.at[j], r3.at[j], to_y)

    def fourth(j, r):
        src = total.at[j, pl.ds(pl.multiple_of((my_z ^ r) * own, 16), own)]
        return remote(src, got4.at[j, r - 1], s4.at[j, r - 1], r4.at[j, r - 1], to_z[r - 1])

    def tail_step(step):
        peer = ([to_core, to_y, to_x] + to_z)[step]
        return remote(
            tail_sum.at[min(step, 3)], tail_got.at[step], tail_s.at[step], tail_r.at[step], peer
        )

    fetch_left(0).start()
    for j in range(n_chunks):
        turn(j)
    pl.semaphore_wait(barrier, len(peers))
    if n_tail:
        tail_sum[0] = jnp.zeros_like(tail_sum[0])
        for row in range(3):
            tail_sum[0, 2 * row : 2 * row + 2] = sum_of(tails, row)
        tail_step(0).start()

    for index, (j, p) in enumerate(tiles):
        for copy in fetch(index):
            copy.wait()
        if index + 1 < len(tiles):
            for copy in fetch(index + 1):
                copy.start()
        right = tile_in.at[index % 2]
        if p >= 2:
            first(j, p - 2).wait_recv()
        edge = 2 * cols // 3
        lanes = lax.broadcasted_iota(jnp.int32, (STEP, cols - edge), 1) + edge

        def body(rows, j=j, p=p, right=right, lanes=lanes, edge=edge):
            value = dot(turned[j][0][rows, :], right[...], NN)
            if kinds[j][0]:
                other = dot(turned[j][1][rows, :], right[:, edge:], NN)
                end = jnp.where(lanes >= 3 * cols // 4, other, value[:, edge:])
                value = jnp.concatenate([value[:, :edge], end], axis=1)
            if p < 2:
                sent[j, p, rows, :] = value.astype(BF)
            else:
                held[j, p - 2, rows, :] = (
                    value + got1[j, p - 2, rows, :].astype(F32)
                ).astype(BF)

        blocks(depth, body)
        if p < 2:
            first(j, p).start()
        elif kinds[j][1] or p == 2:
            second(j, p - 2).start()

    for j in range(n_chunks):
        if kinds[j][1]:
            base = my_y * half
            for p in (0, 1):
                second(j, p).wait_recv()

                def body(rows, j=j, p=p):
                    mine = pl.ds(pl.multiple_of(rows.start + base, STEP), STEP)
                    there = pl.ds(pl.multiple_of(rows.start + p * half, STEP), STEP)
                    held[j, p, mine, :] = (
                        held[j, p, mine, :].astype(F32) + got2[j, there, :].astype(F32)
                    ).astype(BF)

                blocks(half, body)
                if p == 0:
                    third(j).start()
        else:
            second(j, 0).wait_recv()

            def body(rows, j=j):
                held[j, 1, rows, :] = (
                    held[j, 1, rows, :].astype(F32) + got2[j, rows, :].astype(F32)
                ).astype(BF)

            blocks(depth, body)
            third(j).start()
    for j in range(n_chunks):
        third(j).wait_recv()

        def body(rows, j=j):
            mine = pl.ds(pl.multiple_of(rows.start + my_y * half, STEP), STEP)
            total[j, rows, :] = (
                held[j, 1, mine, :].astype(F32) + got3[j, rows, :].astype(F32)
            ).astype(BF)

        blocks(half, body)
        for r in range(1, n_z):
            fourth(j, r).start()
    if n_tail:
        for step in range(3):
            tail_step(step).wait_recv()
            tail_sum[step + 1] = tail_sum[step] + tail_got[step]
            if step < 2:
                tail_step(step + 1).start()
        for r in range(n_z - 1):
            tail_step(3 + r).start()
        value = tail_sum[3]
        for r in range(n_z - 1):
            tail_step(3 + r).wait_recv()
            value = value + tail_got[3 + r]
        tail_out[...] = value
    for j in range(n_chunks):
        value = total[j, pl.ds(pl.multiple_of(my_z * own, 16), own), :].astype(F32)
        for r in range(1, n_z):
            fourth(j, r).wait_recv()
            value = value + got4[j, r - 1].astype(F32)
        out[j] = value
    for j in range(n_chunks):
        for p in (0, 1):
            first(j, p).wait_send()
        for p in (0, 1) if kinds[j][1] else (0,):
            second(j, p).wait_send()
        third(j).wait_send()
        for r in range(1, n_z):
            fourth(j, r).wait_send()
    if n_tail:
        for step in range(3 + n_z - 1):
            tail_step(step).wait_send()


def sum_of(tails, row):
    n = len(tails) // 2
    if row == 0:
        return sum(tail[...] for tail in tails[:n])
    return sum(tail[2 * row - 2 : 2 * row] for tail in tails[n:])


def reduce_grads(chunks, tails, identity):
    n_sets = len(chunks[0][1])
    kinds = tuple((len(lefts) == 2, y_first) for lefts, _, y_first in chunks)
    rows, depth = chunks[0][0][0][0].shape
    cols = chunks[0][1][0].shape[1] // lax.axis_size("tp")
    n_z = lax.axis_size("fp")
    n = len(chunks)
    half, own = depth // 2, depth // (2 * n_z)
    operands = [a for lefts, _, _ in chunks for left in lefts for a in left]
    n_any = len(operands) + n * n_sets
    operands += [a for _, rights, _ in chunks for a in rights]
    operands += tails
    any_spec = pl.BlockSpec(memory_space=pl.ANY)
    vmem = pl.BlockSpec(memory_space=pltpu.VMEM)
    dma = pltpu.SemaphoreType.DMA
    outs = [jax.ShapeDtypeStruct((n, own, cols), F32)]
    scratch = [
        pltpu.VMEM((depth, rows * n_sets), BF) for kind in kinds for _ in range(2 if kind[0] else 1)
    ]
    scratch += [
        pltpu.VMEM((2, rows, depth), BF),
        pltpu.VMEM((2, rows * n_sets, cols), BF),
        pltpu.VMEM((n, 2, depth, cols), BF),
        pltpu.VMEM((n, 2, depth, cols), BF),
        pltpu.VMEM((n, 2, depth, cols), BF),
        pltpu.VMEM((n, depth, cols), BF),
        pltpu.VMEM((n, half, cols), BF),
        pltpu.VMEM((n, half, cols), BF),
        pltpu.VMEM((n, n_z - 1, own, cols), BF),
        dma((2,)),
        dma((2, n_sets)),
        dma((n, 2)),
        dma((n, 2)),
        dma((n, 2)),
        dma((n, 2)),
        dma((n,)),
        dma((n,)),
        dma((n, n_z - 1)),
        dma((n, n_z - 1)),
    ]
    if tails:
        n_rows = 8
        outs.append(jax.ShapeDtypeStruct((n_rows, depth), F32))
        scratch += [
            pltpu.VMEM((4, n_rows, depth), F32),
            pltpu.VMEM((2 + n_z, n_rows, depth), F32),
            dma((2 + n_z,)),
            dma((2 + n_z,)),
        ]
    return pl.pallas_call(
        partial(reduce_kernel, kinds, n_sets, len(tails)),
        in_specs=[any_spec] * n_any + [vmem] * len(tails),
        out_specs=[vmem] * len(outs),
        out_shape=outs,
        scratch_shapes=scratch,
        compiler_params=pltpu.CompilerParams(
            vmem_limit_bytes=62 * MIB, collective_id=identity, has_side_effects=True
        ),
        cost_estimate=pl.CostEstimate(
            flops=2 * n * 4 * depth * cols * rows * n_sets,
            bytes_accessed=n * 5 * rows * n_sets * cols * 2,
            transcendentals=0,
        ),
    )(*operands)


def to_peer(value, axis, step):
    n = lax.axis_size(axis)
    return lax.ppermute(value, axis, [(i, i ^ step) for i in range(n)])


def swap(pieces, axis):
    return [piece if s == 0 else to_peer(piece, axis, s) for s, piece in enumerate(pieces)]


def pick(stack, index):
    return lax.dynamic_index_in_dim(stack, index, 0, keepdims=False)


def shards(
    inputs, cotangent, qkv_weight, out_spatial, out_temporal, mlp_in, mlp_out, ln_gain, ln_bias
):
    micros, clips, frames, local, width = inputs.shape
    n_tp, n_fp = lax.axis_size("tp"), lax.axis_size("fp")
    n_cf = lax.axis_size("clip") * n_fp
    assert clips == n_tp
    my_tp, my_fp = lax.axis_index("tp"), lax.axis_index("fp")
    depth = qkv_weight.shape[2]
    span = qkv_weight.shape[3]
    places = n_tp * local
    chunk = places // n_fp
    at = my_fp.astype(jnp.int32)[None]

    first = jnp.concatenate([qkv_weight[0, i] for i in range(3)] + [out_spatial.T], axis=1)
    second = jnp.concatenate([qkv_weight[1, i] for i in range(3)] + [out_temporal.T], axis=1)
    axes = ("clip", "fp", "tp")

    def gathered(part):
        return lax.all_gather(part, axes).reshape(n_cf, n_tp, depth, part.shape[1])

    def attention_weights(raw):
        raw = raw.reshape(n_cf, n_tp, depth, 4, span).transpose(3, 0, 2, 1, 4)
        raw = raw.reshape(4, n_cf * depth, n_tp * span)
        return jnp.concatenate([raw[0], raw[1], raw[2]], axis=1), raw[3]

    def unit_weights(raw):
        return raw.transpose(1, 0, 2, 3).reshape(n_tp, n_cf * depth, raw.shape[3])

    norms = lax.all_gather(jnp.concatenate([ln_gain, ln_bias]), ("clip", "fp"))
    norms = norms.transpose(1, 0, 2).reshape(6, n_cf * depth).astype(F32)
    order = jnp.array([0, 3, 1, 4, 2, 5])
    norms = jnp.stack([norms[0], norms[3], norms[1], norms[4], norms[2], norms[5]])
    qkv_space_w, out_space_w = attention_weights(gathered(first))
    rest = gathered(jnp.concatenate([second, mlp_in, mlp_out.T], axis=1))
    qkv_time_w, out_time_w = attention_weights(rest[..., : 4 * span])
    in_w = unit_weights(rest[..., 4 * span : 4 * span + mlp_in.shape[1]])
    unit_w = unit_weights(rest[..., 4 * span + mlp_in.shape[1] :])

    def inward(array, m):
        return swap([pick(array[m], my_tp ^ s) for s in range(n_tp)], "tp")

    def to_chunks(pieces):
        joined = jnp.concatenate(pieces, axis=1)
        return [
            lax.dynamic_slice_in_dim(joined, (my_fp ^ r) * chunk, chunk, 1) for r in range(n_fp)
        ]

    def from_chunks(chunks):
        stack = jnp.stack(chunks)
        joined = jnp.concatenate([pick(stack, my_fp ^ c) for c in range(n_fp)], axis=1)
        return [joined[:, s * local : (s + 1) * local] for s in range(n_tp)]

    def outward(pieces):
        stack = jnp.stack(swap(pieces, "tp"))
        return jnp.stack([pick(stack, my_tp ^ c) for c in range(n_tp)])

    space_in = [inward(inputs, m) for m in range(micros)]
    cots = [swap(to_chunks(inward(cotangent, m)), "fp") for m in range(micros)]
    space_kept = []
    time_in = []
    for m in range(micros):
        out = space_forward(space_in[m], qkv_space_w, out_space_w, norms, at, n_fp)
        time_in.append(swap(out[:n_fp], "fp"))
        space_kept.append(out[n_fp:])
    time_kept = []
    results = []
    space_grads = []
    for m in range(micros):
        out = time_layer(time_in[m], cots[m], qkv_time_w, out_time_w, in_w, unit_w, norms)
        results.append(outward(from_chunks(swap(out[:n_fp], "fp"))))
        space_grads.append(swap(out[n_fp : 2 * n_fp], "fp"))
        time_kept.append(out[2 * n_fp :])
    space_rows = []
    input_grads = []
    flat = lambda v: v.reshape(-1, v.shape[-1])
    kept = lambda i: [k[i] for k in time_kept]
    time_chunks = [
        ([kept(3)], kept(4), True),
        ([kept(6)], kept(5), False),
        ([kept(0), kept(2)], kept(1), True),
    ]
    whole_rows = depth % 16 == 0 and n_tp == 4 and lax.axis_size("clip") == 2
    if whole_rows:
        (late,) = reduce_grads(time_chunks, [], 1)
    for m in range(micros):
        qkv, mixed, logsum = space_kept[m]
        out = space_backward(
            space_in[m], space_grads[m], qkv, mixed, logsum, qkv_space_w, out_space_w, norms, at
        )
        input_grads.append(outward(out[:n_tp]).astype(F32))
        normed, low, columns, norm_grad = out[n_tp:]
        space_rows.append((flat(normed), flat(low), flat(columns), norm_grad))
    back = lambda i: [k[i] for k in space_rows]
    space_chunk = ([back(0), back(1)], back(2), True)
    tails = back(3) + kept(7)
    if whole_rows:
        early, norm_grads = reduce_grads([space_chunk], tails, 2)
    else:
        early = scatter_grads([space_chunk], n_cf, n_tp)
        late = scatter_grads(time_chunks, n_cf, n_tp)
        norm_grads = lax.psum(jnp.concatenate([sum(back(3)), sum(kept(7))]), axes)
    norm_grads = norm_grads[:6].reshape(3, 2, n_cf, depth)
    mine = lax.axis_index("clip") * n_fp + my_fp
    norm_grads = lax.dynamic_index_in_dim(norm_grads, mine, 2, keepdims=False)
    kinds = lambda v: [v[:, i * span : (i + 1) * span] for i in range(4)]
    space_g, time_g = kinds(early[0]), kinds(late[2])
    return (
        jnp.stack(results),
        jnp.stack(input_grads),
        jnp.stack([jnp.stack(space_g[:3]), jnp.stack(time_g[:3])]),
        space_g[3].T,
        time_g[3].T,
        late[0],
        late[1].T,
        norm_grads[:, 0],
        norm_grads[:, 1],
    )


def scatter_grads(chunks, n_cf, n_tp):
    tiles = []
    for lefts, rights, _ in chunks:
        cols = rights[0].shape[1] // n_tp
        total = sum(dot(a, b, TN) for a, b in zip(lefts[0], rights))
        total = total.reshape(total.shape[0], n_tp, cols)
        if len(lefts) == 2:
            other = sum(dot(a, b, TN) for a, b in zip(lefts[1], rights))
            other = other.reshape(other.shape[0], n_tp, cols)
            at = 3 * cols // 4
            total = jnp.concatenate([total[..., :at], other[..., at:]], axis=2)
        total = total.reshape(n_cf, total.shape[0] // n_cf, n_tp, cols).transpose(0, 2, 1, 3)
        tiles.append(total.reshape((n_cf * n_tp,) + total.shape[2:]))
    return lax.psum_scatter(jnp.stack(tiles, 1), ("clip", "fp", "tp"), scatter_dimension=0)


def solution(mesh):
    spread = P(None, "clip", "fp", "tp", None)
    return jax.shard_map(
        shards,
        mesh=mesh,
        in_specs=(
            spread,
            spread,
            P(None, None, ("clip", "fp"), "tp"),
            P("tp", ("clip", "fp")),
            P("tp", ("clip", "fp")),
            P(("clip", "fp"), "tp"),
            P("tp", ("clip", "fp")),
            P(None, ("clip", "fp")),
            P(None, ("clip", "fp")),
        ),
        out_specs=(
            spread,
            spread,
            P(None, None, ("clip", "fp"), "tp"),
            P("tp", ("clip", "fp")),
            P("tp", ("clip", "fp")),
            P(("clip", "fp"), "tp"),
            P("tp", ("clip", "fp")),
            P(None, ("clip", "fp")),
            P(None, ("clip", "fp")),
        ),
        check_vma=False,
    )
```

```python
from functools import partial

import jax
import jax.numpy as jnp
from jax import lax
from jax.experimental import pallas as pl
from jax.experimental.pallas import tpu as pltpu
from jax.sharding import PartitionSpec as P

HD = 64
GROUP = 4
WIDE = GROUP * HD
EPS = 1e-06
BF = jnp.bfloat16
F32 = jnp.float32
MIB = 1024 * 1024

NN = (((1,), (0,)), ((), ()))
NT = (((1,), (1,)), ((), ()))
TN = (((0,), (0,)), ((), ()))


def dot(a, b, dims):
    return lax.dot_general(a, b, dims, preferred_element_type=F32)


def normalise(values):
    centre = values - jnp.mean(values, axis=-1, keepdims=True)
    spread = jnp.mean(centre * centre, axis=-1, keepdims=True)
    rate = lax.rsqrt(spread + EPS)
    return centre * rate, rate


def norm_back(upstream, gain, unit, rate):
    weighted = upstream * gain
    inner = jnp.mean(weighted * unit, axis=-1, keepdims=True)
    return rate * (weighted - jnp.mean(weighted, axis=-1, keepdims=True) - unit * inner)


def head_masks(scale):
    lanes = lax.broadcasted_iota(jnp.int32, (1, WIDE), 1) // HD
    return [jnp.where(lanes == h, scale, 0.0).astype(BF) for h in range(GROUP)]


def spread_heads(block, masks):
    return jnp.concatenate([block * mask for mask in masks], axis=0)


def gather_heads(stacked, rows):
    lanes = lax.broadcasted_iota(jnp.int32, (1, WIDE), 1) // HD
    total = stacked[:rows]
    for h in range(1, GROUP):
        total = jnp.where(lanes == h, stacked[h * rows : (h + 1) * rows], total)
    return total


def attend(queries, keys, values, bias):
    rows = queries.shape[0]
    scores = dot(keys, spread_heads(queries, head_masks(HD**-0.5)), NT)
    if bias is not None:
        scores = scores + bias
    top = jnp.max(scores, axis=0, keepdims=True)
    exponent = jnp.exp(scores - top)
    totals = jnp.sum(exponent, axis=0, keepdims=True)
    weights = (exponent * (1.0 / totals)).astype(BF)
    mixed = gather_heads(dot(weights, values, TN), rows).astype(BF)
    return mixed, top + jnp.log(totals)


def attend_back(queries, keys, values, upstream, logsum, bias):
    rows = queries.shape[0]
    spread_q = spread_heads(queries, head_masks(HD**-0.5))
    spread_g = spread_heads(upstream, head_masks(1.0))
    scores = dot(keys, spread_q, NT)
    if bias is not None:
        scores = scores + bias
    probs = jnp.exp(scores - logsum)
    grad_probs = dot(values, spread_g, NT)
    inner = jnp.sum(probs * grad_probs, axis=0, keepdims=True)
    grad_scores = (probs * (grad_probs - inner)).astype(BF)
    grad_values = dot(probs.astype(BF), spread_g, NN)
    grad_keys = dot(grad_scores, spread_q, NN)
    grad_queries = gather_heads(dot(grad_scores, keys, TN), rows) * HD**-0.5
    return grad_queries.astype(BF), grad_keys.astype(BF), grad_values.astype(BF)


def gelu_parts(pre):
    size = jnp.abs(pre) * (0.5**0.5)
    t = 1.0 / (1.0 + 0.3275911 * size)
    bell = jnp.exp(-size * size)
    poly = t * (
        0.254829592
        + t * (-0.284496736 + t * (1.421413741 + t * (-1.453152027 + t * 1.061405429)))
    )
    tail = 0.5 * poly * bell
    return jnp.where(pre >= 0, 1.0 - tail, tail), bell * 0.3989422804014327


def space_forward_kernel(n_in, n_out, at_ref, *refs):
    pieces = refs[:n_in]
    qkv_w, out_w, norm = refs[n_in : n_in + 3]
    outs = refs[n_in + 3 : n_in + 3 + n_out]
    qkv_out, mixed_out, logsum_out, held = refs[n_in + 3 + n_out :]
    width = out_w.shape[1]
    x = jnp.concatenate([piece[0] for piece in pieces], axis=0).astype(F32)
    unit, _ = normalise(x)
    normed = (unit * norm[0:1] + norm[1:2]).astype(BF)
    qkv_out[0] = dot(normed, qkv_w[...], NN).astype(BF)
    for g in range(width // WIDE):
        at = g * WIDE
        mixed, logsum = attend(
            qkv_out[0, :, at : at + WIDE],
            qkv_out[0, :, width + at : width + at + WIDE],
            qkv_out[0, :, 2 * width + at : 2 * width + at + WIDE],
            None,
        )
        mixed_out[0, :, at : at + WIDE] = mixed
        logsum_out[0, g : g + 1] = logsum
    held[...] = x + dot(mixed_out[0], out_w[...], NT)
    rows = outs[0].shape[1]
    for r, out in enumerate(outs):
        start = pl.multiple_of((at_ref[0] ^ r) * rows, 8)
        out[0] = held[pl.ds(start, rows), :].astype(BF)


def space_forward(pieces, qkv_w, out_w, norm, at, n_out):
    frames, rows, width = pieces[0].shape
    places = rows * len(pieces)
    groups = width // WIDE
    whole = pl.BlockSpec(memory_space=pltpu.VMEM)
    frame = lambda *dims: pl.BlockSpec((1,) + dims, lambda f, at: (f,) + (0,) * len(dims))
    return pl.pallas_call(
        partial(space_forward_kernel, len(pieces), n_out),
        grid_spec=pltpu.PrefetchScalarGridSpec(
            num_scalar_prefetch=1,
            grid=(frames,),
            in_specs=[frame(rows, width)] * len(pieces) + [whole] * 3,
            out_specs=[frame(places // n_out, width)] * n_out
            + [frame(places, 3 * width), frame(places, width), frame(groups, GROUP * places)],
            scratch_shapes=[pltpu.VMEM((places, width), F32)],
        ),
        out_shape=[jax.ShapeDtypeStruct((frames, places // n_out, width), BF)] * n_out
        + [
            jax.ShapeDtypeStruct((frames, places, 3 * width), BF),
            jax.ShapeDtypeStruct((frames, places, width), BF),
            jax.ShapeDtypeStruct((frames, groups, GROUP * places), F32),
        ],
        compiler_params=pltpu.CompilerParams(vmem_limit_bytes=48 * MIB),
        cost_estimate=pl.CostEstimate(
            flops=2 * frames * places * width * 5 * width,
            bytes_accessed=frames * places * width * 16,
            transcendentals=0,
        ),
    )(at, *pieces, qkv_w, out_w, norm)


def store_columns(out, kinds, n_parts):
    width = kinds[0].shape[1]
    span = width // n_parts
    for t in range(n_parts):
        for i, kind in enumerate(kinds):
            start = (t * len(kinds) + i) * span
            out[:, start : start + span] = kind[:, t * span : (t + 1) * span]


def space_backward_kernel(n_in, n_grad, n_out, at_ref, *refs):
    pieces = refs[:n_in]
    grads = refs[n_in : n_in + n_grad]
    qkv_in, mixed_in, logsum_in, qkv_w, out_w, norm = refs[n_in + n_grad : n_in + n_grad + 6]
    rest = refs[n_in + n_grad + 6 :]
    outs = rest[:n_out]
    normed_out, grad_out, columns, norm_out, held, dqkv = rest[n_out:]
    width = out_w.shape[1]
    rows = grads[0].shape[1]
    for r, grad in enumerate(grads):
        start = pl.multiple_of((at_ref[0] ^ r) * rows, 8)
        held[pl.ds(start, rows), :] = grad[0].astype(F32)
    x = jnp.concatenate([piece[0] for piece in pieces], axis=0).astype(F32)
    unit, rate = normalise(x)
    normed_out[0] = (unit * norm[0:1] + norm[1:2]).astype(BF)
    low = held[...].astype(BF)
    grad_out[0] = low
    grad_mixed = dot(low, out_w[...], NN).astype(BF)
    for g in range(width // WIDE):
        at = g * WIDE
        parts = attend_back(
            qkv_in[0, :, at : at + WIDE],
            qkv_in[0, :, width + at : width + at + WIDE],
            qkv_in[0, :, 2 * width + at : 2 * width + at + WIDE],
            grad_mixed[:, at : at + WIDE],
            logsum_in[0, g : g + 1],
            None,
        )
        for i, part in enumerate(parts):
            dqkv[:, i * width + at : i * width + at + WIDE] = part
    store_columns(
        columns.at[0],
        [dqkv[:, i * width : (i + 1) * width] for i in range(3)] + [mixed_in[0]],
        n_out,
    )
    grad_normed = dot(dqkv[...], qkv_w[...], NT)

    @pl.when(pl.program_id(0) == 0)
    def _():
        norm_out[...] = jnp.zeros_like(norm_out)

    norm_out[0:1] += jnp.sum(grad_normed * unit, axis=0, keepdims=True)
    norm_out[1:2] += jnp.sum(grad_normed, axis=0, keepdims=True)
    total = held[...] + norm_back(grad_normed, norm[0:1], unit, rate)
    rows = outs[0].shape[1]
    for s, out in enumerate(outs):
        out[0] = total[s * rows : (s + 1) * rows].astype(BF)


def space_backward(pieces, grads, qkv, mixed, logsum, qkv_w, out_w, norm, at, first, n_out):
    frames, width = grads[0].shape[0], grads[0].shape[2]
    places = grads[0].shape[1] * len(grads)
    rows = places // n_out
    groups = width // WIDE
    n_grad = len(grads)
    whole = pl.BlockSpec(memory_space=pltpu.VMEM)
    frame = lambda *dims: pl.BlockSpec((1,) + dims, lambda f, at: (f,) + (0,) * len(dims))
    later = lambda *dims: pl.BlockSpec((1,) + dims, lambda f, at: (f + first,) + (0,) * len(dims))
    return pl.pallas_call(
        partial(space_backward_kernel, len(pieces), n_grad, n_out),
        grid_spec=pltpu.PrefetchScalarGridSpec(
            num_scalar_prefetch=1,
            grid=(frames,),
            in_specs=[later(places // len(pieces), width)] * len(pieces)
            + [frame(places // n_grad, width)] * n_grad
            + [later(places, 3 * width), later(places, width), later(groups, GROUP * places)]
            + [whole] * 3,
            out_specs=[frame(rows, width)] * n_out
            + [frame(places, width), frame(places, width), frame(places, 4 * width)]
            + [pl.BlockSpec((2, width), lambda f, at: (0, 0))],
            scratch_shapes=[
                pltpu.VMEM((places, width), F32),
                pltpu.VMEM((places, 3 * width), BF),
            ],
        ),
        out_shape=[jax.ShapeDtypeStruct((frames, rows, width), BF)] * n_out
        + [
            jax.ShapeDtypeStruct((frames, places, width), BF),
            jax.ShapeDtypeStruct((frames, places, width), BF),
            jax.ShapeDtypeStruct((frames, places, 4 * width), BF),
            jax.ShapeDtypeStruct((2, width), F32),
        ],
        compiler_params=pltpu.CompilerParams(vmem_limit_bytes=48 * MIB),
        cost_estimate=pl.CostEstimate(
            flops=2 * frames * places * width * 7 * width,
            bytes_accessed=frames * places * width * 24,
            transcendentals=0,
        ),
    )(at, *pieces, *grads, qkv, mixed, logsum, qkv_w, out_w, norm)


def time_kernel(n_arrays, n_in, n_parts, sub, *refs):
    pieces = refs[:n_arrays]
    cots = refs[n_arrays : 2 * n_arrays]
    qkv_w, out_w, in_w, unit_w, norm = refs[2 * n_arrays : 2 * n_arrays + 5]
    rest = refs[2 * n_arrays + 5 :]
    results = rest[:n_in]
    grads = rest[n_in : 2 * n_in]
    (
        normed_time,
        columns,
        grad_time,
        normed_mlp,
        grad_pre,
        hidden,
        grad_result,
        norm_out,
        qkv,
        dqkv,
        mixed,
        probs_logsum,
    ) = rest[2 * n_in :]
    width = out_w.shape[1]
    frames, places = results[0].shape[:2]
    all_frames = frames * n_in
    rows = all_frames * sub
    parts = places // sub

    def tokens(blocks):
        blocks = [b[...].reshape(-1, places, width) for b in blocks]
        joined = jnp.concatenate(blocks, axis=0).astype(F32)
        return jnp.concatenate(
            [joined[:, j * sub : (j + 1) * sub, :].reshape(rows, width) for j in range(parts)],
            axis=0,
        )

    def scatter(values, outs):
        grid = jnp.concatenate(
            [
                values[j * rows : (j + 1) * rows].reshape(all_frames, sub, width)
                for j in range(parts)
            ],
            axis=1,
        ).astype(BF)
        for r, out in enumerate(outs):
            out[...] = grid[r * frames : (r + 1) * frames]

    key_place = lax.broadcasted_iota(jnp.int32, (rows, GROUP * rows), 0) % sub
    query_place = lax.broadcasted_iota(jnp.int32, (rows, GROUP * rows), 1) % sub
    bias = jnp.where(key_place == query_place, 0.0, -1e30)

    after_space = tokens(pieces)
    unit, rate = normalise(after_space)
    normed_time[...] = (unit * norm[2:3] + norm[3:4]).astype(BF)
    qkv[...] = dot(normed_time[...], qkv_w[...], NN).astype(BF)
    groups = width // WIDE
    for j in range(parts):
        at_rows = slice(j * rows, (j + 1) * rows)
        for g in range(groups):
            at = g * WIDE
            out, logsum = attend(
                qkv[at_rows, at : at + WIDE],
                qkv[at_rows, width + at : width + at + WIDE],
                qkv[at_rows, 2 * width + at : 2 * width + at + WIDE],
                bias,
            )
            mixed[at_rows, at : at + WIDE] = out
            probs_logsum[j * groups + g : j * groups + g + 1] = logsum
    after_time = after_space + dot(mixed[...], out_w[...], NT)
    unit2, rate2 = normalise(after_time)
    normed_mlp[...] = (unit2 * norm[4:5] + norm[5:6]).astype(BF)
    cot = tokens(cots)
    grad_result[...] = cot.astype(BF)
    result = after_time
    grad_normed = None
    for c in range(in_w.shape[0]):
        cols = slice(c * in_w.shape[2], (c + 1) * in_w.shape[2])
        pre = dot(normed_mlp[...], in_w[c], NN)
        below, density = gelu_parts(pre)
        hidden[:, cols] = (pre * below).astype(BF)
        result = result + dot(hidden[:, cols], unit_w[c], NT)
        grad_hidden = dot(grad_result[...], unit_w[c], NN)
        grad_pre[:, cols] = (grad_hidden * (below + pre * density)).astype(BF)
        term = dot(grad_pre[:, cols], in_w[c], NT)
        grad_normed = term if c == 0 else grad_normed + term
    scatter(result, results)

    @pl.when(pl.program_id(0) == 0)
    def _():
        norm_out[...] = jnp.zeros_like(norm_out)

    norm_out[2:3] += jnp.sum(grad_normed * unit2, axis=0, keepdims=True)
    norm_out[3:4] += jnp.sum(grad_normed, axis=0, keepdims=True)
    grad_after = cot + norm_back(grad_normed, norm[4:5], unit2, rate2)
    grad_time[...] = grad_after.astype(BF)
    grad_mixed = dot(grad_time[...], out_w[...], NN).astype(BF)
    for j in range(parts):
        at_rows = slice(j * rows, (j + 1) * rows)
        for g in range(groups):
            at = g * WIDE
            back = attend_back(
                qkv[at_rows, at : at + WIDE],
                qkv[at_rows, width + at : width + at + WIDE],
                qkv[at_rows, 2 * width + at : 2 * width + at + WIDE],
                grad_mixed[at_rows, at : at + WIDE],
                probs_logsum[j * groups + g : j * groups + g + 1],
                bias,
            )
            for i, part in enumerate(back):
                dqkv[at_rows, i * width + at : i * width + at + WIDE] = part
    store_columns(
        columns,
        [dqkv[:, i * width : (i + 1) * width] for i in range(3)] + [mixed[...]],
        n_parts,
    )
    grad_normed = dot(dqkv[...], qkv_w[...], NT)
    norm_out[0:1] += jnp.sum(grad_normed * unit, axis=0, keepdims=True)
    norm_out[1:2] += jnp.sum(grad_normed, axis=0, keepdims=True)
    scatter(grad_after + norm_back(grad_normed, norm[2:3], unit, rate), grads)


def time_layer(pieces, cots, qkv_w, out_w, in_w, unit_w, norm, at=None):
    frames, places, width = pieces[0].shape[-3:]
    n_in = len(pieces) if at is None else pieces[0].shape[1]
    block = 16 if places % 16 == 0 else 8
    sub = 8
    tokens = frames * n_in * block
    count = frames * n_in * places
    hidden = in_w.shape[0] * in_w.shape[2]
    whole = pl.BlockSpec(memory_space=pltpu.VMEM)
    piece = pl.BlockSpec((frames, block, width), lambda b: (0, b, 0))
    joint = pl.BlockSpec((None, n_in, frames, block, width), lambda b: (at, 0, 0, b, 0))
    given = [piece if at is None else joint] * (2 * len(pieces))
    row = lambda cols: pl.BlockSpec((tokens, cols), lambda b: (b, 0))
    kept = [width, 4 * width, width, width, hidden, hidden, width]
    return pl.pallas_call(
        partial(time_kernel, len(pieces), n_in, in_w.shape[0], sub),
        grid=(places // block,),
        in_specs=given + [whole] * 5,
        out_specs=[piece] * (2 * n_in)
        + [row(cols) for cols in kept]
        + [pl.BlockSpec((4, width), lambda b: (0, 0))],
        out_shape=[jax.ShapeDtypeStruct((frames, places, width), BF)] * (2 * n_in)
        + [jax.ShapeDtypeStruct((count, cols), BF) for cols in kept]
        + [jax.ShapeDtypeStruct((4, width), F32)],
        scratch_shapes=[
            pltpu.VMEM((tokens, 3 * width), BF),
            pltpu.VMEM((tokens, 3 * width), BF),
            pltpu.VMEM((tokens, width), BF),
            pltpu.VMEM((8 * (block // sub), GROUP * frames * n_in * sub), F32),
        ],
        compiler_params=pltpu.CompilerParams(vmem_limit_bytes=60 * MIB),
        cost_estimate=pl.CostEstimate(
            flops=2 * count * width * 2 * (4 * width + 2 * hidden),
            bytes_accessed=count * 26000,
            transcendentals=0,
        ),
    )(*pieces, *cots, qkv_w, out_w, in_w, unit_w, norm)


MESH = pl.DeviceIdType.MESH
STEP = 192


def blocks(count, body):
    lax.fori_loop(
        0, count // STEP, lambda i, _: body(pl.ds(pl.multiple_of(i * STEP, STEP), STEP)), None
    )


def reduce_kernel(kinds, n_sets, n_tail, *refs):
    n_chunks = len(kinds)
    refs = list(refs)

    def take(count):
        got = refs[:count]
        del refs[:count]
        return got

    lefts = [[take(n_sets) for _ in range(2 if kind[0] else 1)] for kind in kinds]
    rights = [take(n_sets) for _ in kinds]
    tails = take(n_tail)
    (out,) = take(1)
    tail_out = take(1)[0] if n_tail else None
    turned = [take(len(left)) for left in lefts]
    (stage, tile_in, sent, got1, held, got2, got3, total, got4) = take(9)
    (stage_sem, tile_sem, s1, r1, s2, r2, s3, r3, s4, r4) = take(10)
    if n_tail:
        (tail_sum, tail_got, tail_s, tail_r) = take(4)

    my_tp, my_y, my_z = lax.axis_index("tp"), lax.axis_index("clip"), lax.axis_index("fp")
    core, x = lax.rem(my_tp, 2), my_tp // 2
    n_z = lax.axis_size("fp")
    to_core = {"tp": my_tp ^ 1}
    to_x = {"tp": my_tp ^ 2}
    to_y = {"clip": my_y ^ 1}
    to_z = [{"fp": my_z ^ r} for r in range(1, n_z)]
    peers = [to_core, to_x, to_y] + to_z
    barrier = pltpu.get_barrier_semaphore()
    for peer in peers:
        pl.semaphore_signal(barrier, inc=1, device_id=peer, device_id_type=MESH)

    depth = held.shape[2]
    cols = held.shape[3]
    half = depth // 2
    own = depth // (2 * n_z)
    rows_set = tile_in.shape[1] // n_sets
    parts = [(1 - x) * 2 + 1 - core, x * 2 + 1 - core, (1 - x) * 2 + core, x * 2 + core]
    tiles = [(j, p) for j in range(n_chunks) for p in (0, 1)]
    tiles += [(j, p) for j in range(n_chunks) for p in (2, 3)]

    def fetch(index):
        j, p = tiles[index]
        return [
            pltpu.make_async_copy(
                rights[j][m].at[:, pl.ds(pl.multiple_of(parts[p] * cols, 128), cols)],
                tile_in.at[index % 2, pl.ds(m * rows_set, rows_set)],
                tile_sem.at[index % 2, m],
            )
            for m in range(n_sets)
        ]

    for copy in fetch(0):
        copy.start()
    lhs = [(j, i, m) for j in range(n_chunks) for i in range(len(lefts[j])) for m in range(n_sets)]

    def fetch_left(index):
        j, i, m = lhs[index]
        return pltpu.make_async_copy(
            lefts[j][i][m], stage.at[index % 2], stage_sem.at[index % 2]
        )

    def turn(chunk):
        for index, (j, i, m) in enumerate(lhs):
            if j != chunk:
                continue
            fetch_left(index).wait()
            if index + 1 < len(lhs):
                fetch_left(index + 1).start()

            turned[j][i][:, m * rows_set : (m + 1) * rows_set] = stage[index % 2].T

    def remote(src, dst, send, recv, peer):
        return pltpu.make_async_remote_copy(
            src_ref=src, dst_ref=dst, send_sem=send, recv_sem=recv, device_id=peer,
            device_id_type=MESH,
        )

    def first(j, p):
        return remote(sent.at[j, p], got1.at[j, p], s1.at[j, p], r1.at[j, p], to_core)

    def second(j, p):
        if kinds[j][1]:
            src = held.at[j, p, pl.ds(pl.multiple_of((1 - my_y) * half, 16), half)]
            dst = got2.at[j, pl.ds(p * half, half)]
            return remote(src, dst, s2.at[j, p], r2.at[j, p], to_y)
        return remote(held.at[j, 0], got2.at[j], s2.at[j, 0], r2.at[j, 0], to_x)

    def third(j):
        if kinds[j][1]:
            src = held.at[j, 0, pl.ds(pl.multiple_of(my_y * half, 16), half)]
            return remote(src, got3.at[j], s3.at[j], r3.at[j], to_x)
        src = held.at[j, 1, pl.ds(pl.multiple_of((1 - my_y) * half, 16), half)]
        return remote(src, got3.at[j], s3.at[j], r3.at[j], to_y)

    def fourth(j, r):
        src = total.at[j, pl.ds(pl.multiple_of((my_z ^ r) * own, 16), own)]
        return remote(src, got4.at[j, r - 1], s4.at[j, r - 1], r4.at[j, r - 1], to_z[r - 1])

    def tail_step(step):
        peer = ([to_core, to_y, to_x] + to_z)[step]
        return remote(
            tail_sum.at[min(step, 3)], tail_got.at[step], tail_s.at[step], tail_r.at[step], peer
        )

    fetch_left(0).start()
    for j in range(n_chunks):
        turn(j)
    pl.semaphore_wait(barrier, len(peers))
    if n_tail:
        tail_sum[0] = jnp.zeros_like(tail_sum[0])
        for row in range(3):
            tail_sum[0, 2 * row : 2 * row + 2] = sum_of(tails, row)
        tail_step(0).start()

    for index, (j, p) in enumerate(tiles):
        for copy in fetch(index):
            copy.wait()
        if index + 1 < len(tiles):
            for copy in fetch(index + 1):
                copy.start()
        right = tile_in.at[index % 2]
        if p >= 2:
            first(j, p - 2).wait_recv()
        edge = 2 * cols // 3
        lanes = lax.broadcasted_iota(jnp.int32, (STEP, cols - edge), 1) + edge

        def body(rows, j=j, p=p, right=right, lanes=lanes, edge=edge):
            value = dot(turned[j][0][rows, :], right[...], NN)
            if kinds[j][0]:
                other = dot(turned[j][1][rows, :], right[:, edge:], NN)
                end = jnp.where(lanes >= 3 * cols // 4, other, value[:, edge:])
                value = jnp.concatenate([value[:, :edge], end], axis=1)
            if p < 2:
                sent[j, p, rows, :] = value.astype(BF)
            else:
                held[j, p - 2, rows, :] = (
                    value + got1[j, p - 2, rows, :].astype(F32)
                ).astype(BF)

        blocks(depth, body)
        if p < 2:
            first(j, p).start()
        elif kinds[j][1] or p == 2:
            second(j, p - 2).start()

    for j in range(n_chunks):
        if kinds[j][1]:
            base = my_y * half
            for p in (0, 1):
                second(j, p).wait_recv()

                def body(rows, j=j, p=p):
                    mine = pl.ds(pl.multiple_of(rows.start + base, STEP), STEP)
                    there = pl.ds(pl.multiple_of(rows.start + p * half, STEP), STEP)
                    held[j, p, mine, :] = (
                        held[j, p, mine, :].astype(F32) + got2[j, there, :].astype(F32)
                    ).astype(BF)

                blocks(half, body)
                if p == 0:
                    third(j).start()
        else:
            second(j, 0).wait_recv()

            def body(rows, j=j):
                held[j, 1, rows, :] = (
                    held[j, 1, rows, :].astype(F32) + got2[j, rows, :].astype(F32)
                ).astype(BF)

            blocks(depth, body)
            third(j).start()
    for j in range(n_chunks):
        third(j).wait_recv()

        def body(rows, j=j):
            mine = pl.ds(pl.multiple_of(rows.start + my_y * half, STEP), STEP)
            total[j, rows, :] = (
                held[j, 1, mine, :].astype(F32) + got3[j, rows, :].astype(F32)
            ).astype(BF)

        blocks(half, body)
        for r in range(1, n_z):
            fourth(j, r).start()
    if n_tail:
        for step in range(3):
            tail_step(step).wait_recv()
            tail_sum[step + 1] = tail_sum[step] + tail_got[step]
            if step < 2:
                tail_step(step + 1).start()
        for r in range(n_z - 1):
            tail_step(3 + r).start()
        value = tail_sum[3]
        for r in range(n_z - 1):
            tail_step(3 + r).wait_recv()
            value = value + tail_got[3 + r]
        tail_out[...] = value
    for j in range(n_chunks):
        value = total[j, pl.ds(pl.multiple_of(my_z * own, 16), own), :].astype(F32)
        for r in range(1, n_z):
            fourth(j, r).wait_recv()
            value = value + got4[j, r - 1].astype(F32)
        out[j] = value
    for j in range(n_chunks):
        for p in (0, 1):
            first(j, p).wait_send()
        for p in (0, 1) if kinds[j][1] else (0,):
            second(j, p).wait_send()
        third(j).wait_send()
        for r in range(1, n_z):
            fourth(j, r).wait_send()
    if n_tail:
        for step in range(3 + n_z - 1):
            tail_step(step).wait_send()


def sum_of(tails, row):
    n = len(tails) // 2
    if row == 0:
        return sum(tail[...] for tail in tails[:n])
    return sum(tail[2 * row - 2 : 2 * row] for tail in tails[n:])


def reduce_grads(chunks, tails, identity):
    n_sets = len(chunks[0][1])
    kinds = tuple((len(lefts) == 2, y_first) for lefts, _, y_first in chunks)
    rows, depth = chunks[0][0][0][0].shape
    cols = chunks[0][1][0].shape[1] // lax.axis_size("tp")
    n_z = lax.axis_size("fp")
    n = len(chunks)
    half, own = depth // 2, depth // (2 * n_z)
    operands = [a for lefts, _, _ in chunks for left in lefts for a in left]
    n_any = len(operands) + n * n_sets
    operands += [a for _, rights, _ in chunks for a in rights]
    operands += tails
    any_spec = pl.BlockSpec(memory_space=pl.ANY)
    vmem = pl.BlockSpec(memory_space=pltpu.VMEM)
    dma = pltpu.SemaphoreType.DMA
    outs = [jax.ShapeDtypeStruct((n, own, cols), F32)]
    scratch = [
        pltpu.VMEM((depth, rows * n_sets), BF) for kind in kinds for _ in range(2 if kind[0] else 1)
    ]
    scratch += [
        pltpu.VMEM((2, rows, depth), BF),
        pltpu.VMEM((2, rows * n_sets, cols), BF),
        pltpu.VMEM((n, 2, depth, cols), BF),
        pltpu.VMEM((n, 2, depth, cols), BF),
        pltpu.VMEM((n, 2, depth, cols), BF),
        pltpu.VMEM((n, depth, cols), BF),
        pltpu.VMEM((n, half, cols), BF),
        pltpu.VMEM((n, half, cols), BF),
        pltpu.VMEM((n, n_z - 1, own, cols), BF),
        dma((2,)),
        dma((2, n_sets)),
        dma((n, 2)),
        dma((n, 2)),
        dma((n, 2)),
        dma((n, 2)),
        dma((n,)),
        dma((n,)),
        dma((n, n_z - 1)),
        dma((n, n_z - 1)),
    ]
    if tails:
        n_rows = 8
        outs.append(jax.ShapeDtypeStruct((n_rows, depth), F32))
        scratch += [
            pltpu.VMEM((4, n_rows, depth), F32),
            pltpu.VMEM((2 + n_z, n_rows, depth), F32),
            dma((2 + n_z,)),
            dma((2 + n_z,)),
        ]
    return pl.pallas_call(
        partial(reduce_kernel, kinds, n_sets, len(tails)),
        in_specs=[any_spec] * n_any + [vmem] * len(tails),
        out_specs=[vmem] * len(outs),
        out_shape=outs,
        scratch_shapes=scratch,
        compiler_params=pltpu.CompilerParams(
            vmem_limit_bytes=62 * MIB, collective_id=identity, has_side_effects=True
        ),
        cost_estimate=pl.CostEstimate(
            flops=2 * n * 4 * depth * cols * rows * n_sets,
            bytes_accessed=n * 5 * rows * n_sets * cols * 2,
            transcendentals=0,
        ),
    )(*operands)


class Copies:
    def __init__(self, send, recv):
        self.send, self.recv, self.count, self.all = send, recv, 0, []

    def add(self, src, dst, peer):
        copy = pltpu.make_async_remote_copy(
            src_ref=src, dst_ref=dst, send_sem=self.send.at[self.count],
            recv_sem=self.recv.at[self.count], device_id=peer, device_id_type=MESH,
        )
        self.count += 1
        self.all.append(copy)
        return copy


def start_all(copies):
    for copy in copies:
        copy.start()


def arrive(copies):
    for copy in copies:
        copy.wait_recv()


N_REMOTE = 96
N_LOCAL = 24


def front_kernel(
    inputs, cot, shard, ln_shard,
    xs_out, time_in, cots, qkv_out, mixed_out, logsum_out,
    qkv_a, out_a, qkv_b, out_b, in_w, unit_w, norms,
    xs, sent, raw, std_qkv, std_out, ln, cot_half, qkv, mixed,
    send, recv, t_send, t_recv, local,
):
    my_tp, my_y, my_z = lax.axis_index("tp"), lax.axis_index("clip"), lax.axis_index("fp")
    n_tp, n_z = lax.axis_size("tp"), lax.axis_size("fp")
    micros, _, frames, part, width = inputs.shape
    places = part * n_tp
    chunk = places // n_z
    own = shard.shape[1]
    half = n_z * own
    cols = shard.shape[2]
    to_tp = [{"tp": my_tp ^ s} for s in range(n_tp)]
    to_core, to_x = to_tp[1], to_tp[2]
    to_y = {"clip": my_y ^ 1}
    to_z = [{"fp": my_z ^ r} for r in range(n_z)]
    peers = to_tp[1:] + to_z[1:] + [to_y]
    barrier = pltpu.get_barrier_semaphore()
    for peer in peers:
        pl.semaphore_signal(barrier, inc=1, device_id=peer, device_id_type=MESH)

    remote = Copies(send, recv)
    locals_ = []

    def here(src, dst):
        copy = pltpu.make_async_copy(src, dst, local.at[len(locals_)])
        locals_.append(copy)
        copy.start()
        return copy

    tiles = [raw.at[0], raw.at[1], in_w, unit_w]
    mine = pl.multiple_of(my_y * half + my_z * own, 16)
    near = pl.multiple_of(my_y * half, 16)
    far = pl.multiple_of((1 - my_y) * half, 16)
    away = my_tp ^ 2
    cuts = [cols // 2, 2 * cols // 3, 2 * cols // 3, 2 * cols // 3]
    own_shards = []
    by_z, by_x, by_y, by_y2, by_x2, by_core = [], [], [], [], [], []
    for j, tile in enumerate(tiles):
        cut = cuts[j]
        one, two = pl.ds(0, cut), pl.ds(cut, cols - cut)
        own_rows, near_rows, far_rows = pl.ds(mine, own), pl.ds(near, half), pl.ds(far, half)

        def same(peer, *index, tile=tile):
            return remote.add(tile.at[index], tile.at[index], peer)

        by_z.append(
            [
                remote.add(shard.at[j], tile.at[my_tp, own_rows], to_z[r])
                for r in range(1, n_z)
            ]
        )
        by_x.append(same(to_x, my_tp, near_rows, one))
        by_y.append([same(to_y, my_tp, near_rows, one), same(to_y, away, near_rows, one)])
        by_y2.append(same(to_y, my_tp, near_rows, two))
        by_x2.append(same(to_x, my_tp, slice(None), two))
        by_core.append(
            [
                same(to_core, my_tp, near_rows),
                same(to_core, away, near_rows, one),
                same(to_core, my_tp, far_rows, one),
                same(to_core, away, far_rows, one),
                same(to_core, my_tp, far_rows, two),
                same(to_core, away, slice(None), two),
            ]
        )
    ln_z = [
        remote.add(ln_shard, ln.at[pl.ds(mine, own)], to_z[r]) for r in range(1, n_z)
    ]
    ln_y = remote.add(ln.at[pl.ds(near, half)], ln.at[pl.ds(near, half)], to_y)
    x_in = [
        [
            remote.add(
                inputs.at[m, my_tp ^ s],
                xs.at[pl.ds(m * frames, frames), pl.ds(s * part, part)],
                to_tp[s],
            )
            for s in range(1, n_tp)
        ]
        for m in range(micros)
    ]
    cot_in = [
        [
            remote.add(
                cot.at[m, my_tp ^ s], cot_half.at[m, :, pl.ds(s * part, part)], to_tp[s]
            )
            for s in range(1, n_tp)
        ]
        for m in range(micros)
    ]
    cot_z = [
        [
            remote.add(
                cot_half.at[m, :, pl.ds(pl.multiple_of((my_z ^ r) * chunk, 16), chunk)],
                cots.at[m, r],
                to_z[r],
            )
            for r in range(1, n_z)
        ]
        for m in range(micros)
    ]

    own_x = [
        here(inputs.at[m, my_tp], xs.at[pl.ds(m * frames, frames), pl.ds(0, part)])
        for m in range(micros)
    ]
    own_cot = [here(cot.at[m, my_tp], cot_half.at[m, :, pl.ds(0, part)]) for m in range(micros)]
    own_w = [here(shard.at[j], tile.at[my_tp, pl.ds(mine, own)]) for j, tile in enumerate(tiles)]
    own_ln = here(ln_shard, ln.at[pl.ds(mine, own)])

    pl.semaphore_wait(barrier, len(peers))
    start_all(by_z[0] + ln_z + x_in[0])
    start_all(by_z[1] + x_in[1] + by_z[2] + by_z[3] + cot_in[0])

    def gather_start(j):
        own_w[j].wait()
        arrive(by_z[j])
        by_x[j].start()
        by_y2[j].start()
        by_core[j][0].start()

    def gather_first(j):
        by_x[j].wait_recv()
        start_all(by_y[j])
        by_core[j][1].start()

    def gather_second(j):
        by_y2[j].wait_recv()
        by_x2[j].start()
        by_core[j][4].start()

    def gather_last(j):
        arrive(by_y[j])
        start_all(by_core[j][2:4])
        by_x2[j].wait_recv()
        by_core[j][5].start()

    def standard(j):
        span = cols // 4
        for t in range(n_tp):
            for i in range(3):
                std_qkv[j, :, i * width + t * span : i * width + (t + 1) * span] = raw[
                    j, t, :, i * span : (i + 1) * span
                ]
            std_out[j, :, t * span : (t + 1) * span] = raw[j, t, :, 3 * span : 4 * span]

    gather_start(0)
    own_ln.wait()
    arrive(ln_z)
    ln_y.start()
    gather_first(0)
    gather_second(0)
    gather_start(1)
    gather_last(0)
    ln_y.wait_recv()
    norms[...] = ln[...].astype(F32).T[: norms.shape[0]]
    gather_start(2)
    arrive(by_core[0])
    standard(0)
    start_all(cot_in[1])
    own_x[0].wait()
    arrive(x_in[0])
    weights_out = [here(std_qkv.at[0], qkv_a), here(std_out.at[0], out_a)]

    def frame(f, carry):
        @pl.when(f == 1)
        def _():
            gather_first(1)
            gather_start(3)

        @pl.when(f == 2)
        def _():
            gather_second(1)
            own_cot[0].wait()
            arrive(cot_in[0])
            start_all(cot_z[0])

        @pl.when(f == 3)
        def _():
            gather_first(2)

        @pl.when(f == frames)
        def _():
            own_x[1].wait()
            arrive(x_in[1])
            gather_second(2)

        @pl.when(f == frames + 2)
        def _():
            gather_first(3)

        x = xs[f].astype(F32)
        unit, _ = normalise(x)
        normed = (unit * norms[0:1] + norms[1:2]).astype(BF)
        qkv[f] = dot(normed, std_qkv[0], NN).astype(BF)
        for g in range(width // WIDE):
            at = g * WIDE
            out, logsum = attend(
                qkv[f, :, at : at + WIDE],
                qkv[f, :, width + at : width + at + WIDE],
                qkv[f, :, 2 * width + at : 2 * width + at + WIDE],
                None,
            )
            mixed[f, :, at : at + WIDE] = out
            logsum_out[f, g : g + 1] = logsum
        sent[f] = (x + dot(mixed[f], std_out[0], NT)).astype(BF)
        m, at_frame = f // frames, lax.rem(f, frames)
        for r in range(n_z):
            src = sent.at[f, pl.ds(pl.multiple_of((my_z ^ r) * chunk, 16), chunk)]
            dst = time_in.at[m, r, at_frame]
            if r == 0:
                pltpu.make_async_copy(src, dst, t_send.at[m, 0]).start()
            else:
                pltpu.make_async_remote_copy(
                    src_ref=src, dst_ref=dst, send_sem=t_send.at[m, r],
                    recv_sem=t_recv.at[m, r], device_id=to_z[r], device_id_type=MESH,
                ).start()
        return carry

    lax.fori_loop(0, micros * frames, frame, 0)
    kept = [here(xs, xs_out), here(qkv, qkv_out), here(mixed, mixed_out)]
    gather_last(1)
    own_cot[1].wait()
    arrive(cot_in[1])
    start_all(cot_z[1])
    gather_second(3)
    arrive(by_core[1])
    standard(1)
    weights_out += [here(std_qkv.at[1], qkv_b), here(std_out.at[1], out_b)]
    own_cots = [
        here(cot_half.at[m, :, pl.ds(pl.multiple_of(my_z * chunk, 16), chunk)], cots.at[m, 0])
        for m in range(micros)
    ]
    gather_last(2)
    gather_last(3)
    arrive(by_core[2])
    arrive(by_core[3])
    for m in range(micros):
        arrive(cot_z[m])
        for r in range(n_z):
            src = sent.at[
                pl.ds(m * frames, frames), pl.ds(pl.multiple_of((my_z ^ r) * chunk, 16), chunk)
            ]
            dst = time_in.at[m, r]
            if r == 0:
                pltpu.make_async_copy(src, dst, t_send.at[m, 0]).wait()
            else:
                pltpu.make_async_remote_copy(
                    src_ref=src, dst_ref=dst, send_sem=t_send.at[m, r],
                    recv_sem=t_recv.at[m, r], device_id=to_z[r], device_id_type=MESH,
                ).wait()
    for copy in remote.all:
        copy.wait_send()
    for copy in kept + weights_out + own_cots:
        copy.wait()


def front(inputs, cot, shard, ln_shard):
    micros, clips, frames, part, width = inputs.shape
    n_tp, n_z = lax.axis_size("tp"), lax.axis_size("fp")
    places = part * n_tp
    total = micros * frames
    chunk = places // n_z
    cols = shard.shape[2]
    groups = width // WIDE
    any_spec = pl.BlockSpec(memory_space=pl.ANY)
    vmem = pl.BlockSpec(memory_space=pltpu.VMEM)
    dma = pltpu.SemaphoreType.DMA
    shape = jax.ShapeDtypeStruct
    weights = [(width, 3 * width), (width, width)] * 2 + [(n_tp, width, cols)] * 2
    return pl.pallas_call(
        front_kernel,
        in_specs=[any_spec] * 4,
        out_specs=[any_spec] * 5 + [vmem] + [any_spec] * 6 + [vmem],
        out_shape=[
            shape((total, places, width), BF),
            shape((micros, n_z, frames, chunk, width), BF),
            shape((micros, n_z, frames, chunk, width), BF),
            shape((total, places, 3 * width), BF),
            shape((total, places, width), BF),
            shape((total, groups, GROUP * places), F32),
        ]
        + [shape(dims, BF) for dims in weights]
        + [shape((8, width), F32)],
        scratch_shapes=[
            pltpu.VMEM((total, places, width), BF),
            pltpu.VMEM((total, places, width), BF),
            pltpu.VMEM((2, n_tp, width, cols), BF),
            pltpu.VMEM((2, width, 3 * width), BF),
            pltpu.VMEM((2, width, width), BF),
            pltpu.VMEM((width, ln_shard.shape[1]), BF),
            pltpu.VMEM((micros, frames, places, width), BF),
            pltpu.VMEM((total, places, 3 * width), BF),
            pltpu.VMEM((total, places, width), BF),
            dma((N_REMOTE,)),
            dma((N_REMOTE,)),
            dma((micros, n_z)),
            dma((micros, n_z)),
            dma((N_LOCAL,)),
        ],
        compiler_params=pltpu.CompilerParams(
            vmem_limit_bytes=60 * MIB, collective_id=3, has_side_effects=True
        ),
        cost_estimate=pl.CostEstimate(
            flops=2 * total * places * width * 5 * width,
            bytes_accessed=total * places * width * 16,
            transcendentals=0,
        ),
    )(inputs, cot, shard, ln_shard)


def to_peer(value, axis, step):
    n = lax.axis_size(axis)
    return lax.ppermute(value, axis, [(i, i ^ step) for i in range(n)])


def swap(pieces, axis):
    return [piece if s == 0 else to_peer(piece, axis, s) for s, piece in enumerate(pieces)]


def pick(stack, index):
    return lax.dynamic_index_in_dim(stack, index, 0, keepdims=False)


def shards(
    inputs, cotangent, qkv_weight, out_spatial, out_temporal, mlp_in, mlp_out, ln_gain, ln_bias
):
    micros, clips, frames, local, width = inputs.shape
    n_tp, n_fp = lax.axis_size("tp"), lax.axis_size("fp")
    n_cf = lax.axis_size("clip") * n_fp
    assert clips == n_tp
    my_tp, my_fp = lax.axis_index("tp"), lax.axis_index("fp")
    depth = qkv_weight.shape[2]
    span = qkv_weight.shape[3]
    places = n_tp * local
    chunk = places // n_fp
    at = my_fp.astype(jnp.int32)[None]

    first = jnp.concatenate([qkv_weight[0, i] for i in range(3)] + [out_spatial.T], axis=1)
    second = jnp.concatenate([qkv_weight[1, i] for i in range(3)] + [out_temporal.T], axis=1)
    axes = ("clip", "fp", "tp")
    ln_rows = [v[i] for i in range(3) for v in (ln_gain, ln_bias)]
    whole_rows = depth % 16 == 0 and n_tp == 4 and lax.axis_size("clip") == 2

    def from_chunks(chunks):
        stack = jnp.stack(chunks)
        joined = jnp.concatenate([pick(stack, my_fp ^ c) for c in range(n_fp)], axis=1)
        return [joined[:, s * local : (s + 1) * local] for s in range(n_tp)]

    def outward(pieces):
        stack = jnp.stack(swap(pieces, "tp"))
        return jnp.stack([pick(stack, my_tp ^ c) for c in range(n_tp)])

    if whole_rows:
        ln_shard = jnp.stack(ln_rows + [jnp.zeros_like(ln_rows[0])] * 122, axis=1)
        shard = jnp.stack([first, second, mlp_in, mlp_out.T])
        (
            xs, time_pieces, cots, qkv, mixed, logsum,
            qkv_space_w, out_space_w, qkv_time_w, out_time_w, in_w, unit_w, norms,
        ) = front(inputs, cotangent, shard, ln_shard)
        space_kept = [([xs], qkv, mixed, logsum, m * frames) for m in range(micros)]
        time_given = [([time_pieces], [cots], m) for m in range(micros)]
    else:

        def gathered(part):
            return lax.all_gather(part, axes).reshape(n_cf, n_tp, depth, part.shape[1])

        def attention_weights(raw):
            raw = raw.reshape(n_cf, n_tp, depth, 4, span).transpose(3, 0, 2, 1, 4)
            raw = raw.reshape(4, n_cf * depth, n_tp * span)
            return jnp.concatenate([raw[0], raw[1], raw[2]], axis=1), raw[3]

        def unit_weights(raw):
            return raw.transpose(1, 0, 2, 3).reshape(n_tp, n_cf * depth, raw.shape[3])

        norms = lax.all_gather(jnp.stack(ln_rows), ("clip", "fp"))
        norms = norms.transpose(1, 0, 2).reshape(6, n_cf * depth).astype(F32)
        qkv_space_w, out_space_w = attention_weights(gathered(first))
        rest = gathered(jnp.concatenate([second, mlp_in, mlp_out.T], axis=1))
        qkv_time_w, out_time_w = attention_weights(rest[..., : 4 * span])
        in_w = unit_weights(rest[..., 4 * span : 4 * span + mlp_in.shape[1]])
        unit_w = unit_weights(rest[..., 4 * span + mlp_in.shape[1] :])

        def inward(array, m):
            return swap([pick(array[m], my_tp ^ s) for s in range(n_tp)], "tp")

        def to_chunks(pieces):
            joined = jnp.concatenate(pieces, axis=1)
            return [
                lax.dynamic_slice_in_dim(joined, (my_fp ^ r) * chunk, chunk, 1)
                for r in range(n_fp)
            ]

        space_kept, time_given = [], []
        for m in range(micros):
            x = inward(inputs, m)
            cots = swap(to_chunks(inward(cotangent, m)), "fp")
            out = space_forward(x, qkv_space_w, out_space_w, norms, at, n_fp)
            time_given.append((swap(out[:n_fp], "fp"), cots, None))
            space_kept.append((x,) + tuple(out[n_fp:]) + (0,))
    time_kept = []
    results = []
    space_grads = []
    for m in range(micros):
        pieces, cots, which = time_given[m]
        out = time_layer(pieces, cots, qkv_time_w, out_time_w, in_w, unit_w, norms, which)
        results.append(outward(from_chunks(swap(out[:n_fp], "fp"))))
        space_grads.append(swap(out[n_fp : 2 * n_fp], "fp"))
        time_kept.append(out[2 * n_fp :])
    space_rows = []
    input_grads = []
    flat = lambda v: v.reshape(-1, v.shape[-1])
    kept = lambda i: [k[i] for k in time_kept]
    time_chunks = [
        ([kept(3)], kept(4), True),
        ([kept(6)], kept(5), False),
        ([kept(0), kept(2)], kept(1), True),
    ]
    if whole_rows:
        (late,) = reduce_grads(time_chunks, [], 1)
    for m in range(micros):
        x, qkv, mixed, logsum, skip = space_kept[m]
        out = space_backward(
            x, space_grads[m], qkv, mixed, logsum, qkv_space_w, out_space_w, norms, at, skip, n_tp
        )
        input_grads.append(outward(out[:n_tp]).astype(F32))
        normed, low, columns, norm_grad = out[n_tp:]
        space_rows.append((flat(normed), flat(low), flat(columns), norm_grad))
    back = lambda i: [k[i] for k in space_rows]
    space_chunk = ([back(0), back(1)], back(2), True)
    tails = back(3) + kept(7)
    if whole_rows:
        early, norm_grads = reduce_grads([space_chunk], tails, 2)
    else:
        early = scatter_grads([space_chunk], n_cf, n_tp)
        late = scatter_grads(time_chunks, n_cf, n_tp)
        norm_grads = lax.psum(jnp.concatenate([sum(back(3)), sum(kept(7))]), axes)
    norm_grads = norm_grads[:6].reshape(3, 2, n_cf, depth)
    mine = lax.axis_index("clip") * n_fp + my_fp
    norm_grads = lax.dynamic_index_in_dim(norm_grads, mine, 2, keepdims=False)
    kinds = lambda v: [v[:, i * span : (i + 1) * span] for i in range(4)]
    space_g, time_g = kinds(early[0]), kinds(late[2])
    return (
        jnp.stack(results),
        jnp.stack(input_grads),
        jnp.stack([jnp.stack(space_g[:3]), jnp.stack(time_g[:3])]),
        space_g[3].T,
        time_g[3].T,
        late[0],
        late[1].T,
        norm_grads[:, 0],
        norm_grads[:, 1],
    )


def scatter_grads(chunks, n_cf, n_tp):
    tiles = []
    for lefts, rights, _ in chunks:
        cols = rights[0].shape[1] // n_tp
        total = sum(dot(a, b, TN) for a, b in zip(lefts[0], rights))
        total = total.reshape(total.shape[0], n_tp, cols)
        if len(lefts) == 2:
            other = sum(dot(a, b, TN) for a, b in zip(lefts[1], rights))
            other = other.reshape(other.shape[0], n_tp, cols)
            at = 3 * cols // 4
            total = jnp.concatenate([total[..., :at], other[..., at:]], axis=2)
        total = total.reshape(n_cf, total.shape[0] // n_cf, n_tp, cols).transpose(0, 2, 1, 3)
        tiles.append(total.reshape((n_cf * n_tp,) + total.shape[2:]))
    return lax.psum_scatter(jnp.stack(tiles, 1), ("clip", "fp", "tp"), scatter_dimension=0)


def solution(mesh):
    spread = P(None, "clip", "fp", "tp", None)
    return jax.shard_map(
        shards,
        mesh=mesh,
        in_specs=(
            spread,
            spread,
            P(None, None, ("clip", "fp"), "tp"),
            P("tp", ("clip", "fp")),
            P("tp", ("clip", "fp")),
            P(("clip", "fp"), "tp"),
            P("tp", ("clip", "fp")),
            P(None, ("clip", "fp")),
            P(None, ("clip", "fp")),
        ),
        out_specs=(
            spread,
            spread,
            P(None, None, ("clip", "fp"), "tp"),
            P("tp", ("clip", "fp")),
            P("tp", ("clip", "fp")),
            P(("clip", "fp"), "tp"),
            P("tp", ("clip", "fp")),
            P(None, ("clip", "fp")),
            P(None, ("clip", "fp")),
        ),
        check_vma=False,
    )
```

```python
from functools import partial

import jax
import jax.numpy as jnp
from jax import lax
from jax.experimental import pallas as pl
from jax.experimental.pallas import tpu as pltpu
from jax.sharding import PartitionSpec as P

HD = 64
GROUP = 4
WIDE = GROUP * HD
EPS = 1e-06
BF = jnp.bfloat16
F32 = jnp.float32
MIB = 1024 * 1024
MESH = pl.DeviceIdType.MESH

NN = (((1,), (0,)), ((), ()))
NT = (((1,), (1,)), ((), ()))
TN = (((0,), (0,)), ((), ()))


def dot(a, b, dims):
    return lax.dot_general(a, b, dims, preferred_element_type=F32)


def normalise(values):
    centre = values - jnp.mean(values, axis=-1, keepdims=True)
    spread = jnp.mean(centre * centre, axis=-1, keepdims=True)
    rate = lax.rsqrt(spread + EPS)
    return centre * rate, rate


def norm_back(upstream, gain, unit, rate):
    weighted = upstream * gain
    inner = jnp.mean(weighted * unit, axis=-1, keepdims=True)
    return rate * (weighted - jnp.mean(weighted, axis=-1, keepdims=True) - unit * inner)


def head_masks(scale):
    lanes = lax.broadcasted_iota(jnp.int32, (1, WIDE), 1) // HD
    return [jnp.where(lanes == h, scale, 0.0).astype(BF) for h in range(GROUP)]


def spread_heads(block, masks):
    return jnp.concatenate([block * mask for mask in masks], axis=0)


def gather_heads(stacked, rows):
    lanes = lax.broadcasted_iota(jnp.int32, (1, WIDE), 1) // HD
    total = stacked[:rows]
    for h in range(1, GROUP):
        total = jnp.where(lanes == h, stacked[h * rows : (h + 1) * rows], total)
    return total


def attend(queries, keys, values, bias):
    rows = queries.shape[0]
    scores = dot(keys, spread_heads(queries, head_masks(HD**-0.5)), NT)
    if bias is not None:
        scores = scores + bias
    top = jnp.max(scores, axis=0, keepdims=True)
    exponent = jnp.exp(scores - top)
    totals = jnp.sum(exponent, axis=0, keepdims=True)
    weights = (exponent * (1.0 / totals)).astype(BF)
    mixed = gather_heads(dot(weights, values, TN), rows).astype(BF)
    return mixed, top + jnp.log(totals)


def attend_back(queries, keys, values, upstream, logsum, bias):
    rows = queries.shape[0]
    spread_q = spread_heads(queries, head_masks(HD**-0.5))
    spread_g = spread_heads(upstream, head_masks(1.0))
    scores = dot(keys, spread_q, NT)
    if bias is not None:
        scores = scores + bias
    probs = jnp.exp(scores - logsum)
    grad_probs = dot(values, spread_g, NT)
    inner = jnp.sum(probs * grad_probs, axis=0, keepdims=True)
    grad_scores = (probs * (grad_probs - inner)).astype(BF)
    grad_values = dot(probs.astype(BF), spread_g, NN)
    grad_keys = dot(grad_scores, spread_q, NN)
    grad_queries = gather_heads(dot(grad_scores, keys, TN), rows) * HD**-0.5
    return grad_queries.astype(BF), grad_keys.astype(BF), grad_values.astype(BF)


def gelu_parts(pre):
    size = jnp.abs(pre) * (0.5**0.5)
    t = 1.0 / (1.0 + 0.3275911 * size)
    bell = jnp.exp(-size * size)
    poly = t * (
        0.254829592
        + t * (-0.284496736 + t * (1.421413741 + t * (-1.453152027 + t * 1.061405429)))
    )
    tail = 0.5 * poly * bell
    return jnp.where(pre >= 0, 1.0 - tail, tail), bell * 0.3989422804014327


def space_forward_kernel(n_in, n_out, at_ref, *refs):
    pieces = refs[:n_in]
    qkv_w, out_w, norm = refs[n_in : n_in + 3]
    outs = refs[n_in + 3 : n_in + 3 + n_out]
    qkv_out, mixed_out, logsum_out, held = refs[n_in + 3 + n_out :]
    width = out_w.shape[1]
    x = jnp.concatenate([piece[0] for piece in pieces], axis=0).astype(F32)
    unit, _ = normalise(x)
    normed = (unit * norm[0:1] + norm[1:2]).astype(BF)
    qkv_out[0] = dot(normed, qkv_w[...], NN).astype(BF)
    for g in range(width // WIDE):
        at = g * WIDE
        mixed, logsum = attend(
            qkv_out[0, :, at : at + WIDE],
            qkv_out[0, :, width + at : width + at + WIDE],
            qkv_out[0, :, 2 * width + at : 2 * width + at + WIDE],
            None,
        )
        mixed_out[0, :, at : at + WIDE] = mixed
        logsum_out[0, g : g + 1] = logsum
    held[...] = x + dot(mixed_out[0], out_w[...], NT)
    rows = outs[0].shape[1]
    for r, out in enumerate(outs):
        start = pl.multiple_of((at_ref[0] ^ r) * rows, 8)
        out[0] = held[pl.ds(start, rows), :].astype(BF)


def space_forward(pieces, qkv_w, out_w, norm, at, n_out):
    frames, rows, width = pieces[0].shape
    places = rows * len(pieces)
    groups = width // WIDE
    whole = pl.BlockSpec(memory_space=pltpu.VMEM)
    frame = lambda *dims: pl.BlockSpec((1,) + dims, lambda f, at: (f,) + (0,) * len(dims))
    return pl.pallas_call(
        partial(space_forward_kernel, len(pieces), n_out),
        grid_spec=pltpu.PrefetchScalarGridSpec(
            num_scalar_prefetch=1,
            grid=(frames,),
            in_specs=[frame(rows, width)] * len(pieces) + [whole] * 3,
            out_specs=[frame(places // n_out, width)] * n_out
            + [frame(places, 3 * width), frame(places, width), frame(groups, GROUP * places)],
            scratch_shapes=[pltpu.VMEM((places, width), F32)],
        ),
        out_shape=[jax.ShapeDtypeStruct((frames, places // n_out, width), BF)] * n_out
        + [
            jax.ShapeDtypeStruct((frames, places, 3 * width), BF),
            jax.ShapeDtypeStruct((frames, places, width), BF),
            jax.ShapeDtypeStruct((frames, groups, GROUP * places), F32),
        ],
        compiler_params=pltpu.CompilerParams(vmem_limit_bytes=48 * MIB),
        cost_estimate=pl.CostEstimate(
            flops=2 * frames * places * width * 5 * width,
            bytes_accessed=frames * places * width * 16,
            transcendentals=0,
        ),
    )(at, *pieces, qkv_w, out_w, norm)


def store_columns(out, kinds, n_parts):
    width = kinds[0].shape[1]
    span = width // n_parts
    for t in range(n_parts):
        for i, kind in enumerate(kinds):
            start = (t * len(kinds) + i) * span
            out[:, start : start + span] = kind[:, t * span : (t + 1) * span]


def space_backward_kernel(n_in, n_grad, n_out, at_ref, *refs):
    pieces = refs[:n_in]
    grads = refs[n_in : n_in + n_grad]
    qkv_in, mixed_in, logsum_in, qkv_w, out_w, norm = refs[n_in + n_grad : n_in + n_grad + 6]
    rest = refs[n_in + n_grad + 6 :]
    outs = rest[:n_out]
    normed_out, grad_out, columns, norm_out, held, dqkv = rest[n_out:]
    width = out_w.shape[1]
    rows = grads[0].shape[1]
    for r, grad in enumerate(grads):
        start = pl.multiple_of((at_ref[0] ^ r) * rows, 8)
        held[pl.ds(start, rows), :] = grad[0].astype(F32)
    x = jnp.concatenate([piece[0] for piece in pieces], axis=0).astype(F32)
    unit, rate = normalise(x)
    normed_out[0] = (unit * norm[0:1] + norm[1:2]).astype(BF)
    low = held[...].astype(BF)
    grad_out[0] = low
    grad_mixed = dot(low, out_w[...], NN).astype(BF)
    for g in range(width // WIDE):
        at = g * WIDE
        parts = attend_back(
            qkv_in[0, :, at : at + WIDE],
            qkv_in[0, :, width + at : width + at + WIDE],
            qkv_in[0, :, 2 * width + at : 2 * width + at + WIDE],
            grad_mixed[:, at : at + WIDE],
            logsum_in[0, g : g + 1],
            None,
        )
        for i, part in enumerate(parts):
            dqkv[:, i * width + at : i * width + at + WIDE] = part
    store_columns(
        columns.at[0],
        [dqkv[:, i * width : (i + 1) * width] for i in range(3)] + [mixed_in[0]],
        n_out,
    )
    grad_normed = dot(dqkv[...], qkv_w[...], NT)

    @pl.when(pl.program_id(0) == 0)
    def _():
        norm_out[...] = jnp.zeros_like(norm_out)

    norm_out[0:1] += jnp.sum(grad_normed * unit, axis=0, keepdims=True)
    norm_out[1:2] += jnp.sum(grad_normed, axis=0, keepdims=True)
    total = held[...] + norm_back(grad_normed, norm[0:1], unit, rate)
    rows = outs[0].shape[1]
    for s, out in enumerate(outs):
        out[0] = total[s * rows : (s + 1) * rows].astype(BF)


def space_backward(pieces, grads, qkv, mixed, logsum, qkv_w, out_w, norm, at, first, n_out):
    frames, width = grads[0].shape[0], grads[0].shape[2]
    places = grads[0].shape[1] * len(grads)
    rows = places // n_out
    groups = width // WIDE
    n_grad = len(grads)
    whole = pl.BlockSpec(memory_space=pltpu.VMEM)
    frame = lambda *dims: pl.BlockSpec((1,) + dims, lambda f, at: (f,) + (0,) * len(dims))
    later = lambda *dims: pl.BlockSpec((1,) + dims, lambda f, at: (f + first,) + (0,) * len(dims))
    return pl.pallas_call(
        partial(space_backward_kernel, len(pieces), n_grad, n_out),
        grid_spec=pltpu.PrefetchScalarGridSpec(
            num_scalar_prefetch=1,
            grid=(frames,),
            in_specs=[later(places // len(pieces), width)] * len(pieces)
            + [frame(places // n_grad, width)] * n_grad
            + [later(places, 3 * width), later(places, width), later(groups, GROUP * places)]
            + [whole] * 3,
            out_specs=[frame(rows, width)] * n_out
            + [frame(places, width), frame(places, width), frame(places, 4 * width)]
            + [pl.BlockSpec((2, width), lambda f, at: (0, 0))],
            scratch_shapes=[
                pltpu.VMEM((places, width), F32),
                pltpu.VMEM((places, 3 * width), BF),
            ],
        ),
        out_shape=[jax.ShapeDtypeStruct((frames, rows, width), BF)] * n_out
        + [
            jax.ShapeDtypeStruct((frames, places, width), BF),
            jax.ShapeDtypeStruct((frames, places, width), BF),
            jax.ShapeDtypeStruct((frames, places, 4 * width), BF),
            jax.ShapeDtypeStruct((2, width), F32),
        ],
        compiler_params=pltpu.CompilerParams(vmem_limit_bytes=48 * MIB),
        cost_estimate=pl.CostEstimate(
            flops=2 * frames * places * width * 7 * width,
            bytes_accessed=frames * places * width * 24,
            transcendentals=0,
        ),
    )(at, *pieces, *grads, qkv, mixed, logsum, qkv_w, out_w, norm)


def time_kernel(joint, n_in, n_parts, sub, *refs):
    n_arrays = 1 if joint else n_in
    pieces = refs[:n_arrays]
    cots = refs[n_arrays : 2 * n_arrays]
    qkv_w, out_w, in_w, unit_w, norm = refs[2 * n_arrays : 2 * n_arrays + 5]
    rest = refs[2 * n_arrays + 5 :]
    results = rest[:n_arrays]
    grads = rest[n_arrays : 2 * n_arrays]
    (
        normed_time,
        columns,
        grad_time,
        normed_mlp,
        grad_pre,
        hidden,
        grad_result,
        norm_out,
        qkv,
        dqkv,
        mixed,
        probs_logsum,
    ) = rest[2 * n_arrays : 2 * n_arrays + 12]
    if joint:
        step, steps = pl.program_id(0), pl.num_programs(0)
        outgoing, send, recv = rest[2 * n_arrays + 12 :]
        my_z = lax.axis_index("fp")
        to_z = [{"fp": my_z ^ r} for r in range(n_in)]

        @pl.when(step == 0)
        def _():
            barrier = pltpu.get_barrier_semaphore()
            for peer in to_z[1:]:
                pl.semaphore_signal(barrier, inc=1, device_id=peer, device_id_type=MESH)
            pl.semaphore_wait(barrier, n_in - 1)

    width = out_w.shape[1]
    frames, places = results[0].shape[-3:-1]
    all_frames = frames * n_in
    rows = all_frames * sub
    parts = places // sub

    def tokens(blocks):
        blocks = [b[...].reshape(-1, places, width) for b in blocks]
        joined = jnp.concatenate(blocks, axis=0).astype(F32)
        return jnp.concatenate(
            [joined[:, j * sub : (j + 1) * sub, :].reshape(rows, width) for j in range(parts)],
            axis=0,
        )

    def scatter(values, outs):
        grid = jnp.concatenate(
            [
                values[j * rows : (j + 1) * rows].reshape(all_frames, sub, width)
                for j in range(parts)
            ],
            axis=1,
        ).astype(BF)
        if len(outs) == 1:
            outs[0][...] = grid.reshape(outs[0].shape)
        else:
            for r, out in enumerate(outs):
                out[...] = grid[r * frames : (r + 1) * frames]

    key_place = lax.broadcasted_iota(jnp.int32, (rows, GROUP * rows), 0) % sub
    query_place = lax.broadcasted_iota(jnp.int32, (rows, GROUP * rows), 1) % sub
    bias = jnp.where(key_place == query_place, 0.0, -1e30)

    after_space = tokens(pieces)
    unit, rate = normalise(after_space)
    normed_time[...] = (unit * norm[2:3] + norm[3:4]).astype(BF)
    qkv[...] = dot(normed_time[...], qkv_w[...], NN).astype(BF)
    groups = width // WIDE
    for j in range(parts):
        at_rows = slice(j * rows, (j + 1) * rows)
        for g in range(groups):
            at = g * WIDE
            out, logsum = attend(
                qkv[at_rows, at : at + WIDE],
                qkv[at_rows, width + at : width + at + WIDE],
                qkv[at_rows, 2 * width + at : 2 * width + at + WIDE],
                bias,
            )
            mixed[at_rows, at : at + WIDE] = out
            probs_logsum[j * groups + g : j * groups + g + 1] = logsum
    after_time = after_space + dot(mixed[...], out_w[...], NT)
    unit2, rate2 = normalise(after_time)
    normed_mlp[...] = (unit2 * norm[4:5] + norm[5:6]).astype(BF)
    cot = tokens(cots)
    grad_result[...] = cot.astype(BF)
    result = after_time
    grad_normed = None
    for c in range(in_w.shape[0]):
        cols = slice(c * in_w.shape[2], (c + 1) * in_w.shape[2])
        pre = dot(normed_mlp[...], in_w[c], NN)
        below, density = gelu_parts(pre)
        hidden[:, cols] = (pre * below).astype(BF)
        result = result + dot(hidden[:, cols], unit_w[c], NT)
        grad_hidden = dot(grad_result[...], unit_w[c], NN)
        grad_pre[:, cols] = (grad_hidden * (below + pre * density)).astype(BF)
        term = dot(grad_pre[:, cols], in_w[c], NT)
        grad_normed = term if c == 0 else grad_normed + term
    scatter(result, results)

    @pl.when(pl.program_id(0) == 0)
    def _():
        norm_out[...] = jnp.zeros_like(norm_out)

    norm_out[2:3] += jnp.sum(grad_normed * unit2, axis=0, keepdims=True)
    norm_out[3:4] += jnp.sum(grad_normed, axis=0, keepdims=True)
    grad_after = cot + norm_back(grad_normed, norm[4:5], unit2, rate2)
    grad_time[...] = grad_after.astype(BF)
    grad_mixed = dot(grad_time[...], out_w[...], NN).astype(BF)
    for j in range(parts):
        at_rows = slice(j * rows, (j + 1) * rows)
        for g in range(groups):
            at = g * WIDE
            back = attend_back(
                qkv[at_rows, at : at + WIDE],
                qkv[at_rows, width + at : width + at + WIDE],
                qkv[at_rows, 2 * width + at : 2 * width + at + WIDE],
                grad_mixed[at_rows, at : at + WIDE],
                probs_logsum[j * groups + g : j * groups + g + 1],
                bias,
            )
            for i, part in enumerate(back):
                dqkv[at_rows, i * width + at : i * width + at + WIDE] = part
    store_columns(
        columns,
        [dqkv[:, i * width : (i + 1) * width] for i in range(3)] + [mixed[...]],
        n_parts,
    )
    grad_normed = dot(dqkv[...], qkv_w[...], NT)
    norm_out[0:1] += jnp.sum(grad_normed * unit, axis=0, keepdims=True)
    norm_out[1:2] += jnp.sum(grad_normed, axis=0, keepdims=True)
    grad_space = grad_after + norm_back(grad_normed, norm[2:3], unit, rate)
    if not joint:
        scatter(grad_space, grads)
        return
    scatter(grad_space, [outgoing.at[step]])
    received = grads[0]
    micros = received.shape[0]
    each = received.shape[3] // places
    m, at = step // each, pl.multiple_of(lax.rem(step, each) * places, 8)
    for r in range(n_in):
        src, dst = outgoing.at[step, r], received.at[m, r, :, pl.ds(at, places)]
        if r == 0:
            pltpu.make_async_copy(src, dst, send.at[m, 0]).start()
        else:
            pltpu.make_async_remote_copy(
                src_ref=src, dst_ref=dst, send_sem=send.at[m, r], recv_sem=recv.at[m, r],
                device_id=to_z[r], device_id_type=MESH,
            ).start()

    @pl.when(step == steps - 1)
    def _():
        for m in range(micros):
            for r in range(n_in):
                src = outgoing.at[pl.ds(m * each, each), r]
                dst = received.at[m, r]
                if r == 0:
                    pltpu.make_async_copy(dst, dst, send.at[m, 0]).wait()
                else:
                    for ref, wait in ((src, "wait_send"), (dst, "wait_recv")):
                        copy = pltpu.make_async_remote_copy(
                            src_ref=ref, dst_ref=ref, send_sem=send.at[m, r],
                            recv_sem=recv.at[m, r], device_id=to_z[r], device_id_type=MESH,
                        )
                        getattr(copy, wait)()


def time_layer(pieces, cots, qkv_w, out_w, in_w, unit_w, norm):
    joint = len(pieces) == 1
    frames, places, width = pieces[0].shape[-3:]
    n_in = pieces[0].shape[1] if joint else len(pieces)
    micros = pieces[0].shape[0] if joint else 1
    block = 16 if places % 16 == 0 else 8
    each = places // block
    sub = 8
    tokens = frames * n_in * block
    count = frames * n_in * places * micros
    hidden = in_w.shape[0] * in_w.shape[2]
    whole = pl.BlockSpec(memory_space=pltpu.VMEM)
    if joint:
        piece = pl.BlockSpec(
            (None, n_in, frames, block, width), lambda b: (b // each, 0, 0, b % each, 0)
        )
        moved = [piece, pl.BlockSpec(memory_space=pl.ANY)]
    else:
        piece = pl.BlockSpec((frames, block, width), lambda b: (0, b, 0))
        moved = [piece] * (2 * n_in)
    row = lambda cols: pl.BlockSpec((tokens, cols), lambda b: (b, 0))
    kept = [width, 4 * width, width, width, hidden, hidden, width]
    dma = pltpu.SemaphoreType.DMA
    sending = [
        pltpu.VMEM((micros * each, n_in, frames, block, width), BF),
        dma((micros, n_in)),
        dma((micros, n_in)),
    ]
    return pl.pallas_call(
        partial(time_kernel, joint, n_in, in_w.shape[0], sub),
        grid=(micros * each,),
        in_specs=[piece] * (2 * len(pieces)) + [whole] * 5,
        out_specs=moved + [row(cols) for cols in kept] + [pl.BlockSpec((4, width), lambda b: (0, 0))],
        out_shape=[jax.ShapeDtypeStruct(pieces[0].shape, BF)] * (2 * len(pieces))
        + [jax.ShapeDtypeStruct((count, cols), BF) for cols in kept]
        + [jax.ShapeDtypeStruct((4, width), F32)],
        scratch_shapes=[
            pltpu.VMEM((tokens, 3 * width), BF),
            pltpu.VMEM((tokens, 3 * width), BF),
            pltpu.VMEM((tokens, width), BF),
            pltpu.VMEM((8 * (block // sub), GROUP * frames * n_in * sub), F32),
        ]
        + (sending if joint else []),
        compiler_params=pltpu.CompilerParams(
            vmem_limit_bytes=60 * MIB,
            collective_id=4 if joint else None,
            has_side_effects=joint,
        ),
        cost_estimate=pl.CostEstimate(
            flops=2 * count * width * 2 * (4 * width + 2 * hidden),
            bytes_accessed=count * 26000,
            transcendentals=0,
        ),
    )(*pieces, *cots, qkv_w, out_w, in_w, unit_w, norm)


STEP = 192


class Copies:
    def __init__(self, send, recv):
        self.send, self.recv, self.count, self.all = send, recv, 0, []

    def add(self, src, dst, peer):
        copy = pltpu.make_async_remote_copy(
            src_ref=src, dst_ref=dst, send_sem=self.send.at[self.count],
            recv_sem=self.recv.at[self.count], device_id=peer, device_id_type=MESH,
        )
        self.count += 1
        self.all.append(copy)
        return copy


def start_all(copies):
    for copy in copies:
        copy.start()


def arrive(copies):
    for copy in copies:
        copy.wait_recv()


def blocks(count, body):
    lax.fori_loop(
        0, count // STEP, lambda i, _: body(pl.ds(pl.multiple_of(i * STEP, STEP), STEP)), None
    )


def back_kernel(
    results, grads, xs, qkv_in, mixed_in, logsum_in, qkv_w, out_w, norm_in,
    tail_time, rows_c, cols_c, rows_d, cols_d, rows_b, rows_b2, cols_b,
    out, tail_out, acts, input_grad, normed_a, low_a, cols_a, res_half,
    turned, stage, tile_in, sent, got1, held, got2, got3, total, got4,
    w_qkv, w_out, norm, logsum, dqkv, tail_sum, tail_got,
    stage_sem, tile_sem, frame_sem, out_sem, load_sem, send, recv, r_send, r_recv, i_send, i_recv,
):
    my_tp, my_y, my_z = lax.axis_index("tp"), lax.axis_index("clip"), lax.axis_index("fp")
    n_tp, n_z = lax.axis_size("tp"), lax.axis_size("fp")
    core, x = lax.rem(my_tp, 2), my_tp // 2
    micros, _, frames, chunk, width = results.shape
    places = chunk * n_z
    part = places // n_tp
    depth, cols = held.shape[2:]
    half, own = depth // 2, depth // (2 * n_z)
    all_rows = tile_in.shape[1]
    to_tp = [{"tp": my_tp ^ s} for s in range(n_tp)]
    to_core, to_x = to_tp[1], to_tp[2]
    to_y = {"clip": my_y ^ 1}
    to_z = [{"fp": my_z ^ r} for r in range(n_z)]
    peers = to_tp[1:] + to_z[1:] + [to_y]
    barrier = pltpu.get_barrier_semaphore()
    for peer in peers:
        pl.semaphore_signal(barrier, inc=1, device_id=peer, device_id_type=MESH)

    remote = Copies(send, recv)
    lefts = [[rows_c], [rows_d], [rows_b, rows_b2], [normed_a, low_a]]
    rights = [cols_c, cols_d, cols_b, cols_a]
    slots = [[0], [1], [2, 3], [0, 1]]
    place = [0, 1, 2, 0]
    lanes = [
        (0, 0, cols, True),
        (1, 0, cols, True),
        (2, 0, cols, True),
        (3, 0, cols // 2, True),
        (3, cols // 2, cols // 2, False),
    ]
    parts = [(1 - x) * 2 + 1 - core, x * 2 + 1 - core, (1 - x) * 2 + core, x * 2 + core]
    far_rows = pl.ds(pl.multiple_of((1 - my_y) * half, 16), half)
    near_rows = pl.ds(pl.multiple_of(my_y * half, 16), half)
    firsts = [
        [remote.add(sent.at[place[j], p], got1.at[j, p], to_core) for p in (0, 1)]
        for j in range(4)
    ]
    seconds, thirds, fourths = [], [], []
    for j, lo, count, y_first in lanes:
        at = pl.ds(lo, count)
        spot = held.at[place[j]]
        if y_first:
            seconds.append(
                [
                    remote.add(
                        spot.at[p, far_rows, at], got2.at[j, pl.ds(p * half, half), at], to_y
                    )
                    for p in (0, 1)
                ]
            )
            thirds.append(remote.add(spot.at[0, near_rows, at], got3.at[j, :, at], to_x))
        else:
            seconds.append([remote.add(spot.at[0, :, at], got2.at[j, :, at], to_x)])
            thirds.append(remote.add(spot.at[1, far_rows, at], got3.at[j, :, at], to_y))
        fourths.append(
            [
                remote.add(
                    total.at[j, pl.ds(pl.multiple_of((my_z ^ r) * own, 16), own), at],
                    got4.at[j, r - 1, :, at],
                    to_z[r],
                )
                for r in range(1, n_z)
            ]
        )
    tails = [
        remote.add(tail_sum.at[min(step, 3)], tail_got.at[step], peer)
        for step, peer in enumerate([to_core, to_y, to_x] + to_z[1:])
    ]
    res_z = [
        [
            remote.add(
                results.at[m, r],
                res_half.at[m, :, pl.ds(pl.multiple_of(my_z * chunk, 16), chunk)],
                to_z[r],
            )
            for r in range(1, n_z)
        ]
        for m in range(micros)
    ]
    res_tp = [
        [
            remote.add(
                res_half.at[m, :, pl.ds(s * part, part)], acts.at[m, my_tp], to_tp[s]
            )
            for s in range(1, n_tp)
        ]
        for m in range(micros)
    ]

    loads = [
        pltpu.make_async_copy(src, dst, load_sem.at[i])
        for i, (src, dst) in enumerate(
            [(qkv_w, w_qkv), (out_w, w_out), (norm_in, norm), (logsum_in, logsum)]
        )
    ]
    own_res = [
        pltpu.make_async_copy(
            results.at[m, 0],
            res_half.at[m, :, pl.ds(pl.multiple_of(my_z * chunk, 16), chunk)],
            load_sem.at[4 + m],
        )
        for m in range(micros)
    ]
    home_res = [
        pltpu.make_async_copy(
            res_half.at[m, :, pl.ds(0, part)], acts.at[m, my_tp], load_sem.at[4 + micros + m]
        )
        for m in range(micros)
    ]

    def fetch(index, tiles):
        j, p = tiles[index]
        return pltpu.make_async_copy(
            rights[j].at[:, pl.ds(pl.multiple_of(parts[p] * cols, 128), cols)],
            tile_in.at[index % 2],
            tile_sem.at[index % 2],
        )

    def fetch_left(index, todo):
        j, i, piece = todo[index]
        return pltpu.make_async_copy(
            lefts[j][i].at[pl.ds(piece * depth, depth)], stage.at[index % 2], stage_sem.at[index % 2]
        )

    def turn(chunks):
        todo = [
            (j, i, piece)
            for j in chunks
            for i in range(len(lefts[j]))
            for piece in range(all_rows // depth)
        ]
        fetch_left(0, todo).start()
        for index, (j, i, piece) in enumerate(todo):
            fetch_left(index, todo).wait()
            if index + 1 < len(todo):
                fetch_left(index + 1, todo).start()
            turned[slots[j][i], :, piece * depth : (piece + 1) * depth] = stage[index % 2].T

    edge = 2 * cols // 3
    lane_index = lax.broadcasted_iota(jnp.int32, (STEP, cols - edge), 1) + edge

    def product(index, tiles):
        j, p = tiles[index]
        fetch(index, tiles).wait()
        if index + 1 < len(tiles):
            fetch(index + 1, tiles).start()
        right = tile_in.at[index % 2]
        if p >= 2:
            firsts[j][p - 2].wait_recv()

        def body(rows):
            value = dot(turned[slots[j][0], rows, :], right[...], NN)
            if len(slots[j]) == 2:
                other = dot(turned[slots[j][1], rows, :], right[:, edge:], NN)
                end = jnp.where(lane_index >= 3 * cols // 4, other, value[:, edge:])
                value = jnp.concatenate([value[:, :edge], end], axis=1)
            if p < 2:
                sent[place[j], p, rows, :] = value.astype(BF)
            else:
                value = value + got1[j, p - 2, rows, :].astype(F32)
                held[place[j], p - 2, rows, :] = value.astype(BF)

        blocks(depth, body)
        if p < 2:
            firsts[j][p].start()
        else:
            for lane, (k, _, _, y_first) in enumerate(lanes):
                if k == j and (y_first or p == 2):
                    seconds[lane][p - 2].start()

    def after_second(lane):
        j, lo, count, y_first = lanes[lane]
        at = pl.ds(lo, count)
        spot = held.at[place[j]]
        if y_first:
            for p in (0, 1):
                seconds[lane][p].wait_recv()

                def body(rows, p=p):
                    mine = pl.ds(pl.multiple_of(rows.start + my_y * half, STEP), STEP)
                    there = pl.ds(pl.multiple_of(rows.start + p * half, STEP), STEP)
                    value = spot[p, mine, at].astype(F32) + got2[j, there, at].astype(F32)
                    spot[p, mine, at] = value.astype(BF)

                blocks(half, body)
                if p == 0:
                    thirds[lane].start()
        else:
            seconds[lane][0].wait_recv()

            def body(rows):
                value = spot[1, rows, at].astype(F32) + got2[j, rows, at].astype(F32)
                spot[1, rows, at] = value.astype(BF)

            blocks(depth, body)
            thirds[lane].start()

    def after_third(lane):
        j, lo, count, _ = lanes[lane]
        at = pl.ds(lo, count)
        thirds[lane].wait_recv()

        def body(rows):
            mine = pl.ds(pl.multiple_of(rows.start + my_y * half, STEP), STEP)
            value = held[place[j], 1, mine, at].astype(F32) + got3[j, rows, at].astype(F32)
            total[j, rows, at] = value.astype(BF)

        blocks(half, body)
        start_all(fourths[lane])

    def after_fourth(lane):
        j, lo, count, _ = lanes[lane]
        at = pl.ds(lo, count)
        value = total[j, pl.ds(pl.multiple_of(my_z * own, 16), own), at].astype(F32)
        for r in range(1, n_z):
            fourths[lane][r - 1].wait_recv()
            value = value + got4[j, r - 1, :, at].astype(F32)
        out[j, :, at] = value

    tiles = [(j, p) for j in range(3) for p in (0, 1)] + [(j, p) for j in range(3) for p in (2, 3)]
    fetch(0, tiles).start()
    for copy in loads + own_res:
        copy.start()
    turn([0])
    pl.semaphore_wait(barrier, len(peers))
    start_all(res_z[0] + res_z[1])
    for index in range(len(tiles)):
        if index == 1:
            turn([1])
        if index == 3:
            turn([2])
        product(index, tiles)

    for copy in loads:
        copy.wait()
    frame_total = micros * frames

    def frame_loads(f, slot):
        buf = tile_in.at[slot]
        m, at = f // frames, lax.rem(f, frames)
        pairs = [
            (xs.at[f], buf.at[pl.ds(0, places)]),
            (mixed_in.at[f], buf.at[pl.ds(places, places)]),
        ]
        pairs += [
            (
                qkv_in.at[f, :, pl.ds(i * width, width)],
                buf.at[pl.ds((2 + i) * places, places)],
            )
            for i in range(3)
        ]
        pairs += [
            (
                grads.at[m, r, at],
                buf.at[pl.ds(pl.multiple_of(5 * places + (my_z ^ r) * chunk, 16), chunk)],
            )
            for r in range(n_z)
        ]
        return [
            pltpu.make_async_copy(src, dst, frame_sem.at[slot, i])
            for i, (src, dst) in enumerate(pairs)
        ]

    def frame_stores(f, slot):
        rows = pl.ds(pl.multiple_of(f * places, 16), places)
        buf = turned.at[slot]
        pairs = [
            (
                buf.at[pl.ds(t * places, places), pl.ds(0, width)],
                cols_a.at[rows, pl.ds(t * cols, cols)],
            )
            for t in range(n_tp)
        ]
        pairs += [
            (buf.at[pl.ds(0, places), pl.ds(width, width)], normed_a.at[rows]),
            (buf.at[pl.ds(places, places), pl.ds(width, width)], low_a.at[rows]),
        ]
        return [
            pltpu.make_async_copy(src, dst, out_sem.at[slot, i])
            for i, (src, dst) in enumerate(pairs)
        ]

    grad = sent.at[1]
    for p in (0, 1):
        firsts[1][p].wait_send()
    tail_sum[...] = jnp.zeros_like(tail_sum)
    tail_sum[0, 2:6] = tail_time[...]
    start_all(frame_loads(0, 0))

    def frame(f, carry):
        slot = lax.rem(f, 2)

        @pl.when(f + 1 < frame_total)
        def _():
            start_all(frame_loads(f + 1, 1 - slot))

        @pl.when(f == 3)
        def _():
            after_second(0)

        @pl.when(f == 6)
        def _():
            after_second(1)

        @pl.when(f == 7)
        def _():
            after_third(0)

        @pl.when(f == 4)
        def _():
            for m in range(1):
                own_res[m].wait()
                arrive(res_z[m])
                start_all(res_tp[m])
                home_res[m].start()

        for copy in frame_loads(f, slot):
            copy.wait()

        @pl.when(f >= 2)
        def _():
            for copy in frame_stores(f - 2, slot):
                copy.wait()

        buf, keep = tile_in.at[slot], turned.at[slot]
        block = lambda i: slice(i * places, (i + 1) * places)
        unit, rate = normalise(buf[block(0)].astype(F32))
        keep[0:places, width : 2 * width] = (unit * norm[0:1] + norm[1:2]).astype(BF)
        low = buf[block(5)]
        keep[places : 2 * places, width : 2 * width] = low
        grad_mixed = dot(low, w_out[...], NN).astype(BF)
        for g in range(width // WIDE):
            at = slice(g * WIDE, (g + 1) * WIDE)
            back = attend_back(
                buf[block(2), at], buf[block(3), at], buf[block(4), at],
                grad_mixed[:, at], logsum[f, g : g + 1], None,
            )
            for i, value in enumerate(back):
                dqkv[:, i * width + g * WIDE : i * width + (g + 1) * WIDE] = value
        span = cols // 4
        for t in range(n_tp):
            for i in range(3):
                keep[block(t), i * span : (i + 1) * span] = dqkv[
                    :, i * width + t * span : i * width + (t + 1) * span
                ]
            keep[block(t), 3 * span : 4 * span] = buf[block(1), t * span : (t + 1) * span]
        start_all(frame_stores(f, slot))
        grad_normed = dot(dqkv[...], w_qkv[...], NT)
        tail_sum[0, 0:1] += jnp.sum(grad_normed * unit, axis=0, keepdims=True)
        tail_sum[0, 1:2] += jnp.sum(grad_normed, axis=0, keepdims=True)
        value = low.astype(F32) + norm_back(grad_normed, norm[0:1], unit, rate)
        m, at = f // frames, lax.rem(f, frames)
        grad[m, pl.ds(pl.multiple_of(at * places, 16), places), :] = value.astype(BF)
        for s in range(n_tp):
            src = grad.at[m, pl.ds(pl.multiple_of(at * places + s * part, 16), part)]
            dst = input_grad.at[m, my_tp, at]
            if s == 0:
                pltpu.make_async_copy(src, dst, i_send.at[0]).start()
            else:
                pltpu.make_async_remote_copy(
                    src_ref=src, dst_ref=dst, send_sem=i_send.at[s], recv_sem=i_recv.at[s],
                    device_id=to_tp[s], device_id_type=MESH,
                ).start()
        return carry

    lax.fori_loop(0, frame_total, frame, 0)
    for f in (frame_total - 2, frame_total - 1):
        for copy in frame_stores(f, f % 2):
            copy.wait()
    tails[0].start()

    for p in (0, 1):
        firsts[0][p].wait_send()
    last = [(3, p) for p in range(4)]
    fetch(0, last).start()
    turn([3])
    product(0, last)
    product(1, last)
    after_second(2)
    after_third(1)
    tails[0].wait_recv()
    tail_sum[1] = tail_sum[0] + tail_got[0]
    tails[1].start()
    for p in (0, 1):
        seconds[0][p].wait_send()
    thirds[0].wait_send()
    product(2, last)
    product(3, last)
    after_fourth(0)
    own_res[1].wait()
    arrive(res_z[1])
    start_all(res_tp[1])
    home_res[1].start()
    tails[1].wait_recv()
    tail_sum[2] = tail_sum[1] + tail_got[1]
    tails[2].start()
    after_third(2)
    after_second(3)
    after_second(4)
    after_fourth(1)
    tails[2].wait_recv()
    tail_sum[3] = tail_sum[2] + tail_got[2]
    start_all(tails[3:])
    after_third(3)
    after_third(4)
    after_fourth(2)
    value = tail_sum[3]
    for r in range(n_z - 1):
        tails[3 + r].wait_recv()
        value = value + tail_got[3 + r]
    tail_out[...] = value
    after_fourth(3)
    after_fourth(4)
    for m in range(micros):
        arrive(res_tp[m])
        home_res[m].wait()
    for s in range(n_tp):
        dst = input_grad.at[:, my_tp ^ s]
        if s == 0:
            pltpu.make_async_copy(dst, dst, i_send.at[0]).wait()
        else:
            for ref, wait in ((dst, "wait_send"), (dst, "wait_recv")):
                copy = pltpu.make_async_remote_copy(
                    src_ref=ref, dst_ref=ref, send_sem=i_send.at[s], recv_sem=i_recv.at[s],
                    device_id=to_tp[s], device_id_type=MESH,
                )
                getattr(copy, wait)()
    done = firsts[0] + firsts[1] + seconds[0] + [thirds[0]]
    for copy in remote.all:
        if not any(copy is other for other in done):
            copy.wait_send()


def back(results, grads, xs, qkv, mixed, logsum, qkv_w, out_w, norm, tail_time, kept):
    normed_time, columns, grad_time, normed_mlp, grad_pre, hidden, grad_result = kept
    micros, n_z, frames, chunk, width = results.shape
    n_tp = lax.axis_size("tp")
    places = chunk * n_z
    total = micros * frames
    rows = total * places
    depth, cols = width, columns.shape[1] // n_tp
    half, own = depth // 2, depth // (2 * n_z)
    part = places // n_tp
    any_spec = pl.BlockSpec(memory_space=pl.ANY)
    vmem = pl.BlockSpec(memory_space=pltpu.VMEM)
    dma = pltpu.SemaphoreType.DMA
    shape = jax.ShapeDtypeStruct
    home = shape((micros, n_tp, frames, part, width), BF)
    return pl.pallas_call(
        back_kernel,
        in_specs=[any_spec] * 9 + [vmem] + [any_spec] * 7,
        out_specs=[vmem] * 2 + [any_spec] * 6,
        out_shape=[
            shape((4, own, cols), F32),
            shape((8, width), F32),
            home,
            home,
            shape((rows, width), BF),
            shape((rows, width), BF),
            shape((rows, n_tp * cols), BF),
            shape((micros, frames, places, width), BF),
        ],
        scratch_shapes=[
            pltpu.VMEM((4, depth, rows), BF),
            pltpu.VMEM((2, depth, width), BF),
            pltpu.VMEM((2, rows, cols), BF),
            pltpu.VMEM((3, 2, depth, cols), BF),
            pltpu.VMEM((4, 2, depth, cols), BF),
            pltpu.VMEM((3, 2, depth, cols), BF),
            pltpu.VMEM((4, depth, cols), BF),
            pltpu.VMEM((4, half, cols), BF),
            pltpu.VMEM((4, half, cols), BF),
            pltpu.VMEM((4, n_z - 1, own, cols), BF),
            pltpu.VMEM((width, 3 * width), BF),
            pltpu.VMEM((width, width), BF),
            pltpu.VMEM((8, width), F32),
            pltpu.VMEM(logsum.shape, F32),
            pltpu.VMEM((places, 3 * width), BF),
            pltpu.VMEM((4, 8, width), F32),
            pltpu.VMEM((2 + n_z, 8, width), F32),
            dma((2,)),
            dma((2,)),
            dma((2, 5 + n_z)),
            dma((2, n_tp + 2)),
            dma((4 + 2 * micros,)),
            dma((N_REMOTE,)),
            dma((N_REMOTE,)),
            dma((1,)),
            dma((1,)),
            dma((n_tp,)),
            dma((n_tp,)),
        ],
        compiler_params=pltpu.CompilerParams(
            vmem_limit_bytes=60 * MIB, collective_id=5, has_side_effects=True
        ),
        cost_estimate=pl.CostEstimate(
            flops=2 * rows * width * 23 * width,
            bytes_accessed=rows * width * 60,
            transcendentals=0,
        ),
    )(
        results, grads, xs, qkv, mixed, logsum, qkv_w, out_w, norm, tail_time,
        normed_mlp, grad_pre, grad_result, hidden, normed_time, grad_time, columns,
    )


N_REMOTE = 96
N_LOCAL = 24


def front_kernel(
    inputs, cot, shard, ln_shard,
    xs_out, time_in, cots, qkv_out, mixed_out, logsum_out,
    qkv_a, out_a, qkv_b, out_b, in_w, unit_w, norms,
    xs, sent, raw, std_qkv, std_out, ln, cot_half, qkv, mixed,
    send, recv, t_send, t_recv, local,
):
    my_tp, my_y, my_z = lax.axis_index("tp"), lax.axis_index("clip"), lax.axis_index("fp")
    n_tp, n_z = lax.axis_size("tp"), lax.axis_size("fp")
    micros, _, frames, part, width = inputs.shape
    places = part * n_tp
    chunk = places // n_z
    own = shard.shape[1]
    half = n_z * own
    cols = shard.shape[2]
    to_tp = [{"tp": my_tp ^ s} for s in range(n_tp)]
    to_core, to_x = to_tp[1], to_tp[2]
    to_y = {"clip": my_y ^ 1}
    to_z = [{"fp": my_z ^ r} for r in range(n_z)]
    peers = to_tp[1:] + to_z[1:] + [to_y]
    barrier = pltpu.get_barrier_semaphore()
    for peer in peers:
        pl.semaphore_signal(barrier, inc=1, device_id=peer, device_id_type=MESH)

    remote = Copies(send, recv)
    locals_ = []

    def here(src, dst):
        copy = pltpu.make_async_copy(src, dst, local.at[len(locals_)])
        locals_.append(copy)
        copy.start()
        return copy

    tiles = [raw.at[0], raw.at[1], in_w, unit_w]
    mine = pl.multiple_of(my_y * half + my_z * own, 16)
    near = pl.multiple_of(my_y * half, 16)
    far = pl.multiple_of((1 - my_y) * half, 16)
    away = my_tp ^ 2
    cuts = [cols // 2, 2 * cols // 3, 2 * cols // 3, 2 * cols // 3]
    own_shards = []
    by_z, by_x, by_y, by_y2, by_x2, by_core = [], [], [], [], [], []
    for j, tile in enumerate(tiles):
        cut = cuts[j]
        one, two = pl.ds(0, cut), pl.ds(cut, cols - cut)
        own_rows, near_rows, far_rows = pl.ds(mine, own), pl.ds(near, half), pl.ds(far, half)

        def same(peer, *index, tile=tile):
            return remote.add(tile.at[index], tile.at[index], peer)

        by_z.append(
            [
                remote.add(shard.at[j], tile.at[my_tp, own_rows], to_z[r])
                for r in range(1, n_z)
            ]
        )
        by_x.append(same(to_x, my_tp, near_rows, one))
        by_y.append([same(to_y, my_tp, near_rows, one), same(to_y, away, near_rows, one)])
        by_y2.append(same(to_y, my_tp, near_rows, two))
        by_x2.append(same(to_x, my_tp, slice(None), two))
        by_core.append(
            [
                same(to_core, my_tp, near_rows),
                same(to_core, away, near_rows, one),
                same(to_core, my_tp, far_rows, one),
                same(to_core, away, far_rows, one),
                same(to_core, my_tp, far_rows, two),
                same(to_core, away, slice(None), two),
            ]
        )
    ln_z = [
        remote.add(ln_shard, ln.at[pl.ds(mine, own)], to_z[r]) for r in range(1, n_z)
    ]
    ln_y = remote.add(ln.at[pl.ds(near, half)], ln.at[pl.ds(near, half)], to_y)
    x_in = [
        [
            remote.add(
                inputs.at[m, my_tp ^ s],
                xs.at[pl.ds(m * frames, frames), pl.ds(s * part, part)],
                to_tp[s],
            )
            for s in range(1, n_tp)
        ]
        for m in range(micros)
    ]
    cot_in = [
        [
            remote.add(
                cot.at[m, my_tp ^ s], cot_half.at[m, :, pl.ds(s * part, part)], to_tp[s]
            )
            for s in range(1, n_tp)
        ]
        for m in range(micros)
    ]
    cot_z = [
        [
            remote.add(
                cot_half.at[m, :, pl.ds(pl.multiple_of((my_z ^ r) * chunk, 16), chunk)],
                cots.at[m, r],
                to_z[r],
            )
            for r in range(1, n_z)
        ]
        for m in range(micros)
    ]

    own_x = [
        here(inputs.at[m, my_tp], xs.at[pl.ds(m * frames, frames), pl.ds(0, part)])
        for m in range(micros)
    ]
    own_cot = [here(cot.at[m, my_tp], cot_half.at[m, :, pl.ds(0, part)]) for m in range(micros)]
    own_w = [here(shard.at[j], tile.at[my_tp, pl.ds(mine, own)]) for j, tile in enumerate(tiles)]
    own_ln = here(ln_shard, ln.at[pl.ds(mine, own)])

    pl.semaphore_wait(barrier, len(peers))
    start_all(by_z[0] + ln_z + x_in[0])
    start_all(by_z[1] + x_in[1] + by_z[2] + by_z[3] + cot_in[0])

    def gather_start(j):
        own_w[j].wait()
        arrive(by_z[j])
        by_x[j].start()
        by_y2[j].start()
        by_core[j][0].start()

    def gather_first(j):
        by_x[j].wait_recv()
        start_all(by_y[j])
        by_core[j][1].start()

    def gather_second(j):
        by_y2[j].wait_recv()
        by_x2[j].start()
        by_core[j][4].start()

    def gather_last(j):
        arrive(by_y[j])
        start_all(by_core[j][2:4])
        by_x2[j].wait_recv()
        by_core[j][5].start()

    def standard(j):
        span = cols // 4
        for t in range(n_tp):
            for i in range(3):
                std_qkv[j, :, i * width + t * span : i * width + (t + 1) * span] = raw[
                    j, t, :, i * span : (i + 1) * span
                ]
            std_out[j, :, t * span : (t + 1) * span] = raw[j, t, :, 3 * span : 4 * span]

    gather_start(0)
    own_ln.wait()
    arrive(ln_z)
    ln_y.start()
    gather_first(0)
    gather_second(0)
    gather_start(1)
    gather_last(0)
    ln_y.wait_recv()
    norms[...] = ln[...].astype(F32).T[: norms.shape[0]]
    gather_start(2)
    arrive(by_core[0])
    standard(0)
    start_all(cot_in[1])
    own_x[0].wait()
    arrive(x_in[0])
    weights_out = [here(std_qkv.at[0], qkv_a), here(std_out.at[0], out_a)]

    def frame(f, carry):
        @pl.when(f == 1)
        def _():
            gather_first(1)
            gather_start(3)

        @pl.when(f == 2)
        def _():
            gather_second(1)
            own_cot[0].wait()
            arrive(cot_in[0])
            start_all(cot_z[0])

        @pl.when(f == 3)
        def _():
            gather_first(2)

        @pl.when(f == frames)
        def _():
            own_x[1].wait()
            arrive(x_in[1])
            gather_second(2)

        @pl.when(f == frames + 2)
        def _():
            gather_first(3)

        x = xs[f].astype(F32)
        unit, _ = normalise(x)
        normed = (unit * norms[0:1] + norms[1:2]).astype(BF)
        qkv[f] = dot(normed, std_qkv[0], NN).astype(BF)
        for g in range(width // WIDE):
            at = g * WIDE
            out, logsum = attend(
                qkv[f, :, at : at + WIDE],
                qkv[f, :, width + at : width + at + WIDE],
                qkv[f, :, 2 * width + at : 2 * width + at + WIDE],
                None,
            )
            mixed[f, :, at : at + WIDE] = out
            logsum_out[f, g : g + 1] = logsum
        sent[f] = (x + dot(mixed[f], std_out[0], NT)).astype(BF)
        m, at_frame = f // frames, lax.rem(f, frames)
        for r in range(n_z):
            src = sent.at[f, pl.ds(pl.multiple_of((my_z ^ r) * chunk, 16), chunk)]
            dst = time_in.at[m, r, at_frame]
            if r == 0:
                pltpu.make_async_copy(src, dst, t_send.at[m, 0]).start()
            else:
                pltpu.make_async_remote_copy(
                    src_ref=src, dst_ref=dst, send_sem=t_send.at[m, r],
                    recv_sem=t_recv.at[m, r], device_id=to_z[r], device_id_type=MESH,
                ).start()
        return carry

    lax.fori_loop(0, micros * frames, frame, 0)
    kept = [here(xs, xs_out), here(qkv, qkv_out), here(mixed, mixed_out)]
    gather_last(1)
    own_cot[1].wait()
    arrive(cot_in[1])
    start_all(cot_z[1])
    gather_second(3)
    arrive(by_core[1])
    standard(1)
    weights_out += [here(std_qkv.at[1], qkv_b), here(std_out.at[1], out_b)]
    own_cots = [
        here(cot_half.at[m, :, pl.ds(pl.multiple_of(my_z * chunk, 16), chunk)], cots.at[m, 0])
        for m in range(micros)
    ]
    gather_last(2)
    gather_last(3)
    arrive(by_core[2])
    arrive(by_core[3])
    for m in range(micros):
        arrive(cot_z[m])
        for r in range(n_z):
            src = sent.at[
                pl.ds(m * frames, frames), pl.ds(pl.multiple_of((my_z ^ r) * chunk, 16), chunk)
            ]
            dst = time_in.at[m, r]
            if r == 0:
                pltpu.make_async_copy(src, dst, t_send.at[m, 0]).wait()
            else:
                pltpu.make_async_remote_copy(
                    src_ref=src, dst_ref=dst, send_sem=t_send.at[m, r],
                    recv_sem=t_recv.at[m, r], device_id=to_z[r], device_id_type=MESH,
                ).wait()
    for copy in remote.all:
        copy.wait_send()
    for copy in kept + weights_out + own_cots:
        copy.wait()


def front(inputs, cot, shard, ln_shard):
    micros, clips, frames, part, width = inputs.shape
    n_tp, n_z = lax.axis_size("tp"), lax.axis_size("fp")
    places = part * n_tp
    total = micros * frames
    chunk = places // n_z
    cols = shard.shape[2]
    groups = width // WIDE
    any_spec = pl.BlockSpec(memory_space=pl.ANY)
    vmem = pl.BlockSpec(memory_space=pltpu.VMEM)
    dma = pltpu.SemaphoreType.DMA
    shape = jax.ShapeDtypeStruct
    weights = [(width, 3 * width), (width, width)] * 2 + [(n_tp, width, cols)] * 2
    return pl.pallas_call(
        front_kernel,
        in_specs=[any_spec] * 4,
        out_specs=[any_spec] * 5 + [vmem] + [any_spec] * 6 + [vmem],
        out_shape=[
            shape((total, places, width), BF),
            shape((micros, n_z, frames, chunk, width), BF),
            shape((micros, n_z, frames, chunk, width), BF),
            shape((total, places, 3 * width), BF),
            shape((total, places, width), BF),
            shape((total, groups, GROUP * places), F32),
        ]
        + [shape(dims, BF) for dims in weights]
        + [shape((8, width), F32)],
        scratch_shapes=[
            pltpu.VMEM((total, places, width), BF),
            pltpu.VMEM((total, places, width), BF),
            pltpu.VMEM((2, n_tp, width, cols), BF),
            pltpu.VMEM((2, width, 3 * width), BF),
            pltpu.VMEM((2, width, width), BF),
            pltpu.VMEM((width, ln_shard.shape[1]), BF),
            pltpu.VMEM((micros, frames, places, width), BF),
            pltpu.VMEM((total, places, 3 * width), BF),
            pltpu.VMEM((total, places, width), BF),
            dma((N_REMOTE,)),
            dma((N_REMOTE,)),
            dma((micros, n_z)),
            dma((micros, n_z)),
            dma((N_LOCAL,)),
        ],
        compiler_params=pltpu.CompilerParams(
            vmem_limit_bytes=60 * MIB, collective_id=3, has_side_effects=True
        ),
        cost_estimate=pl.CostEstimate(
            flops=2 * total * places * width * 5 * width,
            bytes_accessed=total * places * width * 16,
            transcendentals=0,
        ),
    )(inputs, cot, shard, ln_shard)


def to_peer(value, axis, step):
    n = lax.axis_size(axis)
    return lax.ppermute(value, axis, [(i, i ^ step) for i in range(n)])


def swap(pieces, axis):
    return [piece if s == 0 else to_peer(piece, axis, s) for s, piece in enumerate(pieces)]


def pick(stack, index):
    return lax.dynamic_index_in_dim(stack, index, 0, keepdims=False)


def shards(
    inputs, cotangent, qkv_weight, out_spatial, out_temporal, mlp_in, mlp_out, ln_gain, ln_bias
):
    micros, clips, frames, local, width = inputs.shape
    n_tp, n_fp = lax.axis_size("tp"), lax.axis_size("fp")
    n_cf = lax.axis_size("clip") * n_fp
    assert clips == n_tp
    my_tp, my_fp = lax.axis_index("tp"), lax.axis_index("fp")
    depth = qkv_weight.shape[2]
    span = qkv_weight.shape[3]
    places = n_tp * local
    chunk = places // n_fp
    at = my_fp.astype(jnp.int32)[None]

    first = jnp.concatenate([qkv_weight[0, i] for i in range(3)] + [out_spatial.T], axis=1)
    second = jnp.concatenate([qkv_weight[1, i] for i in range(3)] + [out_temporal.T], axis=1)
    axes = ("clip", "fp", "tp")
    ln_rows = [v[i] for i in range(3) for v in (ln_gain, ln_bias)]
    whole_rows = depth % 16 == 0 and n_tp == 4 and lax.axis_size("clip") == 2 and micros == 2
    whole_rows = whole_rows and frames * places == width and span * 4 == width

    def from_chunks(chunks):
        stack = jnp.stack(chunks)
        joined = jnp.concatenate([pick(stack, my_fp ^ c) for c in range(n_fp)], axis=1)
        return [joined[:, s * local : (s + 1) * local] for s in range(n_tp)]

    def outward(pieces):
        stack = jnp.stack(swap(pieces, "tp"))
        return jnp.stack([pick(stack, my_tp ^ c) for c in range(n_tp)])

    mine = lax.axis_index("clip") * n_fp + my_fp
    kinds = lambda v: [v[:, i * span : (i + 1) * span] for i in range(4)]

    def arranged(acts, grad_input, late, space, norm_grads):
        norm_grads = norm_grads[:6].reshape(3, 2, n_cf, depth)
        norm_grads = lax.dynamic_index_in_dim(norm_grads, mine, 2, keepdims=False)
        space_g, time_g = kinds(space), kinds(late[2])
        return (
            acts,
            grad_input,
            jnp.stack([jnp.stack(space_g[:3]), jnp.stack(time_g[:3])]),
            space_g[3].T,
            time_g[3].T,
            late[0],
            late[1].T,
            norm_grads[:, 0],
            norm_grads[:, 1],
        )

    if whole_rows:
        ln_shard = jnp.stack(ln_rows + [jnp.zeros_like(ln_rows[0])] * 122, axis=1)
        shard = jnp.stack([first, second, mlp_in, mlp_out.T])
        (
            xs, time_pieces, cots, qkv, mixed, logsum,
            qkv_space_w, out_space_w, qkv_time_w, out_time_w, in_w, unit_w, norms,
        ) = front(inputs, cotangent, shard, ln_shard)
        results, grads, *kept, tail = time_layer(
            [time_pieces], [cots], qkv_time_w, out_time_w, in_w, unit_w, norms
        )
        sums, norm_grads, acts, input_grad, *_ = back(
            results, grads, xs, qkv, mixed, logsum, qkv_space_w, out_space_w, norms, tail, kept
        )
        return arranged(acts, input_grad.astype(F32), sums, sums[3], norm_grads)

    def gathered(part):
        return lax.all_gather(part, axes).reshape(n_cf, n_tp, depth, part.shape[1])

    def attention_weights(raw):
        raw = raw.reshape(n_cf, n_tp, depth, 4, span).transpose(3, 0, 2, 1, 4)
        raw = raw.reshape(4, n_cf * depth, n_tp * span)
        return jnp.concatenate([raw[0], raw[1], raw[2]], axis=1), raw[3]

    def unit_weights(raw):
        return raw.transpose(1, 0, 2, 3).reshape(n_tp, n_cf * depth, raw.shape[3])

    norms = lax.all_gather(jnp.stack(ln_rows), ("clip", "fp"))
    norms = norms.transpose(1, 0, 2).reshape(6, n_cf * depth).astype(F32)
    qkv_space_w, out_space_w = attention_weights(gathered(first))
    rest = gathered(jnp.concatenate([second, mlp_in, mlp_out.T], axis=1))
    qkv_time_w, out_time_w = attention_weights(rest[..., : 4 * span])
    in_w = unit_weights(rest[..., 4 * span : 4 * span + mlp_in.shape[1]])
    unit_w = unit_weights(rest[..., 4 * span + mlp_in.shape[1] :])

    def inward(array, m):
        return swap([pick(array[m], my_tp ^ s) for s in range(n_tp)], "tp")

    def to_chunks(pieces):
        joined = jnp.concatenate(pieces, axis=1)
        return [
            lax.dynamic_slice_in_dim(joined, (my_fp ^ r) * chunk, chunk, 1)
            for r in range(n_fp)
        ]

    space_kept, time_given = [], []
    for m in range(micros):
        x = inward(inputs, m)
        cots = swap(to_chunks(inward(cotangent, m)), "fp")
        out = space_forward(x, qkv_space_w, out_space_w, norms, at, n_fp)
        time_given.append((swap(out[:n_fp], "fp"), cots))
        space_kept.append((x,) + tuple(out[n_fp:]) + (0,))
    time_kept = []
    results = []
    space_grads = []
    for m in range(micros):
        pieces, cots = time_given[m]
        out = time_layer(pieces, cots, qkv_time_w, out_time_w, in_w, unit_w, norms)
        results.append(outward(from_chunks(swap(out[:n_fp], "fp"))))
        space_grads.append(swap(out[n_fp : 2 * n_fp], "fp"))
        time_kept.append(out[2 * n_fp :])
    space_rows = []
    input_grads = []
    flat = lambda v: v.reshape(-1, v.shape[-1])
    kept = lambda i: [k[i] for k in time_kept]
    time_chunks = [
        ([kept(3)], kept(4), True),
        ([kept(6)], kept(5), False),
        ([kept(0), kept(2)], kept(1), True),
    ]
    for m in range(micros):
        x, qkv, mixed, logsum, skip = space_kept[m]
        out = space_backward(
            x, space_grads[m], qkv, mixed, logsum, qkv_space_w, out_space_w, norms, at, skip, n_tp
        )
        input_grads.append(outward(out[:n_tp]).astype(F32))
        normed, low, columns, norm_grad = out[n_tp:]
        space_rows.append((flat(normed), flat(low), flat(columns), norm_grad))
    rows = lambda i: [k[i] for k in space_rows]
    space_chunk = ([rows(0), rows(1)], rows(2), True)
    early = scatter_grads([space_chunk], n_cf, n_tp)
    late = scatter_grads(time_chunks, n_cf, n_tp)
    norm_grads = lax.psum(jnp.concatenate([sum(rows(3)), sum(kept(7))]), axes)
    return arranged(jnp.stack(results), jnp.stack(input_grads), late, early[0], norm_grads)


def scatter_grads(chunks, n_cf, n_tp):
    tiles = []
    for lefts, rights, _ in chunks:
        cols = rights[0].shape[1] // n_tp
        total = sum(dot(a, b, TN) for a, b in zip(lefts[0], rights))
        total = total.reshape(total.shape[0], n_tp, cols)
        if len(lefts) == 2:
            other = sum(dot(a, b, TN) for a, b in zip(lefts[1], rights))
            other = other.reshape(other.shape[0], n_tp, cols)
            at = 3 * cols // 4
            total = jnp.concatenate([total[..., :at], other[..., at:]], axis=2)
        total = total.reshape(n_cf, total.shape[0] // n_cf, n_tp, cols).transpose(0, 2, 1, 3)
        tiles.append(total.reshape((n_cf * n_tp,) + total.shape[2:]))
    return lax.psum_scatter(jnp.stack(tiles, 1), ("clip", "fp", "tp"), scatter_dimension=0)


def solution(mesh):
    spread = P(None, "clip", "fp", "tp", None)
    return jax.shard_map(
        shards,
        mesh=mesh,
        in_specs=(
            spread,
            spread,
            P(None, None, ("clip", "fp"), "tp"),
            P("tp", ("clip", "fp")),
            P("tp", ("clip", "fp")),
            P(("clip", "fp"), "tp"),
            P("tp", ("clip", "fp")),
            P(None, ("clip", "fp")),
            P(None, ("clip", "fp")),
        ),
        out_specs=(
            spread,
            spread,
            P(None, None, ("clip", "fp"), "tp"),
            P("tp", ("clip", "fp")),
            P("tp", ("clip", "fp")),
            P(("clip", "fp"), "tp"),
            P("tp", ("clip", "fp")),
            P(None, ("clip", "fp")),
            P(None, ("clip", "fp")),
        ),
        check_vma=False,
    )
```

```python
from functools import partial

import jax
import jax.numpy as jnp
from jax import lax
from jax.experimental import pallas as pl
from jax.experimental.pallas import tpu as pltpu
from jax.sharding import PartitionSpec as P

HD = 64
GROUP = 4
WIDE = GROUP * HD
EPS = 1e-06
BF = jnp.bfloat16
F32 = jnp.float32
MIB = 1024 * 1024
MESH = pl.DeviceIdType.MESH

NN = (((1,), (0,)), ((), ()))
NT = (((1,), (1,)), ((), ()))
TN = (((0,), (0,)), ((), ()))


def dot(a, b, dims):
    return lax.dot_general(a, b, dims, preferred_element_type=F32)


def normalise(values):
    centre = values - jnp.mean(values, axis=-1, keepdims=True)
    spread = jnp.mean(centre * centre, axis=-1, keepdims=True)
    rate = lax.rsqrt(spread + EPS)
    return centre * rate, rate


def norm_back(upstream, gain, unit, rate):
    weighted = upstream * gain
    inner = jnp.mean(weighted * unit, axis=-1, keepdims=True)
    return rate * (weighted - jnp.mean(weighted, axis=-1, keepdims=True) - unit * inner)


def head_masks(scale):
    lanes = lax.broadcasted_iota(jnp.int32, (1, WIDE), 1) // HD
    return [jnp.where(lanes == h, scale, 0.0).astype(BF) for h in range(GROUP)]


def spread_heads(block, masks):
    return jnp.concatenate([block * mask for mask in masks], axis=0)


def gather_heads(stacked, rows):
    lanes = lax.broadcasted_iota(jnp.int32, (1, WIDE), 1) // HD
    total = stacked[:rows]
    for h in range(1, GROUP):
        total = jnp.where(lanes == h, stacked[h * rows : (h + 1) * rows], total)
    return total


def attend(queries, keys, values, bias):
    rows = queries.shape[0]
    scores = dot(keys, spread_heads(queries, head_masks(HD**-0.5)), NT)
    if bias is not None:
        scores = scores + bias
    top = jnp.max(scores, axis=0, keepdims=True)
    exponent = jnp.exp(scores - top)
    totals = jnp.sum(exponent, axis=0, keepdims=True)
    weights = (exponent * (1.0 / totals)).astype(BF)
    mixed = gather_heads(dot(weights, values, TN), rows).astype(BF)
    return mixed, top + jnp.log(totals)


def attend_back(queries, keys, values, upstream, logsum, bias):
    rows = queries.shape[0]
    spread_q = spread_heads(queries, head_masks(HD**-0.5))
    spread_g = spread_heads(upstream, head_masks(1.0))
    scores = dot(keys, spread_q, NT)
    if bias is not None:
        scores = scores + bias
    probs = jnp.exp(scores - logsum)
    grad_probs = dot(values, spread_g, NT)
    inner = jnp.sum(probs * grad_probs, axis=0, keepdims=True)
    grad_scores = (probs * (grad_probs - inner)).astype(BF)
    grad_values = dot(probs.astype(BF), spread_g, NN)
    grad_keys = dot(grad_scores, spread_q, NN)
    grad_queries = gather_heads(dot(grad_scores, keys, TN), rows) * HD**-0.5
    return grad_queries.astype(BF), grad_keys.astype(BF), grad_values.astype(BF)


def gelu_parts(pre):
    size = jnp.abs(pre) * (0.5**0.5)
    t = 1.0 / (1.0 + 0.3275911 * size)
    bell = jnp.exp(-size * size)
    poly = t * (
        0.254829592
        + t * (-0.284496736 + t * (1.421413741 + t * (-1.453152027 + t * 1.061405429)))
    )
    tail = 0.5 * poly * bell
    return jnp.where(pre >= 0, 1.0 - tail, tail), bell * 0.3989422804014327


def space_forward_kernel(n_in, n_out, at_ref, *refs):
    pieces = refs[:n_in]
    qkv_w, out_w, norm = refs[n_in : n_in + 3]
    outs = refs[n_in + 3 : n_in + 3 + n_out]
    qkv_out, mixed_out, logsum_out, held = refs[n_in + 3 + n_out :]
    width = out_w.shape[1]
    x = jnp.concatenate([piece[0] for piece in pieces], axis=0).astype(F32)
    unit, _ = normalise(x)
    normed = (unit * norm[0:1] + norm[1:2]).astype(BF)
    qkv_out[0] = dot(normed, qkv_w[...], NN).astype(BF)
    for g in range(width // WIDE):
        at = g * WIDE
        mixed, logsum = attend(
            qkv_out[0, :, at : at + WIDE],
            qkv_out[0, :, width + at : width + at + WIDE],
            qkv_out[0, :, 2 * width + at : 2 * width + at + WIDE],
            None,
        )
        mixed_out[0, :, at : at + WIDE] = mixed
        logsum_out[0, g : g + 1] = logsum
    held[...] = x + dot(mixed_out[0], out_w[...], NT)
    rows = outs[0].shape[1]
    for r, out in enumerate(outs):
        start = pl.multiple_of((at_ref[0] ^ r) * rows, 8)
        out[0] = held[pl.ds(start, rows), :].astype(BF)


def space_forward(pieces, qkv_w, out_w, norm, at, n_out):
    frames, rows, width = pieces[0].shape
    places = rows * len(pieces)
    groups = width // WIDE
    whole = pl.BlockSpec(memory_space=pltpu.VMEM)
    frame = lambda *dims: pl.BlockSpec((1,) + dims, lambda f, at: (f,) + (0,) * len(dims))
    return pl.pallas_call(
        partial(space_forward_kernel, len(pieces), n_out),
        grid_spec=pltpu.PrefetchScalarGridSpec(
            num_scalar_prefetch=1,
            grid=(frames,),
            in_specs=[frame(rows, width)] * len(pieces) + [whole] * 3,
            out_specs=[frame(places // n_out, width)] * n_out
            + [frame(places, 3 * width), frame(places, width), frame(groups, GROUP * places)],
            scratch_shapes=[pltpu.VMEM((places, width), F32)],
        ),
        out_shape=[jax.ShapeDtypeStruct((frames, places // n_out, width), BF)] * n_out
        + [
            jax.ShapeDtypeStruct((frames, places, 3 * width), BF),
            jax.ShapeDtypeStruct((frames, places, width), BF),
            jax.ShapeDtypeStruct((frames, groups, GROUP * places), F32),
        ],
        compiler_params=pltpu.CompilerParams(vmem_limit_bytes=48 * MIB),
        cost_estimate=pl.CostEstimate(
            flops=2 * frames * places * width * 5 * width,
            bytes_accessed=frames * places * width * 16,
            transcendentals=0,
        ),
    )(at, *pieces, qkv_w, out_w, norm)


def store_columns(out, kinds, n_parts):
    width = kinds[0].shape[1]
    span = width // n_parts
    for t in range(n_parts):
        for i, kind in enumerate(kinds):
            start = (t * len(kinds) + i) * span
            out[:, start : start + span] = kind[:, t * span : (t + 1) * span]


def space_backward_kernel(n_in, n_grad, n_out, at_ref, *refs):
    pieces = refs[:n_in]
    grads = refs[n_in : n_in + n_grad]
    qkv_in, mixed_in, logsum_in, qkv_w, out_w, norm = refs[n_in + n_grad : n_in + n_grad + 6]
    rest = refs[n_in + n_grad + 6 :]
    outs = rest[:n_out]
    normed_out, grad_out, columns, norm_out, held, dqkv = rest[n_out:]
    width = out_w.shape[1]
    rows = grads[0].shape[1]
    for r, grad in enumerate(grads):
        start = pl.multiple_of((at_ref[0] ^ r) * rows, 8)
        held[pl.ds(start, rows), :] = grad[0].astype(F32)
    x = jnp.concatenate([piece[0] for piece in pieces], axis=0).astype(F32)
    unit, rate = normalise(x)
    normed_out[0] = (unit * norm[0:1] + norm[1:2]).astype(BF)
    low = held[...].astype(BF)
    grad_out[0] = low
    grad_mixed = dot(low, out_w[...], NN).astype(BF)
    for g in range(width // WIDE):
        at = g * WIDE
        parts = attend_back(
            qkv_in[0, :, at : at + WIDE],
            qkv_in[0, :, width + at : width + at + WIDE],
            qkv_in[0, :, 2 * width + at : 2 * width + at + WIDE],
            grad_mixed[:, at : at + WIDE],
            logsum_in[0, g : g + 1],
            None,
        )
        for i, part in enumerate(parts):
            dqkv[:, i * width + at : i * width + at + WIDE] = part
    store_columns(
        columns.at[0],
        [dqkv[:, i * width : (i + 1) * width] for i in range(3)] + [mixed_in[0]],
        n_out,
    )
    grad_normed = dot(dqkv[...], qkv_w[...], NT)

    @pl.when(pl.program_id(0) == 0)
    def _():
        norm_out[...] = jnp.zeros_like(norm_out)

    norm_out[0:1] += jnp.sum(grad_normed * unit, axis=0, keepdims=True)
    norm_out[1:2] += jnp.sum(grad_normed, axis=0, keepdims=True)
    total = held[...] + norm_back(grad_normed, norm[0:1], unit, rate)
    rows = outs[0].shape[1]
    for s, out in enumerate(outs):
        out[0] = total[s * rows : (s + 1) * rows].astype(BF)


def space_backward(pieces, grads, qkv, mixed, logsum, qkv_w, out_w, norm, at, first, n_out):
    frames, width = grads[0].shape[0], grads[0].shape[2]
    places = grads[0].shape[1] * len(grads)
    rows = places // n_out
    groups = width // WIDE
    n_grad = len(grads)
    whole = pl.BlockSpec(memory_space=pltpu.VMEM)
    frame = lambda *dims: pl.BlockSpec((1,) + dims, lambda f, at: (f,) + (0,) * len(dims))
    later = lambda *dims: pl.BlockSpec((1,) + dims, lambda f, at: (f + first,) + (0,) * len(dims))
    return pl.pallas_call(
        partial(space_backward_kernel, len(pieces), n_grad, n_out),
        grid_spec=pltpu.PrefetchScalarGridSpec(
            num_scalar_prefetch=1,
            grid=(frames,),
            in_specs=[later(places // len(pieces), width)] * len(pieces)
            + [frame(places // n_grad, width)] * n_grad
            + [later(places, 3 * width), later(places, width), later(groups, GROUP * places)]
            + [whole] * 3,
            out_specs=[frame(rows, width)] * n_out
            + [frame(places, width), frame(places, width), frame(places, 4 * width)]
            + [pl.BlockSpec((2, width), lambda f, at: (0, 0))],
            scratch_shapes=[
                pltpu.VMEM((places, width), F32),
                pltpu.VMEM((places, 3 * width), BF),
            ],
        ),
        out_shape=[jax.ShapeDtypeStruct((frames, rows, width), BF)] * n_out
        + [
            jax.ShapeDtypeStruct((frames, places, width), BF),
            jax.ShapeDtypeStruct((frames, places, width), BF),
            jax.ShapeDtypeStruct((frames, places, 4 * width), BF),
            jax.ShapeDtypeStruct((2, width), F32),
        ],
        compiler_params=pltpu.CompilerParams(vmem_limit_bytes=48 * MIB),
        cost_estimate=pl.CostEstimate(
            flops=2 * frames * places * width * 7 * width,
            bytes_accessed=frames * places * width * 24,
            transcendentals=0,
        ),
    )(at, *pieces, *grads, qkv, mixed, logsum, qkv_w, out_w, norm)


def time_kernel(joint, n_in, n_parts, sub, *refs):
    n_arrays = 1 if joint else n_in
    n_cots = 2 if joint else n_in
    n_moved = 2 if joint else n_in
    pieces = refs[:n_arrays]
    cots = refs[n_arrays : n_arrays + n_cots]
    qkv_w, out_w, in_w, unit_w, norm = refs[n_arrays + n_cots : n_arrays + n_cots + 5]
    rest = refs[n_arrays + n_cots + 5 :]
    results = rest[:n_arrays]
    grads = rest[n_arrays : n_arrays + n_moved]
    rest = rest[n_arrays + n_moved :]
    (
        normed_time,
        columns,
        grad_time,
        normed_mlp,
        grad_pre,
        hidden,
        grad_result,
        norm_out,
        qkv,
        dqkv,
        mixed,
        probs_logsum,
    ) = rest[:12]
    if joint:
        step, steps = pl.program_id(0), pl.num_programs(0)
        outgoing, cot_in, send, recv, c_send, c_recv, cot_sem = rest[12:]
        late = grads[1]
        my_z = lax.axis_index("fp")
        to_z = [{"fp": my_z ^ r} for r in range(n_in)]
        block = results[0].shape[-2]
        chunk = late.shape[2]
        each = chunk // block
        slot = lax.rem(step, 2)

        def late_copy(r):
            src = cots[1].at[:, pl.ds(pl.multiple_of((my_z ^ r) * chunk, 16), chunk)]
            if r == 0:
                return pltpu.make_async_copy(src, late.at[0], c_send.at[0])
            return pltpu.make_async_remote_copy(
                src_ref=src, dst_ref=late.at[r], send_sem=c_send.at[r], recv_sem=c_recv.at[r],
                device_id=to_z[r], device_id_type=MESH,
            )

        def cot_fetch(array, at, slot):
            rows = pl.ds(pl.multiple_of(at * block, 8), block)
            return pltpu.make_async_copy(
                array.at[:, :, rows], cot_in.at[slot], cot_sem.at[slot]
            )

        @pl.when(step == 0)
        def _():
            barrier = pltpu.get_barrier_semaphore()
            for peer in to_z[1:]:
                pl.semaphore_signal(barrier, inc=1, device_id=peer, device_id_type=MESH)
            pl.semaphore_wait(barrier, n_in - 1)
            for r in range(n_in):
                late_copy(r).start()
            cot_fetch(cots[0], 0, 0).start()

        @pl.when(jnp.logical_and(step + 1 < each, step + 1 < steps))
        def _():
            cot_fetch(cots[0], step + 1, 1 - slot).start()

    width = out_w.shape[1]
    frames, places = results[0].shape[-3:-1]
    all_frames = frames * n_in
    rows = all_frames * sub
    parts = places // sub

    def tokens(blocks):
        blocks = [b[...].reshape(-1, places, width) for b in blocks]
        joined = jnp.concatenate(blocks, axis=0).astype(F32)
        return jnp.concatenate(
            [joined[:, j * sub : (j + 1) * sub, :].reshape(rows, width) for j in range(parts)],
            axis=0,
        )

    def scatter(values, outs):
        grid = jnp.concatenate(
            [
                values[j * rows : (j + 1) * rows].reshape(all_frames, sub, width)
                for j in range(parts)
            ],
            axis=1,
        ).astype(BF)
        if len(outs) == 1:
            outs[0][...] = grid.reshape(outs[0].shape)
        else:
            for r, out in enumerate(outs):
                out[...] = grid[r * frames : (r + 1) * frames]

    key_place = lax.broadcasted_iota(jnp.int32, (rows, GROUP * rows), 0) % sub
    query_place = lax.broadcasted_iota(jnp.int32, (rows, GROUP * rows), 1) % sub
    bias = jnp.where(key_place == query_place, 0.0, -1e30)

    after_space = tokens(pieces)
    unit, rate = normalise(after_space)
    normed_time[...] = (unit * norm[2:3] + norm[3:4]).astype(BF)
    qkv[...] = dot(normed_time[...], qkv_w[...], NN).astype(BF)
    groups = width // WIDE
    for j in range(parts):
        at_rows = slice(j * rows, (j + 1) * rows)
        for g in range(groups):
            at = g * WIDE
            out, logsum = attend(
                qkv[at_rows, at : at + WIDE],
                qkv[at_rows, width + at : width + at + WIDE],
                qkv[at_rows, 2 * width + at : 2 * width + at + WIDE],
                bias,
            )
            mixed[at_rows, at : at + WIDE] = out
            probs_logsum[j * groups + g : j * groups + g + 1] = logsum
    after_time = after_space + dot(mixed[...], out_w[...], NT)
    unit2, rate2 = normalise(after_time)
    normed_mlp[...] = (unit2 * norm[4:5] + norm[5:6]).astype(BF)
    if joint:

        @pl.when(step == each)
        def _():
            late_copy(0).wait()
            for r in range(1, n_in):
                late_copy(r).wait_recv()
            cot_fetch(late, 0, slot).start()

        @pl.when(jnp.logical_and(step >= each, step + 1 < steps))
        def _():
            cot_fetch(late, step + 1 - each, 1 - slot).start()

        cot_fetch(cots[0], 0, slot).wait()
    cot = tokens([cot_in.at[slot]] if joint else cots)
    grad_result[...] = cot.astype(BF)
    result = after_time
    grad_normed = None
    for c in range(in_w.shape[0]):
        cols = slice(c * in_w.shape[2], (c + 1) * in_w.shape[2])
        pre = dot(normed_mlp[...], in_w[c], NN)
        below, density = gelu_parts(pre)
        hidden[:, cols] = (pre * below).astype(BF)
        result = result + dot(hidden[:, cols], unit_w[c], NT)
        grad_hidden = dot(grad_result[...], unit_w[c], NN)
        grad_pre[:, cols] = (grad_hidden * (below + pre * density)).astype(BF)
        term = dot(grad_pre[:, cols], in_w[c], NT)
        grad_normed = term if c == 0 else grad_normed + term
    scatter(result, results)

    @pl.when(pl.program_id(0) == 0)
    def _():
        norm_out[...] = jnp.zeros_like(norm_out)

    norm_out[2:3] += jnp.sum(grad_normed * unit2, axis=0, keepdims=True)
    norm_out[3:4] += jnp.sum(grad_normed, axis=0, keepdims=True)
    grad_after = cot + norm_back(grad_normed, norm[4:5], unit2, rate2)
    grad_time[...] = grad_after.astype(BF)
    grad_mixed = dot(grad_time[...], out_w[...], NN).astype(BF)
    for j in range(parts):
        at_rows = slice(j * rows, (j + 1) * rows)
        for g in range(groups):
            at = g * WIDE
            back = attend_back(
                qkv[at_rows, at : at + WIDE],
                qkv[at_rows, width + at : width + at + WIDE],
                qkv[at_rows, 2 * width + at : 2 * width + at + WIDE],
                grad_mixed[at_rows, at : at + WIDE],
                probs_logsum[j * groups + g : j * groups + g + 1],
                bias,
            )
            for i, part in enumerate(back):
                dqkv[at_rows, i * width + at : i * width + at + WIDE] = part
    store_columns(
        columns,
        [dqkv[:, i * width : (i + 1) * width] for i in range(3)] + [mixed[...]],
        n_parts,
    )
    grad_normed = dot(dqkv[...], qkv_w[...], NT)
    norm_out[0:1] += jnp.sum(grad_normed * unit, axis=0, keepdims=True)
    norm_out[1:2] += jnp.sum(grad_normed, axis=0, keepdims=True)
    grad_space = grad_after + norm_back(grad_normed, norm[2:3], unit, rate)
    if not joint:
        scatter(grad_space, grads)
        return
    scatter(grad_space, [outgoing.at[step]])
    received = grads[0]
    micros = received.shape[0]
    m, at = step // each, pl.multiple_of(lax.rem(step, each) * places, 8)
    for r in range(n_in):
        src, dst = outgoing.at[step, r], received.at[m, r, :, pl.ds(at, places)]
        if r == 0:
            pltpu.make_async_copy(src, dst, send.at[m, 0]).start()
        else:
            pltpu.make_async_remote_copy(
                src_ref=src, dst_ref=dst, send_sem=send.at[m, r], recv_sem=recv.at[m, r],
                device_id=to_z[r], device_id_type=MESH,
            ).start()

    @pl.when(step == steps - 1)
    def _():
        for r in range(1, n_in):
            late_copy(r).wait_send()
        for m in range(micros):
            for r in range(n_in):
                src = outgoing.at[pl.ds(m * each, each), r]
                dst = received.at[m, r]
                if r == 0:
                    pltpu.make_async_copy(dst, dst, send.at[m, 0]).wait()
                else:
                    for ref, wait in ((src, "wait_send"), (dst, "wait_recv")):
                        copy = pltpu.make_async_remote_copy(
                            src_ref=ref, dst_ref=ref, send_sem=send.at[m, r],
                            recv_sem=recv.at[m, r], device_id=to_z[r], device_id_type=MESH,
                        )
                        getattr(copy, wait)()


def time_layer(pieces, cots, qkv_w, out_w, in_w, unit_w, norm):
    joint = len(pieces) == 1
    frames, places, width = pieces[0].shape[-3:]
    n_in = pieces[0].shape[1] if joint else len(pieces)
    micros = pieces[0].shape[0] if joint else 1
    block = 16 if places % 16 == 0 else 8
    each = places // block
    sub = 8
    tokens = frames * n_in * block
    count = frames * n_in * places * micros
    hidden = in_w.shape[0] * in_w.shape[2]
    whole = pl.BlockSpec(memory_space=pltpu.VMEM)
    if joint:
        piece = pl.BlockSpec(
            (None, n_in, frames, block, width), lambda b: (b // each, 0, 0, b % each, 0)
        )
        any_spec = pl.BlockSpec(memory_space=pl.ANY)
        given = [piece, any_spec, any_spec]
        moved = [piece, any_spec, any_spec]
    else:
        piece = pl.BlockSpec((frames, block, width), lambda b: (0, b, 0))
        given = moved = [piece] * (2 * n_in)
    row = lambda cols: pl.BlockSpec((tokens, cols), lambda b: (b, 0))
    kept = [width, 4 * width, width, width, hidden, hidden, width]
    dma = pltpu.SemaphoreType.DMA
    sending = [
        pltpu.VMEM((micros * each, n_in, frames, block, width), BF),
        pltpu.VMEM((2, n_in, frames, block, width), BF),
        dma((micros, n_in)),
        dma((micros, n_in)),
        dma((n_in,)),
        dma((n_in,)),
        dma((2,)),
    ]
    sent = [jax.ShapeDtypeStruct(a.shape, BF) for a in pieces + cots]
    if joint:
        sent = [jax.ShapeDtypeStruct(a.shape, BF) for a in (pieces[0], pieces[0], cots[0])]
    return pl.pallas_call(
        partial(time_kernel, joint, n_in, in_w.shape[0], sub),
        grid=(micros * each,),
        in_specs=given + [whole] * 5,
        out_specs=moved + [row(cols) for cols in kept] + [pl.BlockSpec((4, width), lambda b: (0, 0))],
        out_shape=sent
        + [jax.ShapeDtypeStruct((count, cols), BF) for cols in kept]
        + [jax.ShapeDtypeStruct((4, width), F32)],
        scratch_shapes=[
            pltpu.VMEM((tokens, 3 * width), BF),
            pltpu.VMEM((tokens, 3 * width), BF),
            pltpu.VMEM((tokens, width), BF),
            pltpu.VMEM((8 * (block // sub), GROUP * frames * n_in * sub), F32),
        ]
        + (sending if joint else []),
        compiler_params=pltpu.CompilerParams(
            vmem_limit_bytes=60 * MIB,
            collective_id=4 if joint else None,
            has_side_effects=joint,
        ),
        cost_estimate=pl.CostEstimate(
            flops=2 * count * width * 2 * (4 * width + 2 * hidden),
            bytes_accessed=count * 26000,
            transcendentals=0,
        ),
    )(*pieces, *cots, qkv_w, out_w, in_w, unit_w, norm)


STEP = 192


class Copies:
    def __init__(self, send, recv):
        self.send, self.recv, self.count, self.all = send, recv, 0, []

    def add(self, src, dst, peer):
        copy = pltpu.make_async_remote_copy(
            src_ref=src, dst_ref=dst, send_sem=self.send.at[self.count],
            recv_sem=self.recv.at[self.count], device_id=peer, device_id_type=MESH,
        )
        self.count += 1
        self.all.append(copy)
        return copy


def start_all(copies):
    for copy in copies:
        copy.start()


def arrive(copies):
    for copy in copies:
        copy.wait_recv()


def blocks(count, body):
    lax.fori_loop(
        0, count // STEP, lambda i, _: body(pl.ds(pl.multiple_of(i * STEP, STEP), STEP)), None
    )


def back_kernel(
    results, grads, xs, qkv_in, mixed_in, logsum_in, qkv_w, out_w, norm_in,
    tail_time, rows_c, cols_c, rows_d, cols_d, rows_b, rows_b2, cols_b,
    out, tail_out, acts, input_grad, normed_a, low_a, cols_a, res_half,
    turned, stage, tile_in, sent, got1, held, got2, got3, total, got4,
    w_qkv, w_out, norm, logsum, dqkv, tail_sum, tail_got,
    stage_sem, tile_sem, frame_sem, out_sem, load_sem, send, recv, r_send, r_recv, i_send, i_recv,
):
    my_tp, my_y, my_z = lax.axis_index("tp"), lax.axis_index("clip"), lax.axis_index("fp")
    n_tp, n_z = lax.axis_size("tp"), lax.axis_size("fp")
    core, x = lax.rem(my_tp, 2), my_tp // 2
    micros, _, frames, chunk, width = results.shape
    places = chunk * n_z
    part = places // n_tp
    depth, cols = held.shape[2:]
    half, own = depth // 2, depth // (2 * n_z)
    all_rows = tile_in.shape[1]
    to_tp = [{"tp": my_tp ^ s} for s in range(n_tp)]
    to_core, to_x = to_tp[1], to_tp[2]
    to_y = {"clip": my_y ^ 1}
    to_z = [{"fp": my_z ^ r} for r in range(n_z)]
    peers = to_tp[1:] + to_z[1:] + [to_y]
    barrier = pltpu.get_barrier_semaphore()
    for peer in peers:
        pl.semaphore_signal(barrier, inc=1, device_id=peer, device_id_type=MESH)

    remote = Copies(send, recv)
    lefts = [[rows_c], [rows_d], [rows_b, rows_b2], [normed_a, low_a]]
    rights = [cols_c, cols_d, cols_b, cols_a]
    slots = [[0], [1], [2, 3], [0, 1]]
    place = [0, 1, 2, 0]
    lanes = [
        (0, 0, cols, True),
        (1, 0, cols, True),
        (2, 0, cols, True),
        (3, 0, cols // 2, True),
        (3, cols // 2, cols // 2, False),
    ]
    parts = [(1 - x) * 2 + 1 - core, x * 2 + 1 - core, (1 - x) * 2 + core, x * 2 + core]
    far_rows = pl.ds(pl.multiple_of((1 - my_y) * half, 16), half)
    near_rows = pl.ds(pl.multiple_of(my_y * half, 16), half)
    firsts = [
        [remote.add(sent.at[place[j], p], got1.at[j, p], to_core) for p in (0, 1)]
        for j in range(4)
    ]
    seconds, thirds, fourths = [], [], []
    for j, lo, count, y_first in lanes:
        at = pl.ds(lo, count)
        spot = held.at[place[j]]
        if y_first:
            seconds.append(
                [
                    remote.add(
                        spot.at[p, far_rows, at], got2.at[j, pl.ds(p * half, half), at], to_y
                    )
                    for p in (0, 1)
                ]
            )
            thirds.append(remote.add(spot.at[0, near_rows, at], got3.at[j, :, at], to_x))
        else:
            seconds.append([remote.add(spot.at[0, :, at], got2.at[j, :, at], to_x)])
            thirds.append(remote.add(spot.at[1, far_rows, at], got3.at[j, :, at], to_y))
        fourths.append(
            [
                remote.add(
                    total.at[j, pl.ds(pl.multiple_of((my_z ^ r) * own, 16), own), at],
                    got4.at[j, r - 1, :, at],
                    to_z[r],
                )
                for r in range(1, n_z)
            ]
        )
    tails = [
        remote.add(tail_sum.at[min(step, 3)], tail_got.at[step], peer)
        for step, peer in enumerate([to_core, to_y, to_x] + to_z[1:])
    ]
    res_z = [
        [
            remote.add(
                results.at[m, r],
                res_half.at[m, :, pl.ds(pl.multiple_of(my_z * chunk, 16), chunk)],
                to_z[r],
            )
            for r in range(1, n_z)
        ]
        for m in range(micros)
    ]
    res_tp = [
        [
            remote.add(
                res_half.at[m, :, pl.ds(s * part, part)], acts.at[m, my_tp], to_tp[s]
            )
            for s in range(1, n_tp)
        ]
        for m in range(micros)
    ]

    loads = [
        pltpu.make_async_copy(src, dst, load_sem.at[i])
        for i, (src, dst) in enumerate(
            [(qkv_w, w_qkv), (out_w, w_out), (norm_in, norm), (logsum_in, logsum)]
        )
    ]
    own_res = [
        pltpu.make_async_copy(
            results.at[m, 0],
            res_half.at[m, :, pl.ds(pl.multiple_of(my_z * chunk, 16), chunk)],
            load_sem.at[4 + m],
        )
        for m in range(micros)
    ]
    home_res = [
        pltpu.make_async_copy(
            res_half.at[m, :, pl.ds(0, part)], acts.at[m, my_tp], load_sem.at[4 + micros + m]
        )
        for m in range(micros)
    ]

    def fetch(index, tiles):
        j, p = tiles[index]
        return pltpu.make_async_copy(
            rights[j].at[:, pl.ds(pl.multiple_of(parts[p] * cols, 128), cols)],
            tile_in.at[index % 2],
            tile_sem.at[index % 2],
        )

    def fetch_left(index, todo):
        j, i, piece = todo[index]
        return pltpu.make_async_copy(
            lefts[j][i].at[pl.ds(piece * depth, depth)], stage.at[index % 2], stage_sem.at[index % 2]
        )

    def left_pieces(chunks):
        return [
            (j, i, piece)
            for j in chunks
            for i in range(len(lefts[j]))
            for piece in range(all_rows // depth)
        ]

    def turn(chunk, todo):
        for index, (j, i, piece) in enumerate(todo):
            if j == chunk:
                fetch_left(index, todo).wait()
                turned[slots[j][i], :, piece * depth : (piece + 1) * depth] = stage[index % 2].T
                if index + 2 < len(todo):
                    fetch_left(index + 2, todo).start()

    def product(index, tiles):
        j, p = tiles[index]
        fetch(index, tiles).wait()
        if index + 1 < len(tiles):
            fetch(index + 1, tiles).start()
        right = tile_in.at[index % 2]
        if p >= 2:
            firsts[j][p - 2].wait_recv()

        for lo in range(0, cols, WIDE):
            at = slice(lo, lo + WIDE)
            value = dot(turned[slots[j][0]], right[:, at], NN)
            if len(slots[j]) == 2 and lo + WIDE > 3 * cols // 4:
                other = dot(turned[slots[j][1]], right[:, at], NN)
                lane_index = lax.broadcasted_iota(jnp.int32, (depth, WIDE), 1) + lo
                value = jnp.where(lane_index >= 3 * cols // 4, other, value)
            if p < 2:
                sent[place[j], p, :, at] = value.astype(BF)
            else:
                value = value + got1[j, p - 2, :, at].astype(F32)
                held[place[j], p - 2, :, at] = value.astype(BF)

        if p < 2:
            firsts[j][p].start()
        else:
            for lane, (k, _, _, y_first) in enumerate(lanes):
                if k == j and (y_first or p == 2):
                    seconds[lane][p - 2].start()

    def after_second(lane):
        j, lo, count, y_first = lanes[lane]
        at = pl.ds(lo, count)
        spot = held.at[place[j]]
        if y_first:
            for p in (0, 1):
                seconds[lane][p].wait_recv()

                def body(rows, p=p):
                    mine = pl.ds(pl.multiple_of(rows.start + my_y * half, STEP), STEP)
                    there = pl.ds(pl.multiple_of(rows.start + p * half, STEP), STEP)
                    value = spot[p, mine, at].astype(F32) + got2[j, there, at].astype(F32)
                    spot[p, mine, at] = value.astype(BF)

                blocks(half, body)
                if p == 0:
                    thirds[lane].start()
        else:
            seconds[lane][0].wait_recv()

            def body(rows):
                value = spot[1, rows, at].astype(F32) + got2[j, rows, at].astype(F32)
                spot[1, rows, at] = value.astype(BF)

            blocks(depth, body)
            thirds[lane].start()

    def after_third(lane):
        j, lo, count, _ = lanes[lane]
        at = pl.ds(lo, count)
        thirds[lane].wait_recv()

        def body(rows):
            mine = pl.ds(pl.multiple_of(rows.start + my_y * half, STEP), STEP)
            value = held[place[j], 1, mine, at].astype(F32) + got3[j, rows, at].astype(F32)
            total[j, rows, at] = value.astype(BF)

        blocks(half, body)
        start_all(fourths[lane])

    def after_fourth(lane):
        j, lo, count, _ = lanes[lane]
        at = pl.ds(lo, count)
        value = total[j, pl.ds(pl.multiple_of(my_z * own, 16), own), at].astype(F32)
        for r in range(1, n_z):
            fourths[lane][r - 1].wait_recv()
            value = value + got4[j, r - 1, :, at].astype(F32)
        out[j, :, at] = value

    tiles = [(j, p) for j in range(3) for p in (0, 1)] + [(j, p) for j in range(3) for p in (2, 3)]
    todo = left_pieces([0, 1, 2])
    fetch_left(0, todo).start()
    fetch(0, tiles).start()
    fetch_left(1, todo).start()
    for copy in loads + own_res:
        copy.start()
    turn(0, todo)
    pl.semaphore_wait(barrier, len(peers))
    start_all(res_z[0] + res_z[1])
    for index in range(len(tiles)):
        product(index, tiles)
        if index in (1, 3):
            turn((index + 1) // 2, todo)

    for copy in loads:
        copy.wait()
    frame_total = micros * frames

    def frame_loads(f, slot):
        buf = tile_in.at[slot]
        m, at = f // frames, lax.rem(f, frames)
        pairs = [
            (xs.at[f], buf.at[pl.ds(0, places)]),
            (mixed_in.at[f], buf.at[pl.ds(places, places)]),
        ]
        pairs += [
            (
                qkv_in.at[f, :, pl.ds(i * width, width)],
                buf.at[pl.ds((2 + i) * places, places)],
            )
            for i in range(3)
        ]
        pairs += [
            (
                grads.at[m, r, at],
                buf.at[pl.ds(pl.multiple_of(5 * places + (my_z ^ r) * chunk, 16), chunk)],
            )
            for r in range(n_z)
        ]
        return [
            pltpu.make_async_copy(src, dst, frame_sem.at[slot, i])
            for i, (src, dst) in enumerate(pairs)
        ]

    def frame_stores(f, slot):
        rows = pl.ds(pl.multiple_of(f * places, 16), places)
        buf = turned.at[slot]
        pairs = [
            (
                buf.at[pl.ds(t * places, places), pl.ds(0, width)],
                cols_a.at[rows, pl.ds(t * cols, cols)],
            )
            for t in range(n_tp)
        ]
        pairs += [
            (buf.at[pl.ds(0, places), pl.ds(width, width)], normed_a.at[rows]),
            (buf.at[pl.ds(places, places), pl.ds(width, width)], low_a.at[rows]),
        ]
        return [
            pltpu.make_async_copy(src, dst, out_sem.at[slot, i])
            for i, (src, dst) in enumerate(pairs)
        ]

    grad = sent.at[1]
    for p in (0, 1):
        firsts[1][p].wait_send()
    tail_sum[...] = jnp.zeros_like(tail_sum)
    tail_sum[0, 2:6] = tail_time[...]
    start_all(frame_loads(0, 0))

    def frame(f, carry):
        slot = lax.rem(f, 2)

        @pl.when(f + 1 < frame_total)
        def _():
            start_all(frame_loads(f + 1, 1 - slot))

        @pl.when(f == 3)
        def _():
            after_second(0)

        @pl.when(f == 6)
        def _():
            after_second(1)

        @pl.when(f == 7)
        def _():
            after_third(0)

        for m in range(micros):

            @pl.when(f == 2 + 3 * m)
            def _(m=m):
                own_res[m].wait()
                arrive(res_z[m])
                start_all(res_tp[m])
                home_res[m].start()

        for copy in frame_loads(f, slot):
            copy.wait()

        @pl.when(f >= 2)
        def _():
            for copy in frame_stores(f - 2, slot):
                copy.wait()

        buf, keep = tile_in.at[slot], turned.at[slot]
        block = lambda i: slice(i * places, (i + 1) * places)
        unit, rate = normalise(buf[block(0)].astype(F32))
        keep[0:places, width : 2 * width] = (unit * norm[0:1] + norm[1:2]).astype(BF)
        low = buf[block(5)]
        keep[places : 2 * places, width : 2 * width] = low
        grad_mixed = dot(low, w_out[...], NN).astype(BF)
        for g in range(width // WIDE):
            at = slice(g * WIDE, (g + 1) * WIDE)
            back = attend_back(
                buf[block(2), at], buf[block(3), at], buf[block(4), at],
                grad_mixed[:, at], logsum[f, g : g + 1], None,
            )
            for i, value in enumerate(back):
                dqkv[:, i * width + g * WIDE : i * width + (g + 1) * WIDE] = value
        span = cols // 4
        for t in range(n_tp):
            for i in range(3):
                keep[block(t), i * span : (i + 1) * span] = dqkv[
                    :, i * width + t * span : i * width + (t + 1) * span
                ]
            keep[block(t), 3 * span : 4 * span] = buf[block(1), t * span : (t + 1) * span]
        start_all(frame_stores(f, slot))
        grad_normed = dot(dqkv[...], w_qkv[...], NT)
        tail_sum[0, 0:1] += jnp.sum(grad_normed * unit, axis=0, keepdims=True)
        tail_sum[0, 1:2] += jnp.sum(grad_normed, axis=0, keepdims=True)
        value = low.astype(F32) + norm_back(grad_normed, norm[0:1], unit, rate)
        m, at = f // frames, lax.rem(f, frames)
        grad[m, pl.ds(pl.multiple_of(at * places, 16), places), :] = value.astype(BF)
        for s in range(n_tp):
            src = grad.at[m, pl.ds(pl.multiple_of(at * places + s * part, 16), part)]
            dst = input_grad.at[m, my_tp, at]
            if s == 0:
                pltpu.make_async_copy(src, dst, i_send.at[0]).start()
            else:
                pltpu.make_async_remote_copy(
                    src_ref=src, dst_ref=dst, send_sem=i_send.at[s], recv_sem=i_recv.at[s],
                    device_id=to_tp[s], device_id_type=MESH,
                ).start()
        return carry

    lax.fori_loop(0, frame_total, frame, 0)
    for f in (frame_total - 2, frame_total - 1):
        for copy in frame_stores(f, f % 2):
            copy.wait()
    tails[0].start()

    for p in (0, 1):
        firsts[0][p].wait_send()
    last = [(3, p) for p in range(4)]
    todo = left_pieces([3])
    fetch_left(0, todo).start()
    fetch(0, last).start()
    fetch_left(1, todo).start()
    turn(3, todo)
    product(0, last)
    product(1, last)
    after_second(2)
    after_third(1)
    tails[0].wait_recv()
    tail_sum[1] = tail_sum[0] + tail_got[0]
    tails[1].start()
    for p in (0, 1):
        seconds[0][p].wait_send()
    thirds[0].wait_send()
    product(2, last)
    product(3, last)
    after_fourth(0)
    tails[1].wait_recv()
    tail_sum[2] = tail_sum[1] + tail_got[1]
    tails[2].start()
    after_third(2)
    after_second(3)
    after_second(4)
    after_fourth(1)
    tails[2].wait_recv()
    tail_sum[3] = tail_sum[2] + tail_got[2]
    start_all(tails[3:])
    after_third(3)
    after_third(4)
    after_fourth(2)
    value = tail_sum[3]
    for r in range(n_z - 1):
        tails[3 + r].wait_recv()
        value = value + tail_got[3 + r]
    tail_out[...] = value
    after_fourth(3)
    after_fourth(4)
    for m in range(micros):
        arrive(res_tp[m])
        home_res[m].wait()
    for s in range(n_tp):
        dst = input_grad.at[:, my_tp ^ s]
        if s == 0:
            pltpu.make_async_copy(dst, dst, i_send.at[0]).wait()
        else:
            for ref, wait in ((dst, "wait_send"), (dst, "wait_recv")):
                copy = pltpu.make_async_remote_copy(
                    src_ref=ref, dst_ref=ref, send_sem=i_send.at[s], recv_sem=i_recv.at[s],
                    device_id=to_tp[s], device_id_type=MESH,
                )
                getattr(copy, wait)()
    done = firsts[0] + firsts[1] + seconds[0] + [thirds[0]]
    for copy in remote.all:
        if not any(copy is other for other in done):
            copy.wait_send()


def back(results, grads, xs, qkv, mixed, logsum, qkv_w, out_w, norm, tail_time, kept):
    normed_time, columns, grad_time, normed_mlp, grad_pre, hidden, grad_result = kept
    micros, n_z, frames, chunk, width = results.shape
    n_tp = lax.axis_size("tp")
    places = chunk * n_z
    total = micros * frames
    rows = total * places
    depth, cols = width, columns.shape[1] // n_tp
    half, own = depth // 2, depth // (2 * n_z)
    part = places // n_tp
    any_spec = pl.BlockSpec(memory_space=pl.ANY)
    vmem = pl.BlockSpec(memory_space=pltpu.VMEM)
    dma = pltpu.SemaphoreType.DMA
    shape = jax.ShapeDtypeStruct
    home = shape((micros, n_tp, frames, part, width), BF)
    return pl.pallas_call(
        back_kernel,
        in_specs=[any_spec] * 9 + [vmem] + [any_spec] * 7,
        out_specs=[vmem] * 2 + [any_spec] * 6,
        out_shape=[
            shape((4, own, cols), F32),
            shape((8, width), F32),
            home,
            home,
            shape((rows, width), BF),
            shape((rows, width), BF),
            shape((rows, n_tp * cols), BF),
            shape((micros, frames, places, width), BF),
        ],
        scratch_shapes=[
            pltpu.VMEM((4, depth, rows), BF),
            pltpu.VMEM((2, depth, width), BF),
            pltpu.VMEM((2, rows, cols), BF),
            pltpu.VMEM((3, 2, depth, cols), BF),
            pltpu.VMEM((4, 2, depth, cols), BF),
            pltpu.VMEM((3, 2, depth, cols), BF),
            pltpu.VMEM((4, depth, cols), BF),
            pltpu.VMEM((4, half, cols), BF),
            pltpu.VMEM((4, half, cols), BF),
            pltpu.VMEM((4, n_z - 1, own, cols), BF),
            pltpu.VMEM((width, 3 * width), BF),
            pltpu.VMEM((width, width), BF),
            pltpu.VMEM((8, width), F32),
            pltpu.VMEM(logsum.shape, F32),
            pltpu.VMEM((places, 3 * width), BF),
            pltpu.VMEM((4, 8, width), F32),
            pltpu.VMEM((2 + n_z, 8, width), F32),
            dma((2,)),
            dma((2,)),
            dma((2, 5 + n_z)),
            dma((2, n_tp + 2)),
            dma((4 + 2 * micros,)),
            dma((N_REMOTE,)),
            dma((N_REMOTE,)),
            dma((1,)),
            dma((1,)),
            dma((n_tp,)),
            dma((n_tp,)),
        ],
        compiler_params=pltpu.CompilerParams(
            vmem_limit_bytes=60 * MIB, collective_id=5, has_side_effects=True
        ),
        cost_estimate=pl.CostEstimate(
            flops=2 * rows * width * 23 * width,
            bytes_accessed=rows * width * 60,
            transcendentals=0,
        ),
    )(
        results, grads, xs, qkv, mixed, logsum, qkv_w, out_w, norm, tail_time,
        normed_mlp, grad_pre, grad_result, hidden, normed_time, grad_time, columns,
    )


N_REMOTE = 96
N_LOCAL = 24


def front_kernel(
    inputs, cot, shard, ln_shard,
    xs_out, time_in, cots, cot_late, qkv_out, mixed_out, logsum_out,
    qkv_a, out_a, qkv_b, out_b, in_w, unit_w, norms,
    xs, sent, raw, std_qkv, std_out, ln, cot_half, qkv, mixed,
    send, recv, t_send, t_recv, local,
):
    my_tp, my_y, my_z = lax.axis_index("tp"), lax.axis_index("clip"), lax.axis_index("fp")
    n_tp, n_z = lax.axis_size("tp"), lax.axis_size("fp")
    micros, _, frames, part, width = inputs.shape
    places = part * n_tp
    chunk = places // n_z
    own = shard.shape[1]
    half = n_z * own
    cols = shard.shape[2]
    to_tp = [{"tp": my_tp ^ s} for s in range(n_tp)]
    to_core, to_x = to_tp[1], to_tp[2]
    to_y = {"clip": my_y ^ 1}
    to_z = [{"fp": my_z ^ r} for r in range(n_z)]
    peers = to_tp[1:] + to_z[1:] + [to_y]
    barrier = pltpu.get_barrier_semaphore()
    for peer in peers:
        pl.semaphore_signal(barrier, inc=1, device_id=peer, device_id_type=MESH)

    remote = Copies(send, recv)
    locals_ = []

    def here(src, dst):
        copy = pltpu.make_async_copy(src, dst, local.at[len(locals_)])
        locals_.append(copy)
        copy.start()
        return copy

    tiles = [raw.at[0], raw.at[1], in_w, unit_w]
    mine = pl.multiple_of(my_y * half + my_z * own, 16)
    near = pl.multiple_of(my_y * half, 16)
    far = pl.multiple_of((1 - my_y) * half, 16)
    away = my_tp ^ 2
    cuts = [cols // 2] + [5 * cols // 6] * 3
    own_shards = []
    by_z, by_x, by_y, by_y2, by_x2, by_core = [], [], [], [], [], []
    for j, tile in enumerate(tiles):
        cut = cuts[j]
        one, two = pl.ds(0, cut), pl.ds(cut, cols - cut)
        own_rows, near_rows, far_rows = pl.ds(mine, own), pl.ds(near, half), pl.ds(far, half)

        def same(peer, *index, tile=tile):
            return remote.add(tile.at[index], tile.at[index], peer)

        by_z.append(
            [
                remote.add(shard.at[j], tile.at[my_tp, own_rows], to_z[r])
                for r in range(1, n_z)
            ]
        )
        by_x.append(same(to_x, my_tp, near_rows, one))
        by_y.append([same(to_y, my_tp, near_rows, one), same(to_y, away, near_rows, one)])
        by_core.append(
            [
                same(to_core, my_tp, near_rows),
                same(to_core, away, near_rows, one),
                same(to_core, my_tp, far_rows, one),
                same(to_core, away, far_rows, one),
            ]
        )
        if cut < cols:
            by_y2.append(same(to_y, my_tp, near_rows, two))
            by_x2.append(same(to_x, my_tp, slice(None), two))
            by_core[j] += [
                same(to_core, my_tp, far_rows, two),
                same(to_core, away, slice(None), two),
            ]
    ln_z = [
        remote.add(ln_shard, ln.at[pl.ds(mine, own)], to_z[r]) for r in range(1, n_z)
    ]
    ln_y = remote.add(ln.at[pl.ds(near, half)], ln.at[pl.ds(near, half)], to_y)
    x_in = [
        [
            remote.add(
                inputs.at[m, my_tp ^ s],
                xs.at[pl.ds(m * frames, frames), pl.ds(s * part, part)],
                to_tp[s],
            )
            for s in range(1, n_tp)
        ]
        for m in range(micros)
    ]
    cot_in = [
        [
            remote.add(cot.at[m, my_tp ^ s], half.at[:, pl.ds(s * part, part)], to_tp[s])
            for s in range(1, n_tp)
        ]
        for m, half in enumerate((cot_half, cot_late))
    ]
    cot_z = [
        remote.add(
            cot_half.at[:, pl.ds(pl.multiple_of((my_z ^ r) * chunk, 16), chunk)],
            cots.at[r],
            to_z[r],
        )
        for r in range(1, n_z)
    ]

    own_x = [
        here(inputs.at[m, my_tp], xs.at[pl.ds(m * frames, frames), pl.ds(0, part)])
        for m in range(micros)
    ]
    own_cot = [
        here(cot.at[m, my_tp], half.at[:, pl.ds(0, part)])
        for m, half in enumerate((cot_half, cot_late))
    ]
    own_w = [here(shard.at[j], tile.at[my_tp, pl.ds(mine, own)]) for j, tile in enumerate(tiles)]
    own_ln = here(ln_shard, ln.at[pl.ds(mine, own)])

    pl.semaphore_wait(barrier, len(peers))
    start_all(by_z[0] + ln_z + x_in[0])

    def gather_start(j):
        own_w[j].wait()
        arrive(by_z[j])
        by_x[j].start()
        by_y2[j].start()
        by_core[j][0].start()

    def gather_first(j):
        by_x[j].wait_recv()
        start_all(by_y[j])
        by_core[j][1].start()

    def gather_second(j):
        by_y2[j].wait_recv()
        by_x2[j].start()
        by_core[j][4].start()

    def gather_last(j):
        arrive(by_y[j])
        start_all(by_core[j][2:4])
        by_x2[j].wait_recv()
        by_core[j][5].start()

    def standard(j):
        span = cols // 4
        for t in range(n_tp):
            for i in range(3):
                std_qkv[j, :, i * width + t * span : i * width + (t + 1) * span] = raw[
                    j, t, :, i * span : (i + 1) * span
                ]
            std_out[j, :, t * span : (t + 1) * span] = raw[j, t, :, 3 * span : 4 * span]

    gather_start(0)
    start_all(by_z[1] + by_z[2] + by_z[3])
    own_ln.wait()
    arrive(ln_z)
    ln_y.start()
    gather_first(0)
    gather_second(0)
    gather_start(1)
    start_all(cot_in[0] + x_in[1])
    gather_last(0)
    ln_y.wait_recv()
    norms[...] = ln[...].astype(F32).T[: norms.shape[0]]
    gather_start(2)
    gather_start(3)
    arrive(by_core[0])
    standard(0)
    gather_second(1)
    gather_first(1)
    own_x[0].wait()
    arrive(x_in[0])
    weights_out = [here(std_qkv.at[0], qkv_a), here(std_out.at[0], out_a)]

    def frame(f, carry):
        @pl.when(f == 2)
        def _():
            own_cot[0].wait()
            arrive(cot_in[0])
            start_all(cot_z)
            gather_second(2)
            gather_second(3)

        @pl.when(f == frames)
        def _():
            own_x[1].wait()
            arrive(x_in[1])
            gather_first(2)

        @pl.when(f == frames + 2)
        def _():
            gather_first(3)
            start_all(cot_in[1])

        x = xs[f].astype(F32)
        unit, _ = normalise(x)
        normed = (unit * norms[0:1] + norms[1:2]).astype(BF)
        qkv[f] = dot(normed, std_qkv[0], NN).astype(BF)
        for g in range(width // WIDE):
            at = g * WIDE
            out, logsum = attend(
                qkv[f, :, at : at + WIDE],
                qkv[f, :, width + at : width + at + WIDE],
                qkv[f, :, 2 * width + at : 2 * width + at + WIDE],
                None,
            )
            mixed[f, :, at : at + WIDE] = out
            logsum_out[f, g : g + 1] = logsum
        sent[f] = (x + dot(mixed[f], std_out[0], NT)).astype(BF)
        m, at_frame = f // frames, lax.rem(f, frames)
        for r in range(n_z):
            src = sent.at[f, pl.ds(pl.multiple_of((my_z ^ r) * chunk, 16), chunk)]
            dst = time_in.at[m, r, at_frame]
            if r == 0:
                pltpu.make_async_copy(src, dst, t_send.at[m, 0]).start()
            else:
                pltpu.make_async_remote_copy(
                    src_ref=src, dst_ref=dst, send_sem=t_send.at[m, r],
                    recv_sem=t_recv.at[m, r], device_id=to_z[r], device_id_type=MESH,
                ).start()
        return carry

    lax.fori_loop(0, micros * frames, frame, 0)
    kept = [here(xs, xs_out), here(qkv, qkv_out), here(mixed, mixed_out)]
    gather_last(1)
    arrive(by_core[1])
    standard(1)
    weights_out += [here(std_qkv.at[1], qkv_b), here(std_out.at[1], out_b)]
    own_cots = [
        here(cot_half.at[:, pl.ds(pl.multiple_of(my_z * chunk, 16), chunk)], cots.at[0])
    ]
    gather_last(2)
    gather_last(3)
    arrive(by_core[2])
    arrive(by_core[3])
    own_cot[1].wait()
    arrive(cot_in[1])
    arrive(cot_z)
    for m in range(micros):
        for r in range(n_z):
            src = sent.at[
                pl.ds(m * frames, frames), pl.ds(pl.multiple_of((my_z ^ r) * chunk, 16), chunk)
            ]
            dst = time_in.at[m, r]
            if r == 0:
                pltpu.make_async_copy(src, dst, t_send.at[m, 0]).wait()
            else:
                pltpu.make_async_remote_copy(
                    src_ref=src, dst_ref=dst, send_sem=t_send.at[m, r],
                    recv_sem=t_recv.at[m, r], device_id=to_z[r], device_id_type=MESH,
                ).wait()
    for copy in remote.all:
        copy.wait_send()
    for copy in kept + weights_out + own_cots:
        copy.wait()


def front(inputs, cot, shard, ln_shard):
    micros, clips, frames, part, width = inputs.shape
    n_tp, n_z = lax.axis_size("tp"), lax.axis_size("fp")
    places = part * n_tp
    total = micros * frames
    chunk = places // n_z
    cols = shard.shape[2]
    groups = width // WIDE
    any_spec = pl.BlockSpec(memory_space=pl.ANY)
    vmem = pl.BlockSpec(memory_space=pltpu.VMEM)
    dma = pltpu.SemaphoreType.DMA
    shape = jax.ShapeDtypeStruct
    weights = [(width, 3 * width), (width, width)] * 2 + [(n_tp, width, cols)] * 2
    return pl.pallas_call(
        front_kernel,
        in_specs=[any_spec] * 4,
        out_specs=[any_spec] * 6 + [vmem] + [any_spec] * 6 + [vmem],
        out_shape=[
            shape((total, places, width), BF),
            shape((micros, n_z, frames, chunk, width), BF),
            shape((n_z, frames, chunk, width), BF),
            shape((frames, places, width), BF),
            shape((total, places, 3 * width), BF),
            shape((total, places, width), BF),
            shape((total, groups, GROUP * places), F32),
        ]
        + [shape(dims, BF) for dims in weights]
        + [shape((8, width), F32)],
        scratch_shapes=[
            pltpu.VMEM((total, places, width), BF),
            pltpu.VMEM((total, places, width), BF),
            pltpu.VMEM((2, n_tp, width, cols), BF),
            pltpu.VMEM((2, width, 3 * width), BF),
            pltpu.VMEM((2, width, width), BF),
            pltpu.VMEM((width, ln_shard.shape[1]), BF),
            pltpu.VMEM((frames, places, width), BF),
            pltpu.VMEM((total, places, 3 * width), BF),
            pltpu.VMEM((total, places, width), BF),
            dma((N_REMOTE,)),
            dma((N_REMOTE,)),
            dma((micros, n_z)),
            dma((micros, n_z)),
            dma((N_LOCAL,)),
        ],
        compiler_params=pltpu.CompilerParams(
            vmem_limit_bytes=60 * MIB, collective_id=3, has_side_effects=True
        ),
        cost_estimate=pl.CostEstimate(
            flops=2 * total * places * width * 5 * width,
            bytes_accessed=total * places * width * 16,
            transcendentals=0,
        ),
    )(inputs, cot, shard, ln_shard)


def to_peer(value, axis, step):
    n = lax.axis_size(axis)
    return lax.ppermute(value, axis, [(i, i ^ step) for i in range(n)])


def swap(pieces, axis):
    return [piece if s == 0 else to_peer(piece, axis, s) for s, piece in enumerate(pieces)]


def pick(stack, index):
    return lax.dynamic_index_in_dim(stack, index, 0, keepdims=False)


def shards(
    inputs, cotangent, qkv_weight, out_spatial, out_temporal, mlp_in, mlp_out, ln_gain, ln_bias
):
    micros, clips, frames, local, width = inputs.shape
    n_tp, n_fp = lax.axis_size("tp"), lax.axis_size("fp")
    n_cf = lax.axis_size("clip") * n_fp
    assert clips == n_tp
    my_tp, my_fp = lax.axis_index("tp"), lax.axis_index("fp")
    depth = qkv_weight.shape[2]
    span = qkv_weight.shape[3]
    places = n_tp * local
    chunk = places // n_fp
    at = my_fp.astype(jnp.int32)[None]

    first = jnp.concatenate([qkv_weight[0, i] for i in range(3)] + [out_spatial.T], axis=1)
    second = jnp.concatenate([qkv_weight[1, i] for i in range(3)] + [out_temporal.T], axis=1)
    axes = ("clip", "fp", "tp")
    ln_rows = [v[i] for i in range(3) for v in (ln_gain, ln_bias)]
    whole_rows = depth % 16 == 0 and n_tp == 4 and lax.axis_size("clip") == 2 and micros == 2
    whole_rows = whole_rows and frames * places == width and span * 4 == width

    def from_chunks(chunks):
        stack = jnp.stack(chunks)
        joined = jnp.concatenate([pick(stack, my_fp ^ c) for c in range(n_fp)], axis=1)
        return [joined[:, s * local : (s + 1) * local] for s in range(n_tp)]

    def outward(pieces):
        stack = jnp.stack(swap(pieces, "tp"))
        return jnp.stack([pick(stack, my_tp ^ c) for c in range(n_tp)])

    mine = lax.axis_index("clip") * n_fp + my_fp
    kinds = lambda v: [v[:, i * span : (i + 1) * span] for i in range(4)]

    def arranged(acts, grad_input, late, space, norm_grads):
        norm_grads = norm_grads[:6].reshape(3, 2, n_cf, depth)
        norm_grads = lax.dynamic_index_in_dim(norm_grads, mine, 2, keepdims=False)
        space_g, time_g = kinds(space), kinds(late[2])
        return (
            acts,
            grad_input,
            jnp.stack([jnp.stack(space_g[:3]), jnp.stack(time_g[:3])]),
            space_g[3].T,
            time_g[3].T,
            late[0],
            late[1].T,
            norm_grads[:, 0],
            norm_grads[:, 1],
        )

    if whole_rows:
        ln_shard = jnp.stack(ln_rows + [jnp.zeros_like(ln_rows[0])] * 122, axis=1)
        shard = jnp.stack([first, second, mlp_in, mlp_out.T])
        (
            xs, time_pieces, cots, cot_late, qkv, mixed, logsum,
            qkv_space_w, out_space_w, qkv_time_w, out_time_w, in_w, unit_w, norms,
        ) = front(inputs, cotangent, shard, ln_shard)
        results, grads, _, *kept, tail = time_layer(
            [time_pieces], [cots, cot_late], qkv_time_w, out_time_w, in_w, unit_w, norms
        )
        sums, norm_grads, acts, input_grad, *_ = back(
            results, grads, xs, qkv, mixed, logsum, qkv_space_w, out_space_w, norms, tail, kept
        )
        return arranged(acts, input_grad.astype(F32), sums, sums[3], norm_grads)

    def gathered(part):
        return lax.all_gather(part, axes).reshape(n_cf, n_tp, depth, part.shape[1])

    def attention_weights(raw):
        raw = raw.reshape(n_cf, n_tp, depth, 4, span).transpose(3, 0, 2, 1, 4)
        raw = raw.reshape(4, n_cf * depth, n_tp * span)
        return jnp.concatenate([raw[0], raw[1], raw[2]], axis=1), raw[3]

    def unit_weights(raw):
        return raw.transpose(1, 0, 2, 3).reshape(n_tp, n_cf * depth, raw.shape[3])

    norms = lax.all_gather(jnp.stack(ln_rows), ("clip", "fp"))
    norms = norms.transpose(1, 0, 2).reshape(6, n_cf * depth).astype(F32)
    qkv_space_w, out_space_w = attention_weights(gathered(first))
    rest = gathered(jnp.concatenate([second, mlp_in, mlp_out.T], axis=1))
    qkv_time_w, out_time_w = attention_weights(rest[..., : 4 * span])
    in_w = unit_weights(rest[..., 4 * span : 4 * span + mlp_in.shape[1]])
    unit_w = unit_weights(rest[..., 4 * span + mlp_in.shape[1] :])

    def inward(array, m):
        return swap([pick(array[m], my_tp ^ s) for s in range(n_tp)], "tp")

    def to_chunks(pieces):
        joined = jnp.concatenate(pieces, axis=1)
        return [
            lax.dynamic_slice_in_dim(joined, (my_fp ^ r) * chunk, chunk, 1)
            for r in range(n_fp)
        ]

    space_kept, time_given = [], []
    for m in range(micros):
        x = inward(inputs, m)
        cots = swap(to_chunks(inward(cotangent, m)), "fp")
        out = space_forward(x, qkv_space_w, out_space_w, norms, at, n_fp)
        time_given.append((swap(out[:n_fp], "fp"), cots))
        space_kept.append((x,) + tuple(out[n_fp:]) + (0,))
    time_kept = []
    results = []
    space_grads = []
    for m in range(micros):
        pieces, cots = time_given[m]
        out = time_layer(pieces, cots, qkv_time_w, out_time_w, in_w, unit_w, norms)
        results.append(outward(from_chunks(swap(out[:n_fp], "fp"))))
        space_grads.append(swap(out[n_fp : 2 * n_fp], "fp"))
        time_kept.append(out[2 * n_fp :])
    space_rows = []
    input_grads = []
    flat = lambda v: v.reshape(-1, v.shape[-1])
    kept = lambda i: [k[i] for k in time_kept]
    time_chunks = [
        ([kept(3)], kept(4), True),
        ([kept(6)], kept(5), False),
        ([kept(0), kept(2)], kept(1), True),
    ]
    for m in range(micros):
        x, qkv, mixed, logsum, skip = space_kept[m]
        out = space_backward(
            x, space_grads[m], qkv, mixed, logsum, qkv_space_w, out_space_w, norms, at, skip, n_tp
        )
        input_grads.append(outward(out[:n_tp]).astype(F32))
        normed, low, columns, norm_grad = out[n_tp:]
        space_rows.append((flat(normed), flat(low), flat(columns), norm_grad))
    rows = lambda i: [k[i] for k in space_rows]
    space_chunk = ([rows(0), rows(1)], rows(2), True)
    early = scatter_grads([space_chunk], n_cf, n_tp)
    late = scatter_grads(time_chunks, n_cf, n_tp)
    norm_grads = lax.psum(jnp.concatenate([sum(rows(3)), sum(kept(7))]), axes)
    return arranged(jnp.stack(results), jnp.stack(input_grads), late, early[0], norm_grads)


def scatter_grads(chunks, n_cf, n_tp):
    tiles = []
    for lefts, rights, _ in chunks:
        cols = rights[0].shape[1] // n_tp
        total = sum(dot(a, b, TN) for a, b in zip(lefts[0], rights))
        total = total.reshape(total.shape[0], n_tp, cols)
        if len(lefts) == 2:
            other = sum(dot(a, b, TN) for a, b in zip(lefts[1], rights))
            other = other.reshape(other.shape[0], n_tp, cols)
            at = 3 * cols // 4
            total = jnp.concatenate([total[..., :at], other[..., at:]], axis=2)
        total = total.reshape(n_cf, total.shape[0] // n_cf, n_tp, cols).transpose(0, 2, 1, 3)
        tiles.append(total.reshape((n_cf * n_tp,) + total.shape[2:]))
    return lax.psum_scatter(jnp.stack(tiles, 1), ("clip", "fp", "tp"), scatter_dimension=0)


def solution(mesh):
    spread = P(None, "clip", "fp", "tp", None)
    return jax.shard_map(
        shards,
        mesh=mesh,
        in_specs=(
            spread,
            spread,
            P(None, None, ("clip", "fp"), "tp"),
            P("tp", ("clip", "fp")),
            P("tp", ("clip", "fp")),
            P(("clip", "fp"), "tp"),
            P("tp", ("clip", "fp")),
            P(None, ("clip", "fp")),
            P(None, ("clip", "fp")),
        ),
        out_specs=(
            spread,
            spread,
            P(None, None, ("clip", "fp"), "tp"),
            P("tp", ("clip", "fp")),
            P("tp", ("clip", "fp")),
            P(("clip", "fp"), "tp"),
            P("tp", ("clip", "fp")),
            P(None, ("clip", "fp")),
            P(None, ("clip", "fp")),
        ),
        check_vma=False,
    )
```

```python
from functools import partial

import jax
import jax.numpy as jnp
from jax import lax
from jax.experimental import pallas as pl
from jax.experimental.pallas import tpu as pltpu
from jax.sharding import PartitionSpec as P

HD = 64
GROUP = 4
WIDE = GROUP * HD
EPS = 1e-06
BF = jnp.bfloat16
F32 = jnp.float32
MIB = 1024 * 1024
MESH = pl.DeviceIdType.MESH

NN = (((1,), (0,)), ((), ()))
NT = (((1,), (1,)), ((), ()))
TN = (((0,), (0,)), ((), ()))


def dot(a, b, dims):
    return lax.dot_general(a, b, dims, preferred_element_type=F32)


def normalise(values):
    centre = values - jnp.mean(values, axis=-1, keepdims=True)
    spread = jnp.mean(centre * centre, axis=-1, keepdims=True)
    rate = lax.rsqrt(spread + EPS)
    return centre * rate, rate


def norm_back(upstream, gain, unit, rate):
    weighted = upstream * gain
    inner = jnp.mean(weighted * unit, axis=-1, keepdims=True)
    return rate * (weighted - jnp.mean(weighted, axis=-1, keepdims=True) - unit * inner)


def head_masks(scale):
    lanes = lax.broadcasted_iota(jnp.int32, (1, WIDE), 1) // HD
    return [jnp.where(lanes == h, scale, 0.0).astype(BF) for h in range(GROUP)]


def spread_heads(block, masks):
    return jnp.concatenate([block * mask for mask in masks], axis=0)


def gather_heads(stacked, rows):
    lanes = lax.broadcasted_iota(jnp.int32, (1, WIDE), 1) // HD
    total = stacked[:rows]
    for h in range(1, GROUP):
        total = jnp.where(lanes == h, stacked[h * rows : (h + 1) * rows], total)
    return total


def attend(queries, keys, values, bias):
    rows = queries.shape[0]
    scores = dot(keys, spread_heads(queries, head_masks(HD**-0.5)), NT)
    if bias is not None:
        scores = scores + bias
    top = jnp.max(scores, axis=0, keepdims=True)
    exponent = jnp.exp(scores - top)
    totals = jnp.sum(exponent, axis=0, keepdims=True)
    weights = (exponent * (1.0 / totals)).astype(BF)
    mixed = gather_heads(dot(weights, values, TN), rows).astype(BF)
    return mixed, top + jnp.log(totals)


def attend_back(queries, keys, values, upstream, logsum, bias):
    rows = queries.shape[0]
    spread_q = spread_heads(queries, head_masks(HD**-0.5))
    spread_g = spread_heads(upstream, head_masks(1.0))
    scores = dot(keys, spread_q, NT)
    if bias is not None:
        scores = scores + bias
    probs = jnp.exp(scores - logsum)
    grad_probs = dot(values, spread_g, NT)
    inner = jnp.sum(probs * grad_probs, axis=0, keepdims=True)
    grad_scores = (probs * (grad_probs - inner)).astype(BF)
    grad_values = dot(probs.astype(BF), spread_g, NN)
    grad_keys = dot(grad_scores, spread_q, NN)
    grad_queries = gather_heads(dot(grad_scores, keys, TN), rows) * HD**-0.5
    return grad_queries.astype(BF), grad_keys.astype(BF), grad_values.astype(BF)


def gelu_parts(pre):
    size = jnp.abs(pre) * (0.5**0.5)
    t = 1.0 / (1.0 + 0.3275911 * size)
    bell = jnp.exp(-size * size)
    poly = t * (
        0.254829592
        + t * (-0.284496736 + t * (1.421413741 + t * (-1.453152027 + t * 1.061405429)))
    )
    tail = 0.5 * poly * bell
    return jnp.where(pre >= 0, 1.0 - tail, tail), bell * 0.3989422804014327


def space_forward_kernel(n_in, n_out, at_ref, *refs):
    pieces = refs[:n_in]
    qkv_w, out_w, norm = refs[n_in : n_in + 3]
    outs = refs[n_in + 3 : n_in + 3 + n_out]
    qkv_out, mixed_out, logsum_out, held = refs[n_in + 3 + n_out :]
    width = out_w.shape[1]
    x = jnp.concatenate([piece[0] for piece in pieces], axis=0).astype(F32)
    unit, _ = normalise(x)
    normed = (unit * norm[0:1] + norm[1:2]).astype(BF)
    qkv_out[0] = dot(normed, qkv_w[...], NN).astype(BF)
    for g in range(width // WIDE):
        at = g * WIDE
        mixed, logsum = attend(
            qkv_out[0, :, at : at + WIDE],
            qkv_out[0, :, width + at : width + at + WIDE],
            qkv_out[0, :, 2 * width + at : 2 * width + at + WIDE],
            None,
        )
        mixed_out[0, :, at : at + WIDE] = mixed
        logsum_out[0, g : g + 1] = logsum
    held[...] = x + dot(mixed_out[0], out_w[...], NT)
    rows = outs[0].shape[1]
    for r, out in enumerate(outs):
        start = pl.multiple_of((at_ref[0] ^ r) * rows, 8)
        out[0] = held[pl.ds(start, rows), :].astype(BF)


def space_forward(pieces, qkv_w, out_w, norm, at, n_out):
    frames, rows, width = pieces[0].shape
    places = rows * len(pieces)
    groups = width // WIDE
    whole = pl.BlockSpec(memory_space=pltpu.VMEM)
    frame = lambda *dims: pl.BlockSpec((1,) + dims, lambda f, at: (f,) + (0,) * len(dims))
    return pl.pallas_call(
        partial(space_forward_kernel, len(pieces), n_out),
        grid_spec=pltpu.PrefetchScalarGridSpec(
            num_scalar_prefetch=1,
            grid=(frames,),
            in_specs=[frame(rows, width)] * len(pieces) + [whole] * 3,
            out_specs=[frame(places // n_out, width)] * n_out
            + [frame(places, 3 * width), frame(places, width), frame(groups, GROUP * places)],
            scratch_shapes=[pltpu.VMEM((places, width), F32)],
        ),
        out_shape=[jax.ShapeDtypeStruct((frames, places // n_out, width), BF)] * n_out
        + [
            jax.ShapeDtypeStruct((frames, places, 3 * width), BF),
            jax.ShapeDtypeStruct((frames, places, width), BF),
            jax.ShapeDtypeStruct((frames, groups, GROUP * places), F32),
        ],
        compiler_params=pltpu.CompilerParams(vmem_limit_bytes=48 * MIB),
        cost_estimate=pl.CostEstimate(
            flops=2 * frames * places * width * 5 * width,
            bytes_accessed=frames * places * width * 16,
            transcendentals=0,
        ),
    )(at, *pieces, qkv_w, out_w, norm)


def store_columns(out, kinds, n_parts):
    width = kinds[0].shape[1]
    span = width // n_parts
    for t in range(n_parts):
        for i, kind in enumerate(kinds):
            start = (t * len(kinds) + i) * span
            out[:, start : start + span] = kind[:, t * span : (t + 1) * span]


def space_backward_kernel(n_in, n_grad, n_out, at_ref, *refs):
    pieces = refs[:n_in]
    grads = refs[n_in : n_in + n_grad]
    qkv_in, mixed_in, logsum_in, qkv_w, out_w, norm = refs[n_in + n_grad : n_in + n_grad + 6]
    rest = refs[n_in + n_grad + 6 :]
    outs = rest[:n_out]
    normed_out, grad_out, columns, norm_out, held, dqkv = rest[n_out:]
    width = out_w.shape[1]
    rows = grads[0].shape[1]
    for r, grad in enumerate(grads):
        start = pl.multiple_of((at_ref[0] ^ r) * rows, 8)
        held[pl.ds(start, rows), :] = grad[0].astype(F32)
    x = jnp.concatenate([piece[0] for piece in pieces], axis=0).astype(F32)
    unit, rate = normalise(x)
    normed_out[0] = (unit * norm[0:1] + norm[1:2]).astype(BF)
    low = held[...].astype(BF)
    grad_out[0] = low
    grad_mixed = dot(low, out_w[...], NN).astype(BF)
    for g in range(width // WIDE):
        at = g * WIDE
        parts = attend_back(
            qkv_in[0, :, at : at + WIDE],
            qkv_in[0, :, width + at : width + at + WIDE],
            qkv_in[0, :, 2 * width + at : 2 * width + at + WIDE],
            grad_mixed[:, at : at + WIDE],
            logsum_in[0, g : g + 1],
            None,
        )
        for i, part in enumerate(parts):
            dqkv[:, i * width + at : i * width + at + WIDE] = part
    store_columns(
        columns.at[0],
        [dqkv[:, i * width : (i + 1) * width] for i in range(3)] + [mixed_in[0]],
        n_out,
    )
    grad_normed = dot(dqkv[...], qkv_w[...], NT)

    @pl.when(pl.program_id(0) == 0)
    def _():
        norm_out[...] = jnp.zeros_like(norm_out)

    norm_out[0:1] += jnp.sum(grad_normed * unit, axis=0, keepdims=True)
    norm_out[1:2] += jnp.sum(grad_normed, axis=0, keepdims=True)
    total = held[...] + norm_back(grad_normed, norm[0:1], unit, rate)
    rows = outs[0].shape[1]
    for s, out in enumerate(outs):
        out[0] = total[s * rows : (s + 1) * rows].astype(BF)


def space_backward(pieces, grads, qkv, mixed, logsum, qkv_w, out_w, norm, at, first, n_out):
    frames, width = grads[0].shape[0], grads[0].shape[2]
    places = grads[0].shape[1] * len(grads)
    rows = places // n_out
    groups = width // WIDE
    n_grad = len(grads)
    whole = pl.BlockSpec(memory_space=pltpu.VMEM)
    frame = lambda *dims: pl.BlockSpec((1,) + dims, lambda f, at: (f,) + (0,) * len(dims))
    later = lambda *dims: pl.BlockSpec((1,) + dims, lambda f, at: (f + first,) + (0,) * len(dims))
    return pl.pallas_call(
        partial(space_backward_kernel, len(pieces), n_grad, n_out),
        grid_spec=pltpu.PrefetchScalarGridSpec(
            num_scalar_prefetch=1,
            grid=(frames,),
            in_specs=[later(places // len(pieces), width)] * len(pieces)
            + [frame(places // n_grad, width)] * n_grad
            + [later(places, 3 * width), later(places, width), later(groups, GROUP * places)]
            + [whole] * 3,
            out_specs=[frame(rows, width)] * n_out
            + [frame(places, width), frame(places, width), frame(places, 4 * width)]
            + [pl.BlockSpec((2, width), lambda f, at: (0, 0))],
            scratch_shapes=[
                pltpu.VMEM((places, width), F32),
                pltpu.VMEM((places, 3 * width), BF),
            ],
        ),
        out_shape=[jax.ShapeDtypeStruct((frames, rows, width), BF)] * n_out
        + [
            jax.ShapeDtypeStruct((frames, places, width), BF),
            jax.ShapeDtypeStruct((frames, places, width), BF),
            jax.ShapeDtypeStruct((frames, places, 4 * width), BF),
            jax.ShapeDtypeStruct((2, width), F32),
        ],
        compiler_params=pltpu.CompilerParams(vmem_limit_bytes=48 * MIB),
        cost_estimate=pl.CostEstimate(
            flops=2 * frames * places * width * 7 * width,
            bytes_accessed=frames * places * width * 24,
            transcendentals=0,
        ),
    )(at, *pieces, *grads, qkv, mixed, logsum, qkv_w, out_w, norm)


def time_kernel(joint, n_in, n_parts, sub, *refs):
    n_arrays = 1 if joint else n_in
    n_cots = 2 if joint else n_in
    n_moved = 2 if joint else n_in
    pieces = refs[:n_arrays]
    cots = refs[n_arrays : n_arrays + n_cots]
    qkv_w, out_w, in_w, unit_w, norm = refs[n_arrays + n_cots : n_arrays + n_cots + 5]
    rest = refs[n_arrays + n_cots + 5 :]
    results = rest[:n_arrays]
    grads = rest[n_arrays : n_arrays + n_moved]
    rest = rest[n_arrays + n_moved :]
    (
        normed_time,
        columns,
        grad_time,
        normed_mlp,
        grad_pre,
        hidden,
        grad_result,
        norm_out,
        qkv_all,
        dqkv,
        mixed_all,
        logsum_all,
        after_all,
    ) = rest[:13]
    if joint:
        (
            outgoing, cot_in, in_held, unit_held, send, recv, c_send, c_recv, cot_sem,
            g_send, g_recv, w_sem,
        ) = rest[13:]
        late = grads[1]
        my_tp, my_y, my_z = lax.axis_index("tp"), lax.axis_index("clip"), lax.axis_index("fp")
        to_z = [{"fp": my_z ^ r} for r in range(n_in)]
        to_core, to_x, to_y = {"tp": my_tp ^ 1}, {"tp": my_tp ^ 2}, {"clip": my_y ^ 1}
        block = results[0].shape[-2]
        chunk = late.shape[3]
        each = chunk // block
        steps = pl.num_programs(0)
        count = steps // 2
        step = pl.program_id(0)
        at_block = lax.rem(step, count)
        slot = lax.rem(at_block, 2)
        half, cols = in_w.shape[1] // 2, in_w.shape[2]
        near = pl.ds(pl.multiple_of(my_y * half, 16), half)
        far = pl.ds(pl.multiple_of((1 - my_y) * half, 16), half)
        one, two = pl.ds(0, cols // 2), pl.ds(cols // 2, cols // 2)
        away = my_tp ^ 2
        ways = [(in_w, in_held), (unit_w, unit_held)]

        def gather(j, i):
            given, held = ways[j]
            src, at, peer = [
                (given, (my_tp, near, one), to_y),
                (given, (away, near, one), to_y),
                (given, (my_tp, slice(None), two), to_x),
                (given, (my_tp, near), to_core),
                (given, (away, near, one), to_core),
                (given, (my_tp, far, two), to_core),
                (held, (my_tp, far, one), to_core),
                (held, (away, far, one), to_core),
                (held, (away, slice(None), two), to_core),
            ][i]
            return pltpu.make_async_remote_copy(
                src_ref=src.at[at], dst_ref=held.at[at], send_sem=g_send.at[j, i],
                recv_sem=g_recv.at[j, i], device_id=peer, device_id_type=MESH,
            )

        def own_parts(j):
            given, held = ways[j]
            return [
                pltpu.make_async_copy(given.at[at], held.at[at], w_sem.at[j, i])
                for i, at in enumerate([(my_tp, near), (my_tp, far, two), (away, near, one)])
            ]

        def late_copy(m, r):
            src = cots[m].at[:, pl.ds(pl.multiple_of((my_z ^ r) * chunk, 16), chunk)]
            if r == 0:
                return pltpu.make_async_copy(src, late.at[m, 0], c_send.at[m, 0])
            return pltpu.make_async_remote_copy(
                src_ref=src, dst_ref=late.at[m, r], send_sem=c_send.at[m, r],
                recv_sem=c_recv.at[m, r], device_id=to_z[r], device_id_type=MESH,
            )

        def cot_fetch(at, slot):
            m, rows = at // each, pl.ds(pl.multiple_of(lax.rem(at, each) * block, 8), block)
            return pltpu.make_async_copy(
                late.at[m, :, :, rows], cot_in.at[slot], cot_sem.at[slot]
            )

        @pl.when(step == 0)
        def _():
            peers = to_z[1:] + [to_core, to_x, to_y]
            barrier = pltpu.get_barrier_semaphore()
            for peer in peers:
                pl.semaphore_signal(barrier, inc=1, device_id=peer, device_id_type=MESH)
            for j in range(2):
                start_all(own_parts(j))
            pl.semaphore_wait(barrier, len(peers))
            for j in range(2):
                start_all([gather(j, i) for i in range(6)])
            start_all([late_copy(0, r) for r in range(n_in)])

        for j in range(2):

            @pl.when(step == count - 2 + j)
            def _(j=j):
                for i in range(3):
                    gather(j, i).wait_recv()
                start_all([gather(j, i) for i in range(6, 9)])

        @pl.when(step == count - 1)
        def _():
            start_all([late_copy(1, r) for r in range(n_in)])

        @pl.when(step == count)
        def _():
            for j in range(2):
                for copy in own_parts(j):
                    copy.wait()
                for i in range(3, 9):
                    gather(j, i).wait_recv()

        for m in range(2):

            @pl.when(step == count + m * each)
            def _(m=m):
                late_copy(m, 0).wait()
                for r in range(1, n_in):
                    late_copy(m, r).wait_recv()
                cot_fetch(m * each, slot).start()

        @pl.when(
            jnp.logical_and(
                step >= count,
                jnp.logical_and(lax.rem(at_block + 1, each) != 0, at_block + 1 < count),
            )
        )
        def _():
            cot_fetch(at_block + 1, 1 - slot).start()

    else:
        at_block = 0

    width = out_w.shape[1]
    frames, places = results[0].shape[-3:-1]
    all_frames = frames * n_in
    rows = all_frames * sub
    parts = places // sub

    def tokens(blocks):
        blocks = [b[...].reshape(-1, places, width) for b in blocks]
        joined = jnp.concatenate(blocks, axis=0).astype(F32)
        return jnp.concatenate(
            [joined[:, j * sub : (j + 1) * sub, :].reshape(rows, width) for j in range(parts)],
            axis=0,
        )

    def scatter(values, outs):
        grid = jnp.concatenate(
            [
                values[j * rows : (j + 1) * rows].reshape(all_frames, sub, width)
                for j in range(parts)
            ],
            axis=1,
        ).astype(BF)
        if len(outs) == 1:
            outs[0][...] = grid.reshape(outs[0].shape)
        else:
            for r, out in enumerate(outs):
                out[...] = grid[r * frames : (r + 1) * frames]

    key_place = lax.broadcasted_iota(jnp.int32, (rows, GROUP * rows), 0) % sub
    query_place = lax.broadcasted_iota(jnp.int32, (rows, GROUP * rows), 1) % sub
    bias = jnp.where(key_place == query_place, 0.0, -1e30)

    groups = width // WIDE
    qkv, mixed = qkv_all.at[at_block], mixed_all.at[at_block]
    probs_logsum, after = logsum_all.at[at_block], after_all.at[at_block]

    def forward():
        after_space = tokens(pieces)
        unit, _ = normalise(after_space)
        normed = (unit * norm[2:3] + norm[3:4]).astype(BF)
        qkv[...] = dot(normed, qkv_w[...], NN).astype(BF)
        for j in range(parts):
            at_rows = slice(j * rows, (j + 1) * rows)
            for g in range(groups):
                at = g * WIDE
                out, logsum = attend(
                    qkv[at_rows, at : at + WIDE],
                    qkv[at_rows, width + at : width + at + WIDE],
                    qkv[at_rows, 2 * width + at : 2 * width + at + WIDE],
                    bias,
                )
                mixed[at_rows, at : at + WIDE] = out
                probs_logsum[j * groups + g : j * groups + g + 1] = logsum
        after[...] = after_space + dot(mixed[...], out_w[...], NT)

    def backward():
        time_backward(after[...])

    def time_backward(after_time):
        after_space = tokens(pieces)
        unit, rate = normalise(after_space)
        normed_time[...] = (unit * norm[2:3] + norm[3:4]).astype(BF)
        unit2, rate2 = normalise(after_time)
        normed_mlp[...] = (unit2 * norm[4:5] + norm[5:6]).astype(BF)
        if joint:
            cot_fetch(at_block, slot).wait()
        cot = tokens([cot_in.at[slot]] if joint else cots)
        w_in, w_unit = (in_held, unit_held) if joint else (in_w, unit_w)
        grad_result[...] = cot.astype(BF)
        result = after_time
        grad_normed = None
        for c in range(in_w.shape[0]):
            cols = slice(c * in_w.shape[2], (c + 1) * in_w.shape[2])
            pre = dot(normed_mlp[...], w_in[c], NN)
            below, density = gelu_parts(pre)
            hidden[:, cols] = (pre * below).astype(BF)
            result = result + dot(hidden[:, cols], w_unit[c], NT)
            grad_hidden = dot(grad_result[...], w_unit[c], NN)
            grad_pre[:, cols] = (grad_hidden * (below + pre * density)).astype(BF)
            term = dot(grad_pre[:, cols], w_in[c], NT)
            grad_normed = term if c == 0 else grad_normed + term
        scatter(result, results)

        @pl.when(at_block == 0 if joint else pl.program_id(0) == 0)
        def _():
            norm_out[...] = jnp.zeros_like(norm_out)

        norm_out[2:3] += jnp.sum(grad_normed * unit2, axis=0, keepdims=True)
        norm_out[3:4] += jnp.sum(grad_normed, axis=0, keepdims=True)
        grad_after = cot + norm_back(grad_normed, norm[4:5], unit2, rate2)
        grad_time[...] = grad_after.astype(BF)
        grad_mixed = dot(grad_time[...], out_w[...], NN).astype(BF)
        for j in range(parts):
            at_rows = slice(j * rows, (j + 1) * rows)
            for g in range(groups):
                at = g * WIDE
                back = attend_back(
                    qkv[at_rows, at : at + WIDE],
                    qkv[at_rows, width + at : width + at + WIDE],
                    qkv[at_rows, 2 * width + at : 2 * width + at + WIDE],
                    grad_mixed[at_rows, at : at + WIDE],
                    probs_logsum[j * groups + g : j * groups + g + 1],
                    bias,
                )
                for i, part in enumerate(back):
                    dqkv[at_rows, i * width + at : i * width + at + WIDE] = part
        store_columns(
            columns,
            [dqkv[:, i * width : (i + 1) * width] for i in range(3)] + [mixed[...]],
            n_parts,
        )
        grad_normed = dot(dqkv[...], qkv_w[...], NT)
        norm_out[0:1] += jnp.sum(grad_normed * unit, axis=0, keepdims=True)
        norm_out[1:2] += jnp.sum(grad_normed, axis=0, keepdims=True)
        grad_space = grad_after + norm_back(grad_normed, norm[2:3], unit, rate)
        if not joint:
            scatter(grad_space, grads)
            return
        scatter(grad_space, [outgoing.at[at_block]])
        received = grads[0]
        micros = received.shape[0]
        m, at = at_block // each, pl.multiple_of(lax.rem(at_block, each) * places, 8)
        for r in range(n_in):
            src, dst = outgoing.at[at_block, r], received.at[m, r, :, pl.ds(at, places)]
            if r == 0:
                pltpu.make_async_copy(src, dst, send.at[m, 0]).start()
            else:
                pltpu.make_async_remote_copy(
                    src_ref=src, dst_ref=dst, send_sem=send.at[m, r], recv_sem=recv.at[m, r],
                    device_id=to_z[r], device_id_type=MESH,
                ).start()

        @pl.when(step == steps - 1)
        def _():
            for j in range(2):
                for i in range(9):
                    gather(j, i).wait_send()
            for m in range(micros):
                for r in range(1, n_in):
                    late_copy(m, r).wait_send()
            for m in range(micros):
                for r in range(n_in):
                    src = outgoing.at[pl.ds(m * each, each), r]
                    dst = received.at[m, r]
                    if r == 0:
                        pltpu.make_async_copy(dst, dst, send.at[m, 0]).wait()
                    else:
                        for ref, wait in ((src, "wait_send"), (dst, "wait_recv")):
                            copy = pltpu.make_async_remote_copy(
                                src_ref=ref, dst_ref=ref, send_sem=send.at[m, r],
                                recv_sem=recv.at[m, r], device_id=to_z[r], device_id_type=MESH,
                            )
                            getattr(copy, wait)()

    if joint:
        pl.when(step < count)(forward)
        pl.when(step >= count)(backward)
    else:
        forward()
        backward()


def time_layer(pieces, cots, qkv_w, out_w, in_w, unit_w, norm):
    joint = len(pieces) == 1
    frames, places, width = pieces[0].shape[-3:]
    n_in = pieces[0].shape[1] if joint else len(pieces)
    micros = pieces[0].shape[0] if joint else 1
    block = 16 if places % 16 == 0 else 8
    each = places // block
    sub = 8
    tokens = frames * n_in * block
    count = frames * n_in * places * micros
    hidden = in_w.shape[0] * in_w.shape[2]
    whole = pl.BlockSpec(memory_space=pltpu.VMEM)
    if joint:
        blocks_all = micros * each

        def joint_piece(place):
            return pl.BlockSpec(
                (None, n_in, frames, block, width),
                lambda b: (place(b) // each, 0, 0, place(b) % each, 0),
            )

        piece = joint_piece(lambda b: b % blocks_all)
        any_spec = pl.BlockSpec(memory_space=pl.ANY)
        later = lambda b: jnp.maximum(b - blocks_all, 0)
        given = [piece, any_spec, any_spec, whole, whole, any_spec, any_spec, whole]
        moved = [joint_piece(later), any_spec, any_spec]
        row = lambda cols: pl.BlockSpec((tokens, cols), lambda b: (later(b), 0))
    else:
        piece = pl.BlockSpec((frames, block, width), lambda b: (0, b, 0))
        moved = [piece] * (2 * n_in)
        given = moved + [whole] * 5
        row = lambda cols: pl.BlockSpec((tokens, cols), lambda b: (b, 0))
    kept = [width, 4 * width, width, width, hidden, hidden, width]
    dma = pltpu.SemaphoreType.DMA
    n_kept = micros * each if joint else 1
    sending = [
        pltpu.VMEM((micros * each, n_in, frames, block, width), BF),
        pltpu.VMEM((2, n_in, frames, block, width), BF),
        pltpu.VMEM(in_w.shape, BF),
        pltpu.VMEM(unit_w.shape, BF),
        dma((micros, n_in)),
        dma((micros, n_in)),
        dma((micros, n_in)),
        dma((micros, n_in)),
        dma((2,)),
        dma((2, 9)),
        dma((2, 9)),
        dma((2, 3)),
    ]
    sent = [jax.ShapeDtypeStruct(a.shape, BF) for a in pieces + cots]
    if joint:
        sent = [jax.ShapeDtypeStruct(pieces[0].shape, BF)] * 3
    return pl.pallas_call(
        partial(time_kernel, joint, n_in, in_w.shape[0], sub),
        grid=(2 * micros * each if joint else each,),
        in_specs=given,
        out_specs=moved + [row(cols) for cols in kept] + [pl.BlockSpec((4, width), lambda b: (0, 0))],
        out_shape=sent
        + [jax.ShapeDtypeStruct((count, cols), BF) for cols in kept]
        + [jax.ShapeDtypeStruct((4, width), F32)],
        scratch_shapes=[
            pltpu.VMEM((n_kept, tokens, 3 * width), BF),
            pltpu.VMEM((tokens, 3 * width), BF),
            pltpu.VMEM((n_kept, tokens, width), BF),
            pltpu.VMEM((n_kept, 8 * (block // sub), GROUP * frames * n_in * sub), F32),
            pltpu.VMEM((n_kept, tokens, width), F32),
        ]
        + (sending if joint else []),
        compiler_params=pltpu.CompilerParams(
            vmem_limit_bytes=60 * MIB,
            collective_id=4 if joint else None,
            has_side_effects=joint,
        ),
        cost_estimate=pl.CostEstimate(
            flops=2 * count * width * 2 * (4 * width + 2 * hidden),
            bytes_accessed=count * 26000,
            transcendentals=0,
        ),
    )(*pieces, *cots, qkv_w, out_w, in_w, unit_w, norm)


STEP = 192


class Copies:
    def __init__(self, send, recv):
        self.send, self.recv, self.count, self.all = send, recv, 0, []

    def add(self, src, dst, peer):
        copy = pltpu.make_async_remote_copy(
            src_ref=src, dst_ref=dst, send_sem=self.send.at[self.count],
            recv_sem=self.recv.at[self.count], device_id=peer, device_id_type=MESH,
        )
        self.count += 1
        self.all.append(copy)
        return copy


def start_all(copies):
    for copy in copies:
        copy.start()


def arrive(copies):
    for copy in copies:
        copy.wait_recv()


def blocks(count, body):
    lax.fori_loop(
        0, count // STEP, lambda i, _: body(pl.ds(pl.multiple_of(i * STEP, STEP), STEP)), None
    )


def back_kernel(
    results, grads, xs, qkv_in, mixed_in, logsum_in, qkv_w, out_w, norm_in,
    tail_time, rows_c, cols_c, rows_d, cols_d, rows_b, rows_b2, cols_b,
    out, tail_out, acts, input_grad, normed_a, low_a, cols_a, res_half,
    turned, stage, tile_in, sent, got1, held, got2, got3, total, got4,
    w_qkv, w_out, norm, logsum, dqkv, tail_sum, tail_got,
    stage_sem, tile_sem, frame_sem, out_sem, load_sem, send, recv, r_send, r_recv, i_send, i_recv,
):
    my_tp, my_y, my_z = lax.axis_index("tp"), lax.axis_index("clip"), lax.axis_index("fp")
    n_tp, n_z = lax.axis_size("tp"), lax.axis_size("fp")
    core, x = lax.rem(my_tp, 2), my_tp // 2
    micros, _, frames, chunk, width = results.shape
    places = chunk * n_z
    part = places // n_tp
    depth, cols = held.shape[2:]
    half, own = depth // 2, depth // (2 * n_z)
    all_rows = tile_in.shape[1]
    to_tp = [{"tp": my_tp ^ s} for s in range(n_tp)]
    to_core, to_x = to_tp[1], to_tp[2]
    to_y = {"clip": my_y ^ 1}
    to_z = [{"fp": my_z ^ r} for r in range(n_z)]
    peers = to_tp[1:] + to_z[1:] + [to_y]
    barrier = pltpu.get_barrier_semaphore()
    for peer in peers:
        pl.semaphore_signal(barrier, inc=1, device_id=peer, device_id_type=MESH)

    remote = Copies(send, recv)
    lefts = [[rows_c], [rows_d], [rows_b, rows_b2], [normed_a, low_a]]
    rights = [cols_c, cols_d, cols_b, cols_a]
    slots = [[0], [1], [2, 3], [0, 1]]
    place = [0, 1, 2, 0]
    lanes = [
        (0, 0, cols, True),
        (1, 0, cols, True),
        (2, 0, cols, True),
        (3, 0, cols // 2, True),
        (3, cols // 2, cols // 2, False),
    ]
    parts = [(1 - x) * 2 + 1 - core, x * 2 + 1 - core, (1 - x) * 2 + core, x * 2 + core]
    far_rows = pl.ds(pl.multiple_of((1 - my_y) * half, 16), half)
    near_rows = pl.ds(pl.multiple_of(my_y * half, 16), half)
    firsts = [
        [remote.add(sent.at[place[j], p], got1.at[j, p], to_core) for p in (0, 1)]
        for j in range(4)
    ]
    seconds, thirds, fourths = [], [], []
    for j, lo, count, y_first in lanes:
        at = pl.ds(lo, count)
        spot = held.at[place[j]]
        if y_first:
            seconds.append(
                [
                    remote.add(
                        spot.at[p, far_rows, at], got2.at[j, pl.ds(p * half, half), at], to_y
                    )
                    for p in (0, 1)
                ]
            )
            thirds.append(remote.add(spot.at[0, near_rows, at], got3.at[j, :, at], to_x))
        else:
            seconds.append([remote.add(spot.at[0, :, at], got2.at[j, :, at], to_x)])
            thirds.append(remote.add(spot.at[1, far_rows, at], got3.at[j, :, at], to_y))
        fourths.append(
            [
                remote.add(
                    total.at[j, pl.ds(pl.multiple_of((my_z ^ r) * own, 16), own), at],
                    got4.at[j, r - 1, :, at],
                    to_z[r],
                )
                for r in range(1, n_z)
            ]
        )
    tails = [
        remote.add(tail_sum.at[min(step, 3)], tail_got.at[step], peer)
        for step, peer in enumerate([to_core, to_y, to_x] + to_z[1:])
    ]
    res_z = [
        [
            remote.add(
                results.at[m, r],
                res_half.at[m, :, pl.ds(pl.multiple_of(my_z * chunk, 16), chunk)],
                to_z[r],
            )
            for r in range(1, n_z)
        ]
        for m in range(micros)
    ]
    res_tp = [
        [
            remote.add(
                res_half.at[m, :, pl.ds(s * part, part)], acts.at[m, my_tp], to_tp[s]
            )
            for s in range(1, n_tp)
        ]
        for m in range(micros)
    ]

    loads = [
        pltpu.make_async_copy(src, dst, load_sem.at[i])
        for i, (src, dst) in enumerate(
            [(qkv_w, w_qkv), (out_w, w_out), (norm_in, norm), (logsum_in, logsum)]
        )
    ]
    own_res = [
        pltpu.make_async_copy(
            results.at[m, 0],
            res_half.at[m, :, pl.ds(pl.multiple_of(my_z * chunk, 16), chunk)],
            load_sem.at[4 + m],
        )
        for m in range(micros)
    ]
    home_res = [
        pltpu.make_async_copy(
            res_half.at[m, :, pl.ds(0, part)], acts.at[m, my_tp], load_sem.at[4 + micros + m]
        )
        for m in range(micros)
    ]

    def fetch(index, tiles):
        j, p = tiles[index]
        return pltpu.make_async_copy(
            rights[j].at[:, pl.ds(pl.multiple_of(parts[p] * cols, 128), cols)],
            tile_in.at[index % 2],
            tile_sem.at[index % 2],
        )

    def fetch_left(index, todo):
        j, i, piece = todo[index]
        return pltpu.make_async_copy(
            lefts[j][i].at[pl.ds(piece * depth, depth)], stage.at[index % 2], stage_sem.at[index % 2]
        )

    def left_pieces(chunks):
        return [
            (j, i, piece)
            for j in chunks
            for i in range(len(lefts[j]))
            for piece in range(all_rows // depth)
        ]

    def turn(chunk, todo):
        for index, (j, i, piece) in enumerate(todo):
            if j == chunk:
                fetch_left(index, todo).wait()
                turned[slots[j][i], :, piece * depth : (piece + 1) * depth] = stage[index % 2].T
                if index + 2 < len(todo):
                    fetch_left(index + 2, todo).start()

    def product(index, tiles):
        j, p = tiles[index]
        fetch(index, tiles).wait()
        if index + 1 < len(tiles):
            fetch(index + 1, tiles).start()
        right = tile_in.at[index % 2]
        if p >= 2:
            firsts[j][p - 2].wait_recv()

        for lo in range(0, cols, WIDE):
            at = slice(lo, lo + WIDE)
            value = dot(turned[slots[j][0]], right[:, at], NN)
            if len(slots[j]) == 2 and lo + WIDE > 3 * cols // 4:
                other = dot(turned[slots[j][1]], right[:, at], NN)
                lane_index = lax.broadcasted_iota(jnp.int32, (depth, WIDE), 1) + lo
                value = jnp.where(lane_index >= 3 * cols // 4, other, value)
            if p < 2:
                sent[place[j], p, :, at] = value.astype(BF)
            else:
                value = value + got1[j, p - 2, :, at].astype(F32)
                held[place[j], p - 2, :, at] = value.astype(BF)

        if p < 2:
            firsts[j][p].start()
        else:
            for lane, (k, _, _, y_first) in enumerate(lanes):
                if k == j and (y_first or p == 2):
                    seconds[lane][p - 2].start()

    def after_second(lane):
        j, lo, count, y_first = lanes[lane]
        at = pl.ds(lo, count)
        spot = held.at[place[j]]
        if y_first:
            for p in (0, 1):
                seconds[lane][p].wait_recv()

                def body(rows, p=p):
                    mine = pl.ds(pl.multiple_of(rows.start + my_y * half, STEP), STEP)
                    there = pl.ds(pl.multiple_of(rows.start + p * half, STEP), STEP)
                    value = spot[p, mine, at].astype(F32) + got2[j, there, at].astype(F32)
                    spot[p, mine, at] = value.astype(BF)

                blocks(half, body)
                if p == 0:
                    thirds[lane].start()
        else:
            seconds[lane][0].wait_recv()

            def body(rows):
                value = spot[1, rows, at].astype(F32) + got2[j, rows, at].astype(F32)
                spot[1, rows, at] = value.astype(BF)

            blocks(depth, body)
            thirds[lane].start()

    def after_third(lane):
        j, lo, count, _ = lanes[lane]
        at = pl.ds(lo, count)
        thirds[lane].wait_recv()

        def body(rows):
            mine = pl.ds(pl.multiple_of(rows.start + my_y * half, STEP), STEP)
            value = held[place[j], 1, mine, at].astype(F32) + got3[j, rows, at].astype(F32)
            total[j, rows, at] = value.astype(BF)

        blocks(half, body)
        start_all(fourths[lane])

    def after_fourth(lane):
        j, lo, count, _ = lanes[lane]
        at = pl.ds(lo, count)
        value = total[j, pl.ds(pl.multiple_of(my_z * own, 16), own), at].astype(F32)
        for r in range(1, n_z):
            fourths[lane][r - 1].wait_recv()
            value = value + got4[j, r - 1, :, at].astype(F32)
        out[j, :, at] = value

    tiles = [(j, p) for j in range(3) for p in (0, 1)] + [(j, p) for j in range(3) for p in (2, 3)]
    todo = left_pieces([0, 1, 2])
    fetch_left(0, todo).start()
    fetch(0, tiles).start()
    fetch_left(1, todo).start()
    for copy in loads + own_res:
        copy.start()
    turn(0, todo)
    pl.semaphore_wait(barrier, len(peers))
    start_all(res_z[0] + res_z[1])
    for index in range(len(tiles)):
        product(index, tiles)
        if index in (1, 3):
            turn((index + 1) // 2, todo)

    for copy in loads:
        copy.wait()
    frame_total = micros * frames

    def frame_loads(f, slot):
        buf = tile_in.at[slot]
        m, at = f // frames, lax.rem(f, frames)
        pairs = [
            (xs.at[f], buf.at[pl.ds(0, places)]),
            (mixed_in.at[f], buf.at[pl.ds(places, places)]),
        ]
        pairs += [
            (
                qkv_in.at[f, :, pl.ds(i * width, width)],
                buf.at[pl.ds((2 + i) * places, places)],
            )
            for i in range(3)
        ]
        pairs += [
            (
                grads.at[m, r, at],
                buf.at[pl.ds(pl.multiple_of(5 * places + (my_z ^ r) * chunk, 16), chunk)],
            )
            for r in range(n_z)
        ]
        return [
            pltpu.make_async_copy(src, dst, frame_sem.at[slot, i])
            for i, (src, dst) in enumerate(pairs)
        ]

    def frame_stores(f, slot):
        rows = pl.ds(pl.multiple_of(f * places, 16), places)
        buf = turned.at[slot]
        pairs = [
            (
                buf.at[pl.ds(t * places, places), pl.ds(0, width)],
                cols_a.at[rows, pl.ds(t * cols, cols)],
            )
            for t in range(n_tp)
        ]
        pairs += [
            (buf.at[pl.ds(0, places), pl.ds(width, width)], normed_a.at[rows]),
            (buf.at[pl.ds(places, places), pl.ds(width, width)], low_a.at[rows]),
        ]
        return [
            pltpu.make_async_copy(src, dst, out_sem.at[slot, i])
            for i, (src, dst) in enumerate(pairs)
        ]

    grad = sent.at[1]
    for p in (0, 1):
        firsts[1][p].wait_send()
    tail_sum[...] = jnp.zeros_like(tail_sum)
    tail_sum[0, 2:6] = tail_time[...]
    start_all(frame_loads(0, 0))

    def frame(f, carry):
        slot = lax.rem(f, 2)

        @pl.when(f + 1 < frame_total)
        def _():
            start_all(frame_loads(f + 1, 1 - slot))

        @pl.when(f == 3)
        def _():
            after_second(0)

        @pl.when(f == 6)
        def _():
            after_second(1)

        @pl.when(f == 7)
        def _():
            after_third(0)

        for m in range(micros):

            @pl.when(f == 2 + 3 * m)
            def _(m=m):
                own_res[m].wait()
                arrive(res_z[m])
                start_all(res_tp[m])
                home_res[m].start()

        for copy in frame_loads(f, slot):
            copy.wait()

        @pl.when(f >= 2)
        def _():
            for copy in frame_stores(f - 2, slot):
                copy.wait()

        buf, keep = tile_in.at[slot], turned.at[slot]
        block = lambda i: slice(i * places, (i + 1) * places)
        unit, rate = normalise(buf[block(0)].astype(F32))
        keep[0:places, width : 2 * width] = (unit * norm[0:1] + norm[1:2]).astype(BF)
        low = buf[block(5)]
        keep[places : 2 * places, width : 2 * width] = low
        grad_mixed = dot(low, w_out[...], NN).astype(BF)
        for g in range(width // WIDE):
            at = slice(g * WIDE, (g + 1) * WIDE)
            back = attend_back(
                buf[block(2), at], buf[block(3), at], buf[block(4), at],
                grad_mixed[:, at], logsum[f, g : g + 1], None,
            )
            for i, value in enumerate(back):
                dqkv[:, i * width + g * WIDE : i * width + (g + 1) * WIDE] = value
        span = cols // 4
        for t in range(n_tp):
            for i in range(3):
                keep[block(t), i * span : (i + 1) * span] = dqkv[
                    :, i * width + t * span : i * width + (t + 1) * span
                ]
            keep[block(t), 3 * span : 4 * span] = buf[block(1), t * span : (t + 1) * span]
        start_all(frame_stores(f, slot))
        grad_normed = dot(dqkv[...], w_qkv[...], NT)
        tail_sum[0, 0:1] += jnp.sum(grad_normed * unit, axis=0, keepdims=True)
        tail_sum[0, 1:2] += jnp.sum(grad_normed, axis=0, keepdims=True)
        value = low.astype(F32) + norm_back(grad_normed, norm[0:1], unit, rate)
        m, at = f // frames, lax.rem(f, frames)
        grad[m, pl.ds(pl.multiple_of(at * places, 16), places), :] = value.astype(BF)
        for s in range(n_tp):
            src = grad.at[m, pl.ds(pl.multiple_of(at * places + s * part, 16), part)]
            dst = input_grad.at[m, my_tp, at]
            if s == 0:
                pltpu.make_async_copy(src, dst, i_send.at[0]).start()
            else:
                pltpu.make_async_remote_copy(
                    src_ref=src, dst_ref=dst, send_sem=i_send.at[s], recv_sem=i_recv.at[s],
                    device_id=to_tp[s], device_id_type=MESH,
                ).start()
        return carry

    lax.fori_loop(0, frame_total, frame, 0)
    for f in (frame_total - 2, frame_total - 1):
        for copy in frame_stores(f, f % 2):
            copy.wait()
    tails[0].start()

    for p in (0, 1):
        firsts[0][p].wait_send()
    last = [(3, p) for p in range(4)]
    todo = left_pieces([3])
    fetch_left(0, todo).start()
    fetch(0, last).start()
    fetch_left(1, todo).start()
    turn(3, todo)
    product(0, last)
    product(1, last)
    after_second(2)
    after_third(1)
    tails[0].wait_recv()
    tail_sum[1] = tail_sum[0] + tail_got[0]
    tails[1].start()
    for p in (0, 1):
        seconds[0][p].wait_send()
    thirds[0].wait_send()
    product(2, last)
    product(3, last)
    after_fourth(0)
    tails[1].wait_recv()
    tail_sum[2] = tail_sum[1] + tail_got[1]
    tails[2].start()
    after_third(2)
    after_second(3)
    after_second(4)
    after_fourth(1)
    tails[2].wait_recv()
    tail_sum[3] = tail_sum[2] + tail_got[2]
    start_all(tails[3:])
    after_third(3)
    after_third(4)
    after_fourth(2)
    value = tail_sum[3]
    for r in range(n_z - 1):
        tails[3 + r].wait_recv()
        value = value + tail_got[3 + r]
    tail_out[...] = value
    after_fourth(3)
    after_fourth(4)
    for m in range(micros):
        arrive(res_tp[m])
        home_res[m].wait()
    for s in range(n_tp):
        dst = input_grad.at[:, my_tp ^ s]
        if s == 0:
            pltpu.make_async_copy(dst, dst, i_send.at[0]).wait()
        else:
            for ref, wait in ((dst, "wait_send"), (dst, "wait_recv")):
                copy = pltpu.make_async_remote_copy(
                    src_ref=ref, dst_ref=ref, send_sem=i_send.at[s], recv_sem=i_recv.at[s],
                    device_id=to_tp[s], device_id_type=MESH,
                )
                getattr(copy, wait)()
    done = firsts[0] + firsts[1] + seconds[0] + [thirds[0]]
    for copy in remote.all:
        if not any(copy is other for other in done):
            copy.wait_send()


def back(results, grads, xs, qkv, mixed, logsum, qkv_w, out_w, norm, tail_time, kept):
    normed_time, columns, grad_time, normed_mlp, grad_pre, hidden, grad_result = kept
    micros, n_z, frames, chunk, width = results.shape
    n_tp = lax.axis_size("tp")
    places = chunk * n_z
    total = micros * frames
    rows = total * places
    depth, cols = width, columns.shape[1] // n_tp
    half, own = depth // 2, depth // (2 * n_z)
    part = places // n_tp
    any_spec = pl.BlockSpec(memory_space=pl.ANY)
    vmem = pl.BlockSpec(memory_space=pltpu.VMEM)
    dma = pltpu.SemaphoreType.DMA
    shape = jax.ShapeDtypeStruct
    home = shape((micros, n_tp, frames, part, width), BF)
    return pl.pallas_call(
        back_kernel,
        in_specs=[any_spec] * 9 + [vmem] + [any_spec] * 7,
        out_specs=[vmem] * 2 + [any_spec] * 6,
        out_shape=[
            shape((4, own, cols), F32),
            shape((8, width), F32),
            home,
            home,
            shape((rows, width), BF),
            shape((rows, width), BF),
            shape((rows, n_tp * cols), BF),
            shape((micros, frames, places, width), BF),
        ],
        scratch_shapes=[
            pltpu.VMEM((4, depth, rows), BF),
            pltpu.VMEM((2, depth, width), BF),
            pltpu.VMEM((2, rows, cols), BF),
            pltpu.VMEM((3, 2, depth, cols), BF),
            pltpu.VMEM((4, 2, depth, cols), BF),
            pltpu.VMEM((3, 2, depth, cols), BF),
            pltpu.VMEM((4, depth, cols), BF),
            pltpu.VMEM((4, half, cols), BF),
            pltpu.VMEM((4, half, cols), BF),
            pltpu.VMEM((4, n_z - 1, own, cols), BF),
            pltpu.VMEM((width, 3 * width), BF),
            pltpu.VMEM((width, width), BF),
            pltpu.VMEM((8, width), F32),
            pltpu.VMEM(logsum.shape, F32),
            pltpu.VMEM((places, 3 * width), BF),
            pltpu.VMEM((4, 8, width), F32),
            pltpu.VMEM((2 + n_z, 8, width), F32),
            dma((2,)),
            dma((2,)),
            dma((2, 5 + n_z)),
            dma((2, n_tp + 2)),
            dma((4 + 2 * micros,)),
            dma((N_REMOTE,)),
            dma((N_REMOTE,)),
            dma((1,)),
            dma((1,)),
            dma((n_tp,)),
            dma((n_tp,)),
        ],
        compiler_params=pltpu.CompilerParams(
            vmem_limit_bytes=60 * MIB, collective_id=5, has_side_effects=True
        ),
        cost_estimate=pl.CostEstimate(
            flops=2 * rows * width * 23 * width,
            bytes_accessed=rows * width * 60,
            transcendentals=0,
        ),
    )(
        results, grads, xs, qkv, mixed, logsum, qkv_w, out_w, norm, tail_time,
        normed_mlp, grad_pre, grad_result, hidden, normed_time, grad_time, columns,
    )


N_REMOTE = 96
N_LOCAL = 24


def front_kernel(
    inputs, cot, shard, ln_shard,
    xs_out, time_in, cot_half, cot_late, qkv_out, mixed_out, logsum_out,
    qkv_a, out_a, qkv_b, out_b, in_w, unit_w, norms,
    xs, sent, raw, std_qkv, std_out, ln, qkv, mixed,
    send, recv, t_send, t_recv, local,
):
    my_tp, my_y, my_z = lax.axis_index("tp"), lax.axis_index("clip"), lax.axis_index("fp")
    n_tp, n_z = lax.axis_size("tp"), lax.axis_size("fp")
    micros, _, frames, part, width = inputs.shape
    places = part * n_tp
    chunk = places // n_z
    own = shard.shape[1]
    half = n_z * own
    cols = shard.shape[2]
    to_tp = [{"tp": my_tp ^ s} for s in range(n_tp)]
    to_core, to_x = to_tp[1], to_tp[2]
    to_y = {"clip": my_y ^ 1}
    to_z = [{"fp": my_z ^ r} for r in range(n_z)]
    peers = to_tp[1:] + to_z[1:] + [to_y]
    barrier = pltpu.get_barrier_semaphore()
    for peer in peers:
        pl.semaphore_signal(barrier, inc=1, device_id=peer, device_id_type=MESH)

    remote = Copies(send, recv)
    locals_ = []

    def here(src, dst):
        copy = pltpu.make_async_copy(src, dst, local.at[len(locals_)])
        locals_.append(copy)
        copy.start()
        return copy

    tiles = [raw.at[0], raw.at[1], in_w, unit_w]
    mine = pl.multiple_of(my_y * half + my_z * own, 16)
    near = pl.multiple_of(my_y * half, 16)
    far = pl.multiple_of((1 - my_y) * half, 16)
    away = my_tp ^ 2
    cuts = [cols // 2, 5 * cols // 6, cols // 2, cols // 2]
    own_shards = []
    by_z, by_x, by_y, by_y2, by_x2, by_core = [], [], [], [], [], []
    for j, tile in enumerate(tiles):
        cut = cuts[j]
        one, two = pl.ds(0, cut), pl.ds(cut, cols - cut)
        own_rows, near_rows, far_rows = pl.ds(mine, own), pl.ds(near, half), pl.ds(far, half)

        def same(peer, *index, tile=tile):
            return remote.add(tile.at[index], tile.at[index], peer)

        by_z.append(
            [
                remote.add(shard.at[j], tile.at[my_tp, own_rows], to_z[r])
                for r in range(1, n_z)
            ]
        )
        by_x.append(same(to_x, my_tp, near_rows, one))
        by_y2.append(same(to_y, my_tp, near_rows, two))
        if j >= 2:
            continue
        by_y.append([same(to_y, my_tp, near_rows, one), same(to_y, away, near_rows, one)])
        by_x2.append(same(to_x, my_tp, slice(None), two))
        by_core.append(
            [
                same(to_core, my_tp, near_rows),
                same(to_core, away, near_rows, one),
                same(to_core, my_tp, far_rows, one),
                same(to_core, away, far_rows, one),
                same(to_core, my_tp, far_rows, two),
                same(to_core, away, slice(None), two),
            ]
        )
    ln_z = [
        remote.add(ln_shard, ln.at[pl.ds(mine, own)], to_z[r]) for r in range(1, n_z)
    ]
    ln_y = remote.add(ln.at[pl.ds(near, half)], ln.at[pl.ds(near, half)], to_y)
    x_in = [
        [
            remote.add(
                inputs.at[m, my_tp ^ s],
                xs.at[pl.ds(m * frames, frames), pl.ds(s * part, part)],
                to_tp[s],
            )
            for s in range(1, n_tp)
        ]
        for m in range(micros)
    ]
    cot_in = [
        [
            remote.add(cot.at[m, my_tp ^ s], half.at[:, pl.ds(s * part, part)], to_tp[s])
            for s in range(1, n_tp)
        ]
        for m, half in enumerate((cot_half, cot_late))
    ]
    own_x = [
        here(inputs.at[m, my_tp], xs.at[pl.ds(m * frames, frames), pl.ds(0, part)])
        for m in range(micros)
    ]
    own_cot = [
        here(cot.at[m, my_tp], half.at[:, pl.ds(0, part)])
        for m, half in enumerate((cot_half, cot_late))
    ]
    own_w = [here(shard.at[j], tile.at[my_tp, pl.ds(mine, own)]) for j, tile in enumerate(tiles)]
    own_ln = here(ln_shard, ln.at[pl.ds(mine, own)])

    pl.semaphore_wait(barrier, len(peers))
    start_all(by_z[0] + ln_z + x_in[0])

    def gather_start(j):
        own_w[j].wait()
        arrive(by_z[j])
        by_x[j].start()
        by_y2[j].start()
        if j < 2:
            by_core[j][0].start()

    def gather_first(j):
        by_x[j].wait_recv()
        start_all(by_y[j])
        by_core[j][1].start()

    def gather_second(j):
        by_y2[j].wait_recv()
        by_x2[j].start()
        by_core[j][4].start()

    def gather_last(j):
        arrive(by_y[j])
        start_all(by_core[j][2:4])
        by_x2[j].wait_recv()
        by_core[j][5].start()

    def standard(j):
        span = cols // 4
        for t in range(n_tp):
            for i in range(3):
                std_qkv[j, :, i * width + t * span : i * width + (t + 1) * span] = raw[
                    j, t, :, i * span : (i + 1) * span
                ]
            std_out[j, :, t * span : (t + 1) * span] = raw[j, t, :, 3 * span : 4 * span]

    gather_start(0)
    start_all(by_z[1] + by_z[2] + by_z[3])
    own_ln.wait()
    arrive(ln_z)
    ln_y.start()
    gather_first(0)
    gather_second(0)
    gather_start(1)
    start_all(cot_in[0] + x_in[1])
    gather_last(0)
    ln_y.wait_recv()
    norms[...] = ln[...].astype(F32).T[: norms.shape[0]]
    gather_start(2)
    gather_start(3)
    arrive(by_core[0])
    standard(0)
    gather_second(1)
    gather_first(1)
    own_x[0].wait()
    arrive(x_in[0])
    weights_out = [here(std_qkv.at[0], qkv_a), here(std_out.at[0], out_a)]

    def frame(f, carry):
        @pl.when(f == frames)
        def _():
            own_x[1].wait()
            arrive(x_in[1])
            start_all(cot_in[1])

        x = xs[f].astype(F32)
        unit, _ = normalise(x)
        normed = (unit * norms[0:1] + norms[1:2]).astype(BF)
        qkv[f] = dot(normed, std_qkv[0], NN).astype(BF)
        for g in range(width // WIDE):
            at = g * WIDE
            out, logsum = attend(
                qkv[f, :, at : at + WIDE],
                qkv[f, :, width + at : width + at + WIDE],
                qkv[f, :, 2 * width + at : 2 * width + at + WIDE],
                None,
            )
            mixed[f, :, at : at + WIDE] = out
            logsum_out[f, g : g + 1] = logsum
        sent[f] = (x + dot(mixed[f], std_out[0], NT)).astype(BF)
        m, at_frame = f // frames, lax.rem(f, frames)
        for r in range(n_z):
            src = sent.at[f, pl.ds(pl.multiple_of((my_z ^ r) * chunk, 16), chunk)]
            dst = time_in.at[m, r, at_frame]
            if r == 0:
                pltpu.make_async_copy(src, dst, t_send.at[m, 0]).start()
            else:
                pltpu.make_async_remote_copy(
                    src_ref=src, dst_ref=dst, send_sem=t_send.at[m, r],
                    recv_sem=t_recv.at[m, r], device_id=to_z[r], device_id_type=MESH,
                ).start()
        return carry

    lax.fori_loop(0, micros * frames, frame, 0)
    kept = [here(xs, xs_out), here(qkv, qkv_out), here(mixed, mixed_out)]
    gather_last(1)
    arrive(by_core[1])
    standard(1)
    weights_out += [here(std_qkv.at[1], qkv_b), here(std_out.at[1], out_b)]
    for j in (2, 3):
        by_x[j].wait_recv()
        by_y2[j].wait_recv()
    for m in range(micros):
        own_cot[m].wait()
        arrive(cot_in[m])
    for m in range(micros):
        for r in range(n_z):
            src = sent.at[
                pl.ds(m * frames, frames), pl.ds(pl.multiple_of((my_z ^ r) * chunk, 16), chunk)
            ]
            dst = time_in.at[m, r]
            if r == 0:
                pltpu.make_async_copy(src, dst, t_send.at[m, 0]).wait()
            else:
                pltpu.make_async_remote_copy(
                    src_ref=src, dst_ref=dst, send_sem=t_send.at[m, r],
                    recv_sem=t_recv.at[m, r], device_id=to_z[r], device_id_type=MESH,
                ).wait()
    for copy in remote.all:
        copy.wait_send()
    for copy in kept + weights_out:
        copy.wait()


def front(inputs, cot, shard, ln_shard):
    micros, clips, frames, part, width = inputs.shape
    n_tp, n_z = lax.axis_size("tp"), lax.axis_size("fp")
    places = part * n_tp
    total = micros * frames
    chunk = places // n_z
    cols = shard.shape[2]
    groups = width // WIDE
    any_spec = pl.BlockSpec(memory_space=pl.ANY)
    vmem = pl.BlockSpec(memory_space=pltpu.VMEM)
    dma = pltpu.SemaphoreType.DMA
    shape = jax.ShapeDtypeStruct
    weights = [(width, 3 * width), (width, width)] * 2 + [(n_tp, width, cols)] * 2
    return pl.pallas_call(
        front_kernel,
        in_specs=[any_spec] * 4,
        out_specs=[any_spec] * 6 + [vmem] + [any_spec] * 6 + [vmem],
        out_shape=[
            shape((total, places, width), BF),
            shape((micros, n_z, frames, chunk, width), BF),
            shape((frames, places, width), BF),
            shape((frames, places, width), BF),
            shape((total, places, 3 * width), BF),
            shape((total, places, width), BF),
            shape((total, groups, GROUP * places), F32),
        ]
        + [shape(dims, BF) for dims in weights]
        + [shape((8, width), F32)],
        scratch_shapes=[
            pltpu.VMEM((total, places, width), BF),
            pltpu.VMEM((total, places, width), BF),
            pltpu.VMEM((2, n_tp, width, cols), BF),
            pltpu.VMEM((2, width, 3 * width), BF),
            pltpu.VMEM((2, width, width), BF),
            pltpu.VMEM((width, ln_shard.shape[1]), BF),
            pltpu.VMEM((total, places, 3 * width), BF),
            pltpu.VMEM((total, places, width), BF),
            dma((N_REMOTE,)),
            dma((N_REMOTE,)),
            dma((micros, n_z)),
            dma((micros, n_z)),
            dma((N_LOCAL,)),
        ],
        compiler_params=pltpu.CompilerParams(
            vmem_limit_bytes=60 * MIB, collective_id=3, has_side_effects=True
        ),
        cost_estimate=pl.CostEstimate(
            flops=2 * total * places * width * 5 * width,
            bytes_accessed=total * places * width * 16,
            transcendentals=0,
        ),
    )(inputs, cot, shard, ln_shard)


def to_peer(value, axis, step):
    n = lax.axis_size(axis)
    return lax.ppermute(value, axis, [(i, i ^ step) for i in range(n)])


def swap(pieces, axis):
    return [piece if s == 0 else to_peer(piece, axis, s) for s, piece in enumerate(pieces)]


def pick(stack, index):
    return lax.dynamic_index_in_dim(stack, index, 0, keepdims=False)


def shards(
    inputs, cotangent, qkv_weight, out_spatial, out_temporal, mlp_in, mlp_out, ln_gain, ln_bias
):
    micros, clips, frames, local, width = inputs.shape
    n_tp, n_fp = lax.axis_size("tp"), lax.axis_size("fp")
    n_cf = lax.axis_size("clip") * n_fp
    assert clips == n_tp
    my_tp, my_fp = lax.axis_index("tp"), lax.axis_index("fp")
    depth = qkv_weight.shape[2]
    span = qkv_weight.shape[3]
    places = n_tp * local
    chunk = places // n_fp
    at = my_fp.astype(jnp.int32)[None]

    first = jnp.concatenate([qkv_weight[0, i] for i in range(3)] + [out_spatial.T], axis=1)
    second = jnp.concatenate([qkv_weight[1, i] for i in range(3)] + [out_temporal.T], axis=1)
    axes = ("clip", "fp", "tp")
    ln_rows = [v[i] for i in range(3) for v in (ln_gain, ln_bias)]
    whole_rows = depth % 16 == 0 and n_tp == 4 and lax.axis_size("clip") == 2 and micros == 2
    whole_rows = whole_rows and frames * places == width and span * 4 == width

    def from_chunks(chunks):
        stack = jnp.stack(chunks)
        joined = jnp.concatenate([pick(stack, my_fp ^ c) for c in range(n_fp)], axis=1)
        return [joined[:, s * local : (s + 1) * local] for s in range(n_tp)]

    def outward(pieces):
        stack = jnp.stack(swap(pieces, "tp"))
        return jnp.stack([pick(stack, my_tp ^ c) for c in range(n_tp)])

    mine = lax.axis_index("clip") * n_fp + my_fp
    kinds = lambda v: [v[:, i * span : (i + 1) * span] for i in range(4)]

    def arranged(acts, grad_input, late, space, norm_grads):
        norm_grads = norm_grads[:6].reshape(3, 2, n_cf, depth)
        norm_grads = lax.dynamic_index_in_dim(norm_grads, mine, 2, keepdims=False)
        space_g, time_g = kinds(space), kinds(late[2])
        return (
            acts,
            grad_input,
            jnp.stack([jnp.stack(space_g[:3]), jnp.stack(time_g[:3])]),
            space_g[3].T,
            time_g[3].T,
            late[0],
            late[1].T,
            norm_grads[:, 0],
            norm_grads[:, 1],
        )

    if whole_rows:
        ln_shard = jnp.stack(ln_rows + [jnp.zeros_like(ln_rows[0])] * 122, axis=1)
        shard = jnp.stack([first, second, mlp_in, mlp_out.T])
        (
            xs, time_pieces, cot_half, cot_late, qkv, mixed, logsum,
            qkv_space_w, out_space_w, qkv_time_w, out_time_w, in_w, unit_w, norms,
        ) = front(inputs, cotangent, shard, ln_shard)
        results, grads, _, *kept, tail = time_layer(
            [time_pieces], [cot_half, cot_late], qkv_time_w, out_time_w, in_w, unit_w, norms
        )
        sums, norm_grads, acts, input_grad, *_ = back(
            results, grads, xs, qkv, mixed, logsum, qkv_space_w, out_space_w, norms, tail, kept
        )
        return arranged(acts, input_grad.astype(F32), sums, sums[3], norm_grads)

    def gathered(part):
        return lax.all_gather(part, axes).reshape(n_cf, n_tp, depth, part.shape[1])

    def attention_weights(raw):
        raw = raw.reshape(n_cf, n_tp, depth, 4, span).transpose(3, 0, 2, 1, 4)
        raw = raw.reshape(4, n_cf * depth, n_tp * span)
        return jnp.concatenate([raw[0], raw[1], raw[2]], axis=1), raw[3]

    def unit_weights(raw):
        return raw.transpose(1, 0, 2, 3).reshape(n_tp, n_cf * depth, raw.shape[3])

    norms = lax.all_gather(jnp.stack(ln_rows), ("clip", "fp"))
    norms = norms.transpose(1, 0, 2).reshape(6, n_cf * depth).astype(F32)
    qkv_space_w, out_space_w = attention_weights(gathered(first))
    rest = gathered(jnp.concatenate([second, mlp_in, mlp_out.T], axis=1))
    qkv_time_w, out_time_w = attention_weights(rest[..., : 4 * span])
    in_w = unit_weights(rest[..., 4 * span : 4 * span + mlp_in.shape[1]])
    unit_w = unit_weights(rest[..., 4 * span + mlp_in.shape[1] :])

    def inward(array, m):
        return swap([pick(array[m], my_tp ^ s) for s in range(n_tp)], "tp")

    def to_chunks(pieces):
        joined = jnp.concatenate(pieces, axis=1)
        return [
            lax.dynamic_slice_in_dim(joined, (my_fp ^ r) * chunk, chunk, 1)
            for r in range(n_fp)
        ]

    space_kept, time_given = [], []
    for m in range(micros):
        x = inward(inputs, m)
        cots = swap(to_chunks(inward(cotangent, m)), "fp")
        out = space_forward(x, qkv_space_w, out_space_w, norms, at, n_fp)
        time_given.append((swap(out[:n_fp], "fp"), cots))
        space_kept.append((x,) + tuple(out[n_fp:]) + (0,))
    time_kept = []
    results = []
    space_grads = []
    for m in range(micros):
        pieces, cots = time_given[m]
        out = time_layer(pieces, cots, qkv_time_w, out_time_w, in_w, unit_w, norms)
        results.append(outward(from_chunks(swap(out[:n_fp], "fp"))))
        space_grads.append(swap(out[n_fp : 2 * n_fp], "fp"))
        time_kept.append(out[2 * n_fp :])
    space_rows = []
    input_grads = []
    flat = lambda v: v.reshape(-1, v.shape[-1])
    kept = lambda i: [k[i] for k in time_kept]
    time_chunks = [
        ([kept(3)], kept(4), True),
        ([kept(6)], kept(5), False),
        ([kept(0), kept(2)], kept(1), True),
    ]
    for m in range(micros):
        x, qkv, mixed, logsum, skip = space_kept[m]
        out = space_backward(
            x, space_grads[m], qkv, mixed, logsum, qkv_space_w, out_space_w, norms, at, skip, n_tp
        )
        input_grads.append(outward(out[:n_tp]).astype(F32))
        normed, low, columns, norm_grad = out[n_tp:]
        space_rows.append((flat(normed), flat(low), flat(columns), norm_grad))
    rows = lambda i: [k[i] for k in space_rows]
    space_chunk = ([rows(0), rows(1)], rows(2), True)
    early = scatter_grads([space_chunk], n_cf, n_tp)
    late = scatter_grads(time_chunks, n_cf, n_tp)
    norm_grads = lax.psum(jnp.concatenate([sum(rows(3)), sum(kept(7))]), axes)
    return arranged(jnp.stack(results), jnp.stack(input_grads), late, early[0], norm_grads)


def scatter_grads(chunks, n_cf, n_tp):
    tiles = []
    for lefts, rights, _ in chunks:
        cols = rights[0].shape[1] // n_tp
        total = sum(dot(a, b, TN) for a, b in zip(lefts[0], rights))
        total = total.reshape(total.shape[0], n_tp, cols)
        if len(lefts) == 2:
            other = sum(dot(a, b, TN) for a, b in zip(lefts[1], rights))
            other = other.reshape(other.shape[0], n_tp, cols)
            at = 3 * cols // 4
            total = jnp.concatenate([total[..., :at], other[..., at:]], axis=2)
        total = total.reshape(n_cf, total.shape[0] // n_cf, n_tp, cols).transpose(0, 2, 1, 3)
        tiles.append(total.reshape((n_cf * n_tp,) + total.shape[2:]))
    return lax.psum_scatter(jnp.stack(tiles, 1), ("clip", "fp", "tp"), scatter_dimension=0)


def solution(mesh):
    spread = P(None, "clip", "fp", "tp", None)
    return jax.shard_map(
        shards,
        mesh=mesh,
        in_specs=(
            spread,
            spread,
            P(None, None, ("clip", "fp"), "tp"),
            P("tp", ("clip", "fp")),
            P("tp", ("clip", "fp")),
            P(("clip", "fp"), "tp"),
            P("tp", ("clip", "fp")),
            P(None, ("clip", "fp")),
            P(None, ("clip", "fp")),
        ),
        out_specs=(
            spread,
            spread,
            P(None, None, ("clip", "fp"), "tp"),
            P("tp", ("clip", "fp")),
            P("tp", ("clip", "fp")),
            P(("clip", "fp"), "tp"),
            P("tp", ("clip", "fp")),
            P(None, ("clip", "fp")),
            P(None, ("clip", "fp")),
        ),
        check_vma=False,
    )
```

```python
from functools import partial

import jax
import jax.numpy as jnp
from jax import lax
from jax.experimental import pallas as pl
from jax.experimental.pallas import tpu as pltpu
from jax.sharding import PartitionSpec as P

HD = 64
GROUP = 4
WIDE = GROUP * HD
EPS = 1e-06
BF = jnp.bfloat16
F32 = jnp.float32
MIB = 1024 * 1024
MESH = pl.DeviceIdType.MESH

NN = (((1,), (0,)), ((), ()))
NT = (((1,), (1,)), ((), ()))
TN = (((0,), (0,)), ((), ()))


def dot(a, b, dims):
    return lax.dot_general(a, b, dims, preferred_element_type=F32)


def normalise(values):
    centre = values - jnp.mean(values, axis=-1, keepdims=True)
    spread = jnp.mean(centre * centre, axis=-1, keepdims=True)
    rate = lax.rsqrt(spread + EPS)
    return centre * rate, rate


def norm_back(upstream, gain, unit, rate):
    weighted = upstream * gain
    inner = jnp.mean(weighted * unit, axis=-1, keepdims=True)
    return rate * (weighted - jnp.mean(weighted, axis=-1, keepdims=True) - unit * inner)


def head_masks(scale):
    lanes = lax.broadcasted_iota(jnp.int32, (1, WIDE), 1) // HD
    return [jnp.where(lanes == h, scale, 0.0).astype(BF) for h in range(GROUP)]


def spread_heads(block, masks):
    return jnp.concatenate([block * mask for mask in masks], axis=0)


def gather_heads(stacked, rows):
    lanes = lax.broadcasted_iota(jnp.int32, (1, WIDE), 1) // HD
    total = stacked[:rows]
    for h in range(1, GROUP):
        total = jnp.where(lanes == h, stacked[h * rows : (h + 1) * rows], total)
    return total


def attend(queries, keys, values, bias):
    rows = queries.shape[0]
    scores = dot(keys, spread_heads(queries, head_masks(HD**-0.5)), NT)
    if bias is not None:
        scores = scores + bias
    top = jnp.max(scores, axis=0, keepdims=True)
    exponent = jnp.exp(scores - top)
    totals = jnp.sum(exponent, axis=0, keepdims=True)
    weights = (exponent * (1.0 / totals)).astype(BF)
    mixed = gather_heads(dot(weights, values, TN), rows).astype(BF)
    return mixed, top + jnp.log(totals)


def attend_back(queries, keys, values, upstream, logsum, bias):
    rows = queries.shape[0]
    spread_q = spread_heads(queries, head_masks(HD**-0.5))
    spread_g = spread_heads(upstream, head_masks(1.0))
    scores = dot(keys, spread_q, NT)
    if bias is not None:
        scores = scores + bias
    probs = jnp.exp(scores - logsum)
    grad_probs = dot(values, spread_g, NT)
    inner = jnp.sum(probs * grad_probs, axis=0, keepdims=True)
    grad_scores = (probs * (grad_probs - inner)).astype(BF)
    grad_values = dot(probs.astype(BF), spread_g, NN)
    grad_keys = dot(grad_scores, spread_q, NN)
    grad_queries = gather_heads(dot(grad_scores, keys, TN), rows) * HD**-0.5
    return grad_queries.astype(BF), grad_keys.astype(BF), grad_values.astype(BF)


def gelu_parts(pre):
    size = jnp.abs(pre) * (0.5**0.5)
    t = 1.0 / (1.0 + 0.3275911 * size)
    bell = jnp.exp(-size * size)
    poly = t * (
        0.254829592
        + t * (-0.284496736 + t * (1.421413741 + t * (-1.453152027 + t * 1.061405429)))
    )
    tail = 0.5 * poly * bell
    return jnp.where(pre >= 0, 1.0 - tail, tail), bell * 0.3989422804014327


def space_forward_kernel(n_in, n_out, at_ref, *refs):
    pieces = refs[:n_in]
    qkv_w, out_w, norm = refs[n_in : n_in + 3]
    outs = refs[n_in + 3 : n_in + 3 + n_out]
    qkv_out, mixed_out, logsum_out, held = refs[n_in + 3 + n_out :]
    width = out_w.shape[1]
    x = jnp.concatenate([piece[0] for piece in pieces], axis=0).astype(F32)
    unit, _ = normalise(x)
    normed = (unit * norm[0:1] + norm[1:2]).astype(BF)
    qkv_out[0] = dot(normed, qkv_w[...], NN).astype(BF)
    for g in range(width // WIDE):
        at = g * WIDE
        mixed, logsum = attend(
            qkv_out[0, :, at : at + WIDE],
            qkv_out[0, :, width + at : width + at + WIDE],
            qkv_out[0, :, 2 * width + at : 2 * width + at + WIDE],
            None,
        )
        mixed_out[0, :, at : at + WIDE] = mixed
        logsum_out[0, g : g + 1] = logsum
    held[...] = x + dot(mixed_out[0], out_w[...], NT)
    rows = outs[0].shape[1]
    for r, out in enumerate(outs):
        start = pl.multiple_of((at_ref[0] ^ r) * rows, 8)
        out[0] = held[pl.ds(start, rows), :].astype(BF)


def space_forward(pieces, qkv_w, out_w, norm, at, n_out):
    frames, rows, width = pieces[0].shape
    places = rows * len(pieces)
    groups = width // WIDE
    whole = pl.BlockSpec(memory_space=pltpu.VMEM)
    frame = lambda *dims: pl.BlockSpec((1,) + dims, lambda f, at: (f,) + (0,) * len(dims))
    return pl.pallas_call(
        partial(space_forward_kernel, len(pieces), n_out),
        grid_spec=pltpu.PrefetchScalarGridSpec(
            num_scalar_prefetch=1,
            grid=(frames,),
            in_specs=[frame(rows, width)] * len(pieces) + [whole] * 3,
            out_specs=[frame(places // n_out, width)] * n_out
            + [frame(places, 3 * width), frame(places, width), frame(groups, GROUP * places)],
            scratch_shapes=[pltpu.VMEM((places, width), F32)],
        ),
        out_shape=[jax.ShapeDtypeStruct((frames, places // n_out, width), BF)] * n_out
        + [
            jax.ShapeDtypeStruct((frames, places, 3 * width), BF),
            jax.ShapeDtypeStruct((frames, places, width), BF),
            jax.ShapeDtypeStruct((frames, groups, GROUP * places), F32),
        ],
        compiler_params=pltpu.CompilerParams(vmem_limit_bytes=48 * MIB),
        cost_estimate=pl.CostEstimate(
            flops=2 * frames * places * width * 5 * width,
            bytes_accessed=frames * places * width * 16,
            transcendentals=0,
        ),
    )(at, *pieces, qkv_w, out_w, norm)


def store_columns(out, kinds, n_parts):
    width = kinds[0].shape[1]
    span = width // n_parts
    for t in range(n_parts):
        for i, kind in enumerate(kinds):
            start = (t * len(kinds) + i) * span
            out[:, start : start + span] = kind[:, t * span : (t + 1) * span]


def space_backward_kernel(n_in, n_grad, n_out, at_ref, *refs):
    pieces = refs[:n_in]
    grads = refs[n_in : n_in + n_grad]
    qkv_in, mixed_in, logsum_in, qkv_w, out_w, norm = refs[n_in + n_grad : n_in + n_grad + 6]
    rest = refs[n_in + n_grad + 6 :]
    outs = rest[:n_out]
    normed_out, grad_out, columns, norm_out, held, dqkv = rest[n_out:]
    width = out_w.shape[1]
    rows = grads[0].shape[1]
    for r, grad in enumerate(grads):
        start = pl.multiple_of((at_ref[0] ^ r) * rows, 8)
        held[pl.ds(start, rows), :] = grad[0].astype(F32)
    x = jnp.concatenate([piece[0] for piece in pieces], axis=0).astype(F32)
    unit, rate = normalise(x)
    normed_out[0] = (unit * norm[0:1] + norm[1:2]).astype(BF)
    low = held[...].astype(BF)
    grad_out[0] = low
    grad_mixed = dot(low, out_w[...], NN).astype(BF)
    for g in range(width // WIDE):
        at = g * WIDE
        parts = attend_back(
            qkv_in[0, :, at : at + WIDE],
            qkv_in[0, :, width + at : width + at + WIDE],
            qkv_in[0, :, 2 * width + at : 2 * width + at + WIDE],
            grad_mixed[:, at : at + WIDE],
            logsum_in[0, g : g + 1],
            None,
        )
        for i, part in enumerate(parts):
            dqkv[:, i * width + at : i * width + at + WIDE] = part
    store_columns(
        columns.at[0],
        [dqkv[:, i * width : (i + 1) * width] for i in range(3)] + [mixed_in[0]],
        n_out,
    )
    grad_normed = dot(dqkv[...], qkv_w[...], NT)

    @pl.when(pl.program_id(0) == 0)
    def _():
        norm_out[...] = jnp.zeros_like(norm_out)

    norm_out[0:1] += jnp.sum(grad_normed * unit, axis=0, keepdims=True)
    norm_out[1:2] += jnp.sum(grad_normed, axis=0, keepdims=True)
    total = held[...] + norm_back(grad_normed, norm[0:1], unit, rate)
    rows = outs[0].shape[1]
    for s, out in enumerate(outs):
        out[0] = total[s * rows : (s + 1) * rows].astype(BF)


def space_backward(pieces, grads, qkv, mixed, logsum, qkv_w, out_w, norm, at, first, n_out):
    frames, width = grads[0].shape[0], grads[0].shape[2]
    places = grads[0].shape[1] * len(grads)
    rows = places // n_out
    groups = width // WIDE
    n_grad = len(grads)
    whole = pl.BlockSpec(memory_space=pltpu.VMEM)
    frame = lambda *dims: pl.BlockSpec((1,) + dims, lambda f, at: (f,) + (0,) * len(dims))
    later = lambda *dims: pl.BlockSpec((1,) + dims, lambda f, at: (f + first,) + (0,) * len(dims))
    return pl.pallas_call(
        partial(space_backward_kernel, len(pieces), n_grad, n_out),
        grid_spec=pltpu.PrefetchScalarGridSpec(
            num_scalar_prefetch=1,
            grid=(frames,),
            in_specs=[later(places // len(pieces), width)] * len(pieces)
            + [frame(places // n_grad, width)] * n_grad
            + [later(places, 3 * width), later(places, width), later(groups, GROUP * places)]
            + [whole] * 3,
            out_specs=[frame(rows, width)] * n_out
            + [frame(places, width), frame(places, width), frame(places, 4 * width)]
            + [pl.BlockSpec((2, width), lambda f, at: (0, 0))],
            scratch_shapes=[
                pltpu.VMEM((places, width), F32),
                pltpu.VMEM((places, 3 * width), BF),
            ],
        ),
        out_shape=[jax.ShapeDtypeStruct((frames, rows, width), BF)] * n_out
        + [
            jax.ShapeDtypeStruct((frames, places, width), BF),
            jax.ShapeDtypeStruct((frames, places, width), BF),
            jax.ShapeDtypeStruct((frames, places, 4 * width), BF),
            jax.ShapeDtypeStruct((2, width), F32),
        ],
        compiler_params=pltpu.CompilerParams(vmem_limit_bytes=48 * MIB),
        cost_estimate=pl.CostEstimate(
            flops=2 * frames * places * width * 7 * width,
            bytes_accessed=frames * places * width * 24,
            transcendentals=0,
        ),
    )(at, *pieces, *grads, qkv, mixed, logsum, qkv_w, out_w, norm)


def time_kernel(joint, n_in, n_parts, sub, *refs):
    n_arrays = 1 if joint else n_in
    n_cots = 2 if joint else n_in
    n_moved = 2 if joint else n_in
    pieces = refs[:n_arrays]
    cots = refs[n_arrays : n_arrays + n_cots]
    qkv_w, out_w, in_w, unit_w, norm = refs[n_arrays + n_cots : n_arrays + n_cots + 5]
    rest = refs[n_arrays + n_cots + 5 :]
    results = rest[:n_arrays]
    grads = rest[n_arrays : n_arrays + n_moved]
    rest = rest[n_arrays + n_moved :]
    (
        normed_time,
        columns,
        grad_time,
        normed_mlp,
        grad_pre,
        hidden,
        grad_result,
        norm_out,
        qkv_all,
        dqkv,
        mixed_all,
        logsum_all,
        after_all,
    ) = rest[:13]
    if joint:
        (
            outgoing, cot_in, in_held, unit_held, send, recv, c_send, c_recv, cot_sem,
            g_send, g_recv, w_sem,
        ) = rest[13:]
        late = grads[1]
        my_tp, my_y, my_z = lax.axis_index("tp"), lax.axis_index("clip"), lax.axis_index("fp")
        to_z = [{"fp": my_z ^ r} for r in range(n_in)]
        to_core, to_x, to_y = {"tp": my_tp ^ 1}, {"tp": my_tp ^ 2}, {"clip": my_y ^ 1}
        block = results[0].shape[-2]
        chunk = late.shape[3]
        each = chunk // block
        steps = pl.num_programs(0)
        count = steps // 2
        step = pl.program_id(0)
        at_block = lax.rem(step, count)
        slot = lax.rem(at_block, 2)
        half, cols = in_w.shape[1] // 2, in_w.shape[2]
        near = pl.ds(pl.multiple_of(my_y * half, 16), half)
        far = pl.ds(pl.multiple_of((1 - my_y) * half, 16), half)
        one, two = pl.ds(0, cols // 2), pl.ds(cols // 2, cols // 2)
        away = my_tp ^ 2
        ways = [(in_w, in_held), (unit_w, unit_held)]

        def gather(j, i):
            given, held = ways[j]
            src, at, peer = [
                (given, (my_tp, near, one), to_y),
                (given, (away, near, one), to_y),
                (given, (my_tp, slice(None), two), to_x),
                (given, (my_tp, near), to_core),
                (given, (away, near, one), to_core),
                (given, (my_tp, far, two), to_core),
                (held, (my_tp, far, one), to_core),
                (held, (away, far, one), to_core),
                (held, (away, slice(None), two), to_core),
            ][i]
            return pltpu.make_async_remote_copy(
                src_ref=src.at[at], dst_ref=held.at[at], send_sem=g_send.at[j, i],
                recv_sem=g_recv.at[j, i], device_id=peer, device_id_type=MESH,
            )

        def own_parts(j):
            given, held = ways[j]
            return [
                pltpu.make_async_copy(given.at[at], held.at[at], w_sem.at[j, i])
                for i, at in enumerate([(my_tp, near), (my_tp, far, two), (away, near, one)])
            ]

        def late_copy(m, r):
            src = cots[m].at[:, pl.ds(pl.multiple_of((my_z ^ r) * chunk, 16), chunk)]
            if r == 0:
                return pltpu.make_async_copy(src, late.at[m, 0], c_send.at[m, 0])
            return pltpu.make_async_remote_copy(
                src_ref=src, dst_ref=late.at[m, r], send_sem=c_send.at[m, r],
                recv_sem=c_recv.at[m, r], device_id=to_z[r], device_id_type=MESH,
            )

        def cot_fetch(at, slot):
            m, rows = at // each, pl.ds(pl.multiple_of(lax.rem(at, each) * block, 8), block)
            return pltpu.make_async_copy(
                late.at[m, :, :, rows], cot_in.at[slot], cot_sem.at[slot]
            )

        @pl.when(step == 0)
        def _():
            peers = to_z[1:] + [to_core, to_x, to_y]
            barrier = pltpu.get_barrier_semaphore()
            for peer in peers:
                pl.semaphore_signal(barrier, inc=1, device_id=peer, device_id_type=MESH)
            for j in range(2):
                start_all(own_parts(j))
            pl.semaphore_wait(barrier, len(peers))
            start_all([gather(0, i) for i in range(6)])
            start_all([late_copy(0, r) for r in range(n_in)])

        @pl.when(step == 1)
        def _():
            start_all([gather(1, i) for i in range(6)])

        for j in range(2):

            @pl.when(step == count - 3 + 2 * j)
            def _(j=j):
                for i in range(3):
                    gather(j, i).wait_recv()
                start_all([gather(j, i) for i in range(6, 9)])

        @pl.when(step == count - 1)
        def _():
            start_all([late_copy(1, r) for r in range(n_in)])

        @pl.when(step == count)
        def _():
            for j in range(2):
                for copy in own_parts(j):
                    copy.wait()
                for i in range(3, 9):
                    gather(j, i).wait_recv()

        for m in range(2):

            @pl.when(step == count + m * each)
            def _(m=m):
                late_copy(m, 0).wait()
                for r in range(1, n_in):
                    late_copy(m, r).wait_recv()
                cot_fetch(m * each, slot).start()

        @pl.when(
            jnp.logical_and(
                step >= count,
                jnp.logical_and(lax.rem(at_block + 1, each) != 0, at_block + 1 < count),
            )
        )
        def _():
            cot_fetch(at_block + 1, 1 - slot).start()

    else:
        at_block = 0

    width = out_w.shape[1]
    frames, places = results[0].shape[-3:-1]
    all_frames = frames * n_in
    rows = all_frames * sub
    parts = places // sub

    def tokens(blocks):
        blocks = [b[...].reshape(-1, places, width) for b in blocks]
        joined = jnp.concatenate(blocks, axis=0).astype(F32)
        return jnp.concatenate(
            [joined[:, j * sub : (j + 1) * sub, :].reshape(rows, width) for j in range(parts)],
            axis=0,
        )

    def scatter(values, outs):
        grid = jnp.concatenate(
            [
                values[j * rows : (j + 1) * rows].reshape(all_frames, sub, width)
                for j in range(parts)
            ],
            axis=1,
        ).astype(BF)
        if len(outs) == 1:
            outs[0][...] = grid.reshape(outs[0].shape)
        else:
            for r, out in enumerate(outs):
                out[...] = grid[r * frames : (r + 1) * frames]

    key_place = lax.broadcasted_iota(jnp.int32, (rows, GROUP * rows), 0) % sub
    query_place = lax.broadcasted_iota(jnp.int32, (rows, GROUP * rows), 1) % sub
    bias = jnp.where(key_place == query_place, 0.0, -1e30)

    groups = width // WIDE
    qkv, mixed = qkv_all.at[at_block], mixed_all.at[at_block]
    probs_logsum, after = logsum_all.at[at_block], after_all.at[at_block]

    def forward():
        after_space = tokens(pieces)
        unit, _ = normalise(after_space)
        normed = (unit * norm[2:3] + norm[3:4]).astype(BF)
        qkv[...] = dot(normed, qkv_w[...], NN).astype(BF)
        for j in range(parts):
            at_rows = slice(j * rows, (j + 1) * rows)
            for g in range(groups):
                at = g * WIDE
                out, logsum = attend(
                    qkv[at_rows, at : at + WIDE],
                    qkv[at_rows, width + at : width + at + WIDE],
                    qkv[at_rows, 2 * width + at : 2 * width + at + WIDE],
                    bias,
                )
                mixed[at_rows, at : at + WIDE] = out
                probs_logsum[j * groups + g : j * groups + g + 1] = logsum
        after[...] = after_space + dot(mixed[...], out_w[...], NT)

    def backward():
        time_backward(after[...])

    def time_backward(after_time):
        after_space = tokens(pieces)
        unit, rate = normalise(after_space)
        normed_time[...] = (unit * norm[2:3] + norm[3:4]).astype(BF)
        unit2, rate2 = normalise(after_time)
        normed_mlp[...] = (unit2 * norm[4:5] + norm[5:6]).astype(BF)
        if joint:
            cot_fetch(at_block, slot).wait()
        cot = tokens([cot_in.at[slot]] if joint else cots)
        w_in, w_unit = (in_held, unit_held) if joint else (in_w, unit_w)
        grad_result[...] = cot.astype(BF)
        result = after_time
        grad_normed = None
        for c in range(in_w.shape[0]):
            cols = slice(c * in_w.shape[2], (c + 1) * in_w.shape[2])
            pre = dot(normed_mlp[...], w_in[c], NN)
            below, density = gelu_parts(pre)
            hidden[:, cols] = (pre * below).astype(BF)
            result = result + dot(hidden[:, cols], w_unit[c], NT)
            grad_hidden = dot(grad_result[...], w_unit[c], NN)
            grad_pre[:, cols] = (grad_hidden * (below + pre * density)).astype(BF)
            term = dot(grad_pre[:, cols], w_in[c], NT)
            grad_normed = term if c == 0 else grad_normed + term
        scatter(result, results)

        @pl.when(at_block == 0 if joint else pl.program_id(0) == 0)
        def _():
            norm_out[...] = jnp.zeros_like(norm_out)

        norm_out[2:3] += jnp.sum(grad_normed * unit2, axis=0, keepdims=True)
        norm_out[3:4] += jnp.sum(grad_normed, axis=0, keepdims=True)
        grad_after = cot + norm_back(grad_normed, norm[4:5], unit2, rate2)
        grad_time[...] = grad_after.astype(BF)
        grad_mixed = dot(grad_time[...], out_w[...], NN).astype(BF)
        for j in range(parts):
            at_rows = slice(j * rows, (j + 1) * rows)
            for g in range(groups):
                at = g * WIDE
                back = attend_back(
                    qkv[at_rows, at : at + WIDE],
                    qkv[at_rows, width + at : width + at + WIDE],
                    qkv[at_rows, 2 * width + at : 2 * width + at + WIDE],
                    grad_mixed[at_rows, at : at + WIDE],
                    probs_logsum[j * groups + g : j * groups + g + 1],
                    bias,
                )
                for i, part in enumerate(back):
                    dqkv[at_rows, i * width + at : i * width + at + WIDE] = part
        store_columns(
            columns,
            [dqkv[:, i * width : (i + 1) * width] for i in range(3)] + [mixed[...]],
            n_parts,
        )
        grad_normed = dot(dqkv[...], qkv_w[...], NT)
        norm_out[0:1] += jnp.sum(grad_normed * unit, axis=0, keepdims=True)
        norm_out[1:2] += jnp.sum(grad_normed, axis=0, keepdims=True)
        grad_space = grad_after + norm_back(grad_normed, norm[2:3], unit, rate)
        if not joint:
            scatter(grad_space, grads)
            return
        scatter(grad_space, [outgoing.at[at_block]])
        received = grads[0]
        micros = received.shape[0]
        m, at = at_block // each, pl.multiple_of(lax.rem(at_block, each) * places, 8)
        for r in range(n_in):
            src, dst = outgoing.at[at_block, r], received.at[m, r, :, pl.ds(at, places)]
            if r == 0:
                pltpu.make_async_copy(src, dst, send.at[m, 0]).start()
            else:
                pltpu.make_async_remote_copy(
                    src_ref=src, dst_ref=dst, send_sem=send.at[m, r], recv_sem=recv.at[m, r],
                    device_id=to_z[r], device_id_type=MESH,
                ).start()

        @pl.when(step == steps - 1)
        def _():
            for j in range(2):
                for i in range(9):
                    gather(j, i).wait_send()
            for m in range(micros):
                for r in range(1, n_in):
                    late_copy(m, r).wait_send()
            for m in range(micros):
                for r in range(n_in):
                    src = outgoing.at[pl.ds(m * each, each), r]
                    dst = received.at[m, r]
                    if r == 0:
                        pltpu.make_async_copy(dst, dst, send.at[m, 0]).wait()
                    else:
                        for ref, wait in ((src, "wait_send"), (dst, "wait_recv")):
                            copy = pltpu.make_async_remote_copy(
                                src_ref=ref, dst_ref=ref, send_sem=send.at[m, r],
                                recv_sem=recv.at[m, r], device_id=to_z[r], device_id_type=MESH,
                            )
                            getattr(copy, wait)()

    if joint:
        pl.when(step < count)(forward)
        pl.when(step >= count)(backward)
    else:
        forward()
        backward()


def time_layer(pieces, cots, qkv_w, out_w, in_w, unit_w, norm):
    joint = len(pieces) == 1
    frames, places, width = pieces[0].shape[-3:]
    n_in = pieces[0].shape[1] if joint else len(pieces)
    micros = pieces[0].shape[0] if joint else 1
    block = 16 if places % 16 == 0 else 8
    each = places // block
    sub = 8
    tokens = frames * n_in * block
    count = frames * n_in * places * micros
    hidden = in_w.shape[0] * in_w.shape[2]
    whole = pl.BlockSpec(memory_space=pltpu.VMEM)
    if joint:
        blocks_all = micros * each

        def joint_piece(place):
            return pl.BlockSpec(
                (None, n_in, frames, block, width),
                lambda b: (place(b) // each, 0, 0, place(b) % each, 0),
            )

        piece = joint_piece(lambda b: b % blocks_all)
        any_spec = pl.BlockSpec(memory_space=pl.ANY)
        later = lambda b: jnp.maximum(b - blocks_all, 0)
        given = [piece, any_spec, any_spec, whole, whole, any_spec, any_spec, whole]
        moved = [joint_piece(later), any_spec, any_spec]
        row = lambda cols: pl.BlockSpec((tokens, cols), lambda b: (later(b), 0))
    else:
        piece = pl.BlockSpec((frames, block, width), lambda b: (0, b, 0))
        moved = [piece] * (2 * n_in)
        given = moved + [whole] * 5
        row = lambda cols: pl.BlockSpec((tokens, cols), lambda b: (b, 0))
    kept = [width, 4 * width, width, width, hidden, hidden, width]
    dma = pltpu.SemaphoreType.DMA
    n_kept = micros * each if joint else 1
    sending = [
        pltpu.VMEM((micros * each, n_in, frames, block, width), BF),
        pltpu.VMEM((2, n_in, frames, block, width), BF),
        pltpu.VMEM(in_w.shape, BF),
        pltpu.VMEM(unit_w.shape, BF),
        dma((micros, n_in)),
        dma((micros, n_in)),
        dma((micros, n_in)),
        dma((micros, n_in)),
        dma((2,)),
        dma((2, 9)),
        dma((2, 9)),
        dma((2, 3)),
    ]
    sent = [jax.ShapeDtypeStruct(a.shape, BF) for a in pieces + cots]
    if joint:
        sent = [jax.ShapeDtypeStruct(pieces[0].shape, BF)] * 3
    return pl.pallas_call(
        partial(time_kernel, joint, n_in, in_w.shape[0], sub),
        grid=(2 * micros * each if joint else each,),
        in_specs=given,
        out_specs=moved + [row(cols) for cols in kept] + [pl.BlockSpec((4, width), lambda b: (0, 0))],
        out_shape=sent
        + [jax.ShapeDtypeStruct((count, cols), BF) for cols in kept]
        + [jax.ShapeDtypeStruct((4, width), F32)],
        scratch_shapes=[
            pltpu.VMEM((n_kept, tokens, 3 * width), BF),
            pltpu.VMEM((tokens, 3 * width), BF),
            pltpu.VMEM((n_kept, tokens, width), BF),
            pltpu.VMEM((n_kept, 8 * (block // sub), GROUP * frames * n_in * sub), F32),
            pltpu.VMEM((n_kept, tokens, width), F32),
        ]
        + (sending if joint else []),
        compiler_params=pltpu.CompilerParams(
            vmem_limit_bytes=60 * MIB,
            collective_id=4 if joint else None,
            has_side_effects=joint,
        ),
        cost_estimate=pl.CostEstimate(
            flops=2 * count * width * 2 * (4 * width + 2 * hidden),
            bytes_accessed=count * 26000,
            transcendentals=0,
        ),
    )(*pieces, *cots, qkv_w, out_w, in_w, unit_w, norm)


STEP = 192


class Copies:
    def __init__(self, send, recv):
        self.send, self.recv, self.count, self.all = send, recv, 0, []

    def add(self, src, dst, peer):
        copy = pltpu.make_async_remote_copy(
            src_ref=src, dst_ref=dst, send_sem=self.send.at[self.count],
            recv_sem=self.recv.at[self.count], device_id=peer, device_id_type=MESH,
        )
        self.count += 1
        self.all.append(copy)
        return copy


def start_all(copies):
    for copy in copies:
        copy.start()


def arrive(copies):
    for copy in copies:
        copy.wait_recv()


def blocks(count, body):
    lax.fori_loop(
        0, count // STEP, lambda i, _: body(pl.ds(pl.multiple_of(i * STEP, STEP), STEP)), None
    )


def back_kernel(
    results, grads, xs, qkv_in, mixed_in, logsum_in, qkv_w, out_w, norm_in,
    tail_time, rows_c, cols_c, rows_d, cols_d, rows_b, rows_b2, cols_b,
    out, tail_out, acts, input_grad, normed_a, low_a, cols_a, res_half,
    turned, stage, tile_in, sent, got1, held, got2, got3, total, got4,
    w_qkv, w_out, norm, logsum, dqkv, tail_sum, tail_got,
    stage_sem, tile_sem, frame_sem, out_sem, load_sem, send, recv, r_send, r_recv, i_send, i_recv,
):
    my_tp, my_y, my_z = lax.axis_index("tp"), lax.axis_index("clip"), lax.axis_index("fp")
    n_tp, n_z = lax.axis_size("tp"), lax.axis_size("fp")
    core, x = lax.rem(my_tp, 2), my_tp // 2
    micros, _, frames, chunk, width = results.shape
    places = chunk * n_z
    part = places // n_tp
    depth, cols = held.shape[2:]
    half, own = depth // 2, depth // (2 * n_z)
    all_rows = tile_in.shape[1]
    to_tp = [{"tp": my_tp ^ s} for s in range(n_tp)]
    to_core, to_x = to_tp[1], to_tp[2]
    to_y = {"clip": my_y ^ 1}
    to_z = [{"fp": my_z ^ r} for r in range(n_z)]
    peers = to_tp[1:] + to_z[1:] + [to_y]
    barrier = pltpu.get_barrier_semaphore()
    for peer in peers:
        pl.semaphore_signal(barrier, inc=1, device_id=peer, device_id_type=MESH)

    remote = Copies(send, recv)
    lefts = [[rows_c], [rows_d], [rows_b, rows_b2], [normed_a, low_a]]
    rights = [cols_c, cols_d, cols_b, cols_a]
    slots = [[0], [1], [2, 3], [0, 1]]
    place = [0, 1, 2, 0]
    lanes = [
        (0, 0, cols, True),
        (1, 0, cols, True),
        (2, 0, cols, True),
        (3, 0, cols // 2, True),
        (3, cols // 2, cols // 2, False),
    ]
    parts = [(1 - x) * 2 + 1 - core, x * 2 + 1 - core, (1 - x) * 2 + core, x * 2 + core]
    far_rows = pl.ds(pl.multiple_of((1 - my_y) * half, 16), half)
    near_rows = pl.ds(pl.multiple_of(my_y * half, 16), half)
    firsts = [
        [remote.add(sent.at[place[j], p], got1.at[j, p], to_core) for p in (0, 1)]
        for j in range(4)
    ]
    seconds, thirds, fourths = [], [], []
    for j, lo, count, y_first in lanes:
        at = pl.ds(lo, count)
        spot = held.at[place[j]]
        if y_first:
            seconds.append(
                [
                    remote.add(
                        spot.at[p, far_rows, at], got2.at[j, pl.ds(p * half, half), at], to_y
                    )
                    for p in (0, 1)
                ]
            )
            thirds.append(remote.add(spot.at[0, near_rows, at], got3.at[j, :, at], to_x))
        else:
            seconds.append([remote.add(spot.at[0, :, at], got2.at[j, :, at], to_x)])
            thirds.append(remote.add(spot.at[1, far_rows, at], got3.at[j, :, at], to_y))
        fourths.append(
            [
                remote.add(
                    total.at[j, pl.ds(pl.multiple_of((my_z ^ r) * own, 16), own), at],
                    got4.at[j, r - 1, :, at],
                    to_z[r],
                )
                for r in range(1, n_z)
            ]
        )
    tails = [
        remote.add(tail_sum.at[min(step, 3)], tail_got.at[step], peer)
        for step, peer in enumerate([to_core, to_y, to_x] + to_z[1:])
    ]
    res_z = [
        [
            remote.add(
                results.at[m, r],
                res_half.at[m, :, pl.ds(pl.multiple_of(my_z * chunk, 16), chunk)],
                to_z[r],
            )
            for r in range(1, n_z)
        ]
        for m in range(micros)
    ]
    res_tp = [
        [
            remote.add(
                res_half.at[m, :, pl.ds(s * part, part)], acts.at[m, my_tp], to_tp[s]
            )
            for s in range(1, n_tp)
        ]
        for m in range(micros)
    ]

    loads = [
        pltpu.make_async_copy(src, dst, load_sem.at[i])
        for i, (src, dst) in enumerate(
            [(qkv_w, w_qkv), (out_w, w_out), (norm_in, norm), (logsum_in, logsum)]
        )
    ]
    own_res = [
        pltpu.make_async_copy(
            results.at[m, 0],
            res_half.at[m, :, pl.ds(pl.multiple_of(my_z * chunk, 16), chunk)],
            load_sem.at[4 + m],
        )
        for m in range(micros)
    ]
    home_res = [
        pltpu.make_async_copy(
            res_half.at[m, :, pl.ds(0, part)], acts.at[m, my_tp], load_sem.at[4 + micros + m]
        )
        for m in range(micros)
    ]

    def fetch(index, tiles):
        j, p = tiles[index]
        return pltpu.make_async_copy(
            rights[j].at[:, pl.ds(pl.multiple_of(parts[p] * cols, 128), cols)],
            tile_in.at[index % 2],
            tile_sem.at[index % 2],
        )

    def fetch_left(index, todo):
        j, i, piece = todo[index]
        return pltpu.make_async_copy(
            lefts[j][i].at[pl.ds(piece * depth, depth)], stage.at[index % 2], stage_sem.at[index % 2]
        )

    def left_pieces(chunks):
        return [
            (j, i, piece)
            for j in chunks
            for i in range(len(lefts[j]))
            for piece in range(all_rows // depth)
        ]

    def turn(chunk, todo):
        for index, (j, i, piece) in enumerate(todo):
            if j == chunk:
                fetch_left(index, todo).wait()
                turned[slots[j][i], :, piece * depth : (piece + 1) * depth] = stage[index % 2].T
                if index + 2 < len(todo):
                    fetch_left(index + 2, todo).start()

    def product(index, tiles):
        j, p = tiles[index]
        fetch(index, tiles).wait()
        if index + 1 < len(tiles):
            fetch(index + 1, tiles).start()
        right = tile_in.at[index % 2]
        if p >= 2:
            firsts[j][p - 2].wait_recv()

        for lo in range(0, cols, WIDE):
            at = slice(lo, lo + WIDE)
            value = dot(turned[slots[j][0]], right[:, at], NN)
            if len(slots[j]) == 2 and lo + WIDE > 3 * cols // 4:
                other = dot(turned[slots[j][1]], right[:, at], NN)
                lane_index = lax.broadcasted_iota(jnp.int32, (depth, WIDE), 1) + lo
                value = jnp.where(lane_index >= 3 * cols // 4, other, value)
            if p < 2:
                sent[place[j], p, :, at] = value.astype(BF)
            else:
                value = value + got1[j, p - 2, :, at].astype(F32)
                held[place[j], p - 2, :, at] = value.astype(BF)

        if p < 2:
            firsts[j][p].start()
        else:
            for lane, (k, _, _, y_first) in enumerate(lanes):
                if k == j and (y_first or p == 2):
                    seconds[lane][p - 2].start()

    def after_second(lane):
        j, lo, count, y_first = lanes[lane]
        at = pl.ds(lo, count)
        spot = held.at[place[j]]
        if y_first:
            for p in (0, 1):
                seconds[lane][p].wait_recv()

                def body(rows, p=p):
                    mine = pl.ds(pl.multiple_of(rows.start + my_y * half, STEP), STEP)
                    there = pl.ds(pl.multiple_of(rows.start + p * half, STEP), STEP)
                    value = spot[p, mine, at].astype(F32) + got2[j, there, at].astype(F32)
                    spot[p, mine, at] = value.astype(BF)

                blocks(half, body)
                if p == 0:
                    thirds[lane].start()
        else:
            seconds[lane][0].wait_recv()

            def body(rows):
                value = spot[1, rows, at].astype(F32) + got2[j, rows, at].astype(F32)
                spot[1, rows, at] = value.astype(BF)

            blocks(depth, body)
            thirds[lane].start()

    def after_third(lane):
        j, lo, count, _ = lanes[lane]
        at = pl.ds(lo, count)
        thirds[lane].wait_recv()

        def body(rows):
            mine = pl.ds(pl.multiple_of(rows.start + my_y * half, STEP), STEP)
            value = held[place[j], 1, mine, at].astype(F32) + got3[j, rows, at].astype(F32)
            total[j, rows, at] = value.astype(BF)

        blocks(half, body)
        start_all(fourths[lane])

    def after_fourth(lane):
        j, lo, count, _ = lanes[lane]
        at = pl.ds(lo, count)
        value = total[j, pl.ds(pl.multiple_of(my_z * own, 16), own), at].astype(F32)
        for r in range(1, n_z):
            fourths[lane][r - 1].wait_recv()
            value = value + got4[j, r - 1, :, at].astype(F32)
        out[j, :, at] = value

    tiles = [(j, p) for j in range(3) for p in (0, 1)] + [(j, p) for j in range(3) for p in (2, 3)]
    todo = left_pieces([0, 1, 2])
    fetch_left(0, todo).start()
    fetch(0, tiles).start()
    fetch_left(1, todo).start()
    for copy in loads + own_res:
        copy.start()
    turn(0, todo)
    pl.semaphore_wait(barrier, len(peers))
    start_all(res_z[0] + res_z[1])
    for index in range(len(tiles)):
        product(index, tiles)
        if index in (1, 3):
            turn((index + 1) // 2, todo)

    for copy in loads:
        copy.wait()
    frame_total = micros * frames

    def frame_loads(f, slot):
        buf = tile_in.at[slot]
        m, at = f // frames, lax.rem(f, frames)
        pairs = [
            (xs.at[f], buf.at[pl.ds(0, places)]),
            (mixed_in.at[f], buf.at[pl.ds(places, places)]),
        ]
        pairs += [
            (
                qkv_in.at[f, :, pl.ds(i * width, width)],
                buf.at[pl.ds((2 + i) * places, places)],
            )
            for i in range(3)
        ]
        pairs += [
            (
                grads.at[m, r, at],
                buf.at[pl.ds(pl.multiple_of(5 * places + (my_z ^ r) * chunk, 16), chunk)],
            )
            for r in range(n_z)
        ]
        return [
            pltpu.make_async_copy(src, dst, frame_sem.at[slot, i])
            for i, (src, dst) in enumerate(pairs)
        ]

    def frame_stores(f, slot):
        rows = pl.ds(pl.multiple_of(f * places, 16), places)
        buf = turned.at[slot]
        pairs = [
            (
                buf.at[pl.ds(t * places, places), pl.ds(0, width)],
                cols_a.at[rows, pl.ds(t * cols, cols)],
            )
            for t in range(n_tp)
        ]
        pairs += [
            (buf.at[pl.ds(0, places), pl.ds(width, width)], normed_a.at[rows]),
            (buf.at[pl.ds(places, places), pl.ds(width, width)], low_a.at[rows]),
        ]
        return [
            pltpu.make_async_copy(src, dst, out_sem.at[slot, i])
            for i, (src, dst) in enumerate(pairs)
        ]

    grad = sent.at[1]
    for p in (0, 1):
        firsts[1][p].wait_send()
    tail_sum[...] = jnp.zeros_like(tail_sum)
    tail_sum[0, 2:6] = tail_time[...]
    start_all(frame_loads(0, 0))

    def frame(f, carry):
        slot = lax.rem(f, 2)

        @pl.when(f + 1 < frame_total)
        def _():
            start_all(frame_loads(f + 1, 1 - slot))

        @pl.when(f == 3)
        def _():
            after_second(0)

        @pl.when(f == 7)
        def _():
            after_third(0)

        for m in range(micros):

            @pl.when(f == 2 + 3 * m)
            def _(m=m):
                own_res[m].wait()
                arrive(res_z[m])
                start_all(res_tp[m])
                home_res[m].start()

        for copy in frame_loads(f, slot):
            copy.wait()

        @pl.when(f >= 2)
        def _():
            for copy in frame_stores(f - 2, slot):
                copy.wait()

        buf, keep = tile_in.at[slot], turned.at[slot]
        block = lambda i: slice(i * places, (i + 1) * places)
        unit, rate = normalise(buf[block(0)].astype(F32))
        keep[0:places, width : 2 * width] = (unit * norm[0:1] + norm[1:2]).astype(BF)
        low = buf[block(5)]
        keep[places : 2 * places, width : 2 * width] = low
        grad_mixed = dot(low, w_out[...], NN).astype(BF)
        for g in range(width // WIDE):
            at = slice(g * WIDE, (g + 1) * WIDE)
            back = attend_back(
                buf[block(2), at], buf[block(3), at], buf[block(4), at],
                grad_mixed[:, at], logsum[f, g : g + 1], None,
            )
            for i, value in enumerate(back):
                dqkv[:, i * width + g * WIDE : i * width + (g + 1) * WIDE] = value
        span = cols // 4
        for t in range(n_tp):
            for i in range(3):
                keep[block(t), i * span : (i + 1) * span] = dqkv[
                    :, i * width + t * span : i * width + (t + 1) * span
                ]
            keep[block(t), 3 * span : 4 * span] = buf[block(1), t * span : (t + 1) * span]
        start_all(frame_stores(f, slot))
        grad_normed = dot(dqkv[...], w_qkv[...], NT)
        tail_sum[0, 0:1] += jnp.sum(grad_normed * unit, axis=0, keepdims=True)
        tail_sum[0, 1:2] += jnp.sum(grad_normed, axis=0, keepdims=True)
        value = low.astype(F32) + norm_back(grad_normed, norm[0:1], unit, rate)
        m, at = f // frames, lax.rem(f, frames)
        grad[m, pl.ds(pl.multiple_of(at * places, 16), places), :] = value.astype(BF)
        for s in range(n_tp):
            src = grad.at[m, pl.ds(pl.multiple_of(at * places + s * part, 16), part)]
            dst = input_grad.at[m, my_tp, at]
            if s == 0:
                pltpu.make_async_copy(src, dst, i_send.at[0]).start()
            else:
                pltpu.make_async_remote_copy(
                    src_ref=src, dst_ref=dst, send_sem=i_send.at[s], recv_sem=i_recv.at[s],
                    device_id=to_tp[s], device_id_type=MESH,
                ).start()
        return carry

    lax.fori_loop(0, frame_total, frame, 0)
    for f in (frame_total - 2, frame_total - 1):
        for copy in frame_stores(f, f % 2):
            copy.wait()
    tails[0].start()

    for p in (0, 1):
        firsts[0][p].wait_send()
    last = [(3, p) for p in range(4)]
    todo = left_pieces([3])
    fetch_left(0, todo).start()
    fetch(0, last).start()
    fetch_left(1, todo).start()
    turn(3, todo)
    product(0, last)
    product(1, last)
    after_second(1)
    tails[0].wait_recv()
    tail_sum[1] = tail_sum[0] + tail_got[0]
    tails[1].start()
    for p in (0, 1):
        seconds[0][p].wait_send()
    thirds[0].wait_send()
    product(2, last)
    product(3, last)
    after_fourth(0)
    tails[1].wait_recv()
    tail_sum[2] = tail_sum[1] + tail_got[1]
    tails[2].start()
    after_second(2)
    after_second(3)
    after_second(4)
    after_third(1)
    after_fourth(1)
    tails[2].wait_recv()
    tail_sum[3] = tail_sum[2] + tail_got[2]
    start_all(tails[3:])
    after_third(3)
    after_third(4)
    after_third(2)
    after_fourth(2)
    value = tail_sum[3]
    for r in range(n_z - 1):
        tails[3 + r].wait_recv()
        value = value + tail_got[3 + r]
    tail_out[...] = value
    after_fourth(3)
    after_fourth(4)
    for m in range(micros):
        arrive(res_tp[m])
        home_res[m].wait()
    for s in range(n_tp):
        dst = input_grad.at[:, my_tp ^ s]
        if s == 0:
            pltpu.make_async_copy(dst, dst, i_send.at[0]).wait()
        else:
            for ref, wait in ((dst, "wait_send"), (dst, "wait_recv")):
                copy = pltpu.make_async_remote_copy(
                    src_ref=ref, dst_ref=ref, send_sem=i_send.at[s], recv_sem=i_recv.at[s],
                    device_id=to_tp[s], device_id_type=MESH,
                )
                getattr(copy, wait)()
    done = firsts[0] + firsts[1] + seconds[0] + [thirds[0]]
    for copy in remote.all:
        if not any(copy is other for other in done):
            copy.wait_send()


def back(results, grads, xs, qkv, mixed, logsum, qkv_w, out_w, norm, tail_time, kept):
    normed_time, columns, grad_time, normed_mlp, grad_pre, hidden, grad_result = kept
    micros, n_z, frames, chunk, width = results.shape
    n_tp = lax.axis_size("tp")
    places = chunk * n_z
    total = micros * frames
    rows = total * places
    depth, cols = width, columns.shape[1] // n_tp
    half, own = depth // 2, depth // (2 * n_z)
    part = places // n_tp
    any_spec = pl.BlockSpec(memory_space=pl.ANY)
    vmem = pl.BlockSpec(memory_space=pltpu.VMEM)
    dma = pltpu.SemaphoreType.DMA
    shape = jax.ShapeDtypeStruct
    home = shape((micros, n_tp, frames, part, width), BF)
    return pl.pallas_call(
        back_kernel,
        in_specs=[any_spec] * 9 + [vmem] + [any_spec] * 7,
        out_specs=[vmem] * 2 + [any_spec] * 6,
        out_shape=[
            shape((4, own, cols), F32),
            shape((8, width), F32),
            home,
            home,
            shape((rows, width), BF),
            shape((rows, width), BF),
            shape((rows, n_tp * cols), BF),
            shape((micros, frames, places, width), BF),
        ],
        scratch_shapes=[
            pltpu.VMEM((4, depth, rows), BF),
            pltpu.VMEM((2, depth, width), BF),
            pltpu.VMEM((2, rows, cols), BF),
            pltpu.VMEM((3, 2, depth, cols), BF),
            pltpu.VMEM((4, 2, depth, cols), BF),
            pltpu.VMEM((3, 2, depth, cols), BF),
            pltpu.VMEM((4, depth, cols), BF),
            pltpu.VMEM((4, half, cols), BF),
            pltpu.VMEM((4, half, cols), BF),
            pltpu.VMEM((4, n_z - 1, own, cols), BF),
            pltpu.VMEM((width, 3 * width), BF),
            pltpu.VMEM((width, width), BF),
            pltpu.VMEM((8, width), F32),
            pltpu.VMEM(logsum.shape, F32),
            pltpu.VMEM((places, 3 * width), BF),
            pltpu.VMEM((4, 8, width), F32),
            pltpu.VMEM((2 + n_z, 8, width), F32),
            dma((2,)),
            dma((2,)),
            dma((2, 5 + n_z)),
            dma((2, n_tp + 2)),
            dma((4 + 2 * micros,)),
            dma((N_REMOTE,)),
            dma((N_REMOTE,)),
            dma((1,)),
            dma((1,)),
            dma((n_tp,)),
            dma((n_tp,)),
        ],
        compiler_params=pltpu.CompilerParams(
            vmem_limit_bytes=60 * MIB, collective_id=5, has_side_effects=True
        ),
        cost_estimate=pl.CostEstimate(
            flops=2 * rows * width * 23 * width,
            bytes_accessed=rows * width * 60,
            transcendentals=0,
        ),
    )(
        results, grads, xs, qkv, mixed, logsum, qkv_w, out_w, norm, tail_time,
        normed_mlp, grad_pre, grad_result, hidden, normed_time, grad_time, columns,
    )


N_REMOTE = 96
N_LOCAL = 24


def front_kernel(
    inputs, cot, shard, ln_shard,
    xs_out, time_in, cot_half, cot_late, qkv_out, mixed_out, logsum_out,
    qkv_a, out_a, qkv_b, out_b, in_w, unit_w, norms,
    xs, sent, raw, std_qkv, std_out, ln, qkv, mixed,
    send, recv, t_send, t_recv, local,
):
    my_tp, my_y, my_z = lax.axis_index("tp"), lax.axis_index("clip"), lax.axis_index("fp")
    n_tp, n_z = lax.axis_size("tp"), lax.axis_size("fp")
    micros, _, frames, part, width = inputs.shape
    places = part * n_tp
    chunk = places // n_z
    own = shard.shape[1]
    half = n_z * own
    cols = shard.shape[2]
    to_tp = [{"tp": my_tp ^ s} for s in range(n_tp)]
    to_core, to_x = to_tp[1], to_tp[2]
    to_y = {"clip": my_y ^ 1}
    to_z = [{"fp": my_z ^ r} for r in range(n_z)]
    peers = to_tp[1:] + to_z[1:] + [to_y]
    barrier = pltpu.get_barrier_semaphore()
    for peer in peers:
        pl.semaphore_signal(barrier, inc=1, device_id=peer, device_id_type=MESH)

    remote = Copies(send, recv)
    locals_ = []

    def here(src, dst):
        copy = pltpu.make_async_copy(src, dst, local.at[len(locals_)])
        locals_.append(copy)
        copy.start()
        return copy

    tiles = [raw.at[0], raw.at[1], in_w, unit_w]
    mine = pl.multiple_of(my_y * half + my_z * own, 16)
    near = pl.multiple_of(my_y * half, 16)
    far = pl.multiple_of((1 - my_y) * half, 16)
    away = my_tp ^ 2
    cuts = [cols // 2, 5 * cols // 6, cols // 2, cols // 2]
    own_shards = []
    by_z, by_x, by_y, by_y2, by_x2, by_core = [], [], [], [], [], []
    for j, tile in enumerate(tiles):
        cut = cuts[j]
        one, two = pl.ds(0, cut), pl.ds(cut, cols - cut)
        own_rows, near_rows, far_rows = pl.ds(mine, own), pl.ds(near, half), pl.ds(far, half)

        def same(peer, *index, tile=tile):
            return remote.add(tile.at[index], tile.at[index], peer)

        by_z.append(
            [
                remote.add(shard.at[j], tile.at[my_tp, own_rows], to_z[r])
                for r in range(1, n_z)
            ]
        )
        by_x.append(same(to_x, my_tp, near_rows, one))
        by_y2.append(same(to_y, my_tp, near_rows, two))
        if j >= 2:
            continue
        by_y.append([same(to_y, my_tp, near_rows, one), same(to_y, away, near_rows, one)])
        by_x2.append(same(to_x, my_tp, slice(None), two))
        by_core.append(
            [
                same(to_core, my_tp, near_rows),
                same(to_core, away, near_rows, one),
                same(to_core, my_tp, far_rows, one),
                same(to_core, away, far_rows, one),
                same(to_core, my_tp, far_rows, two),
                same(to_core, away, slice(None), two),
            ]
        )
    ln_z = [
        remote.add(ln_shard, ln.at[pl.ds(mine, own)], to_z[r]) for r in range(1, n_z)
    ]
    ln_y = remote.add(ln.at[pl.ds(near, half)], ln.at[pl.ds(near, half)], to_y)
    x_in = [
        [
            remote.add(
                inputs.at[m, my_tp ^ s],
                xs.at[pl.ds(m * frames, frames), pl.ds(s * part, part)],
                to_tp[s],
            )
            for s in range(1, n_tp)
        ]
        for m in range(micros)
    ]
    cot_in = [
        [
            remote.add(cot.at[m, my_tp ^ s], half.at[:, pl.ds(s * part, part)], to_tp[s])
            for s in range(1, n_tp)
        ]
        for m, half in enumerate((cot_half, cot_late))
    ]
    own_x = [
        here(inputs.at[m, my_tp], xs.at[pl.ds(m * frames, frames), pl.ds(0, part)])
        for m in range(micros)
    ]
    own_cot = [
        here(cot.at[m, my_tp], half.at[:, pl.ds(0, part)])
        for m, half in enumerate((cot_half, cot_late))
    ]
    own_w = [here(shard.at[j], tile.at[my_tp, pl.ds(mine, own)]) for j, tile in enumerate(tiles)]
    own_ln = here(ln_shard, ln.at[pl.ds(mine, own)])

    pl.semaphore_wait(barrier, len(peers))
    start_all(by_z[0] + ln_z + x_in[0])

    def gather_start(j):
        own_w[j].wait()
        arrive(by_z[j])
        by_x[j].start()
        by_y2[j].start()
        if j < 2:
            by_core[j][0].start()

    def gather_first(j):
        by_x[j].wait_recv()
        start_all(by_y[j])
        by_core[j][1].start()

    def gather_second(j):
        by_y2[j].wait_recv()
        by_x2[j].start()
        by_core[j][4].start()

    def gather_last(j):
        arrive(by_y[j])
        start_all(by_core[j][2:4])
        by_x2[j].wait_recv()
        by_core[j][5].start()

    def standard(j):
        span = cols // 4
        for t in range(n_tp):
            for i in range(3):
                std_qkv[j, :, i * width + t * span : i * width + (t + 1) * span] = raw[
                    j, t, :, i * span : (i + 1) * span
                ]
            std_out[j, :, t * span : (t + 1) * span] = raw[j, t, :, 3 * span : 4 * span]

    gather_start(0)
    start_all(by_z[1] + by_z[2] + by_z[3])
    own_ln.wait()
    arrive(ln_z)
    ln_y.start()
    gather_first(0)
    gather_second(0)
    gather_start(1)
    start_all(cot_in[0] + x_in[1])
    gather_last(0)
    ln_y.wait_recv()
    norms[...] = ln[...].astype(F32).T[: norms.shape[0]]
    gather_start(2)
    gather_start(3)
    arrive(by_core[0])
    standard(0)
    gather_second(1)
    gather_first(1)
    own_x[0].wait()
    arrive(x_in[0])
    weights_out = [here(std_qkv.at[0], qkv_a), here(std_out.at[0], out_a)]

    def frame(f, carry):
        @pl.when(f == frames)
        def _():
            own_x[1].wait()
            arrive(x_in[1])
            start_all(cot_in[1])

        x = xs[f].astype(F32)
        unit, _ = normalise(x)
        normed = (unit * norms[0:1] + norms[1:2]).astype(BF)
        qkv[f] = dot(normed, std_qkv[0], NN).astype(BF)
        for g in range(width // WIDE):
            at = g * WIDE
            out, logsum = attend(
                qkv[f, :, at : at + WIDE],
                qkv[f, :, width + at : width + at + WIDE],
                qkv[f, :, 2 * width + at : 2 * width + at + WIDE],
                None,
            )
            mixed[f, :, at : at + WIDE] = out
            logsum_out[f, g : g + 1] = logsum
        sent[f] = (x + dot(mixed[f], std_out[0], NT)).astype(BF)
        m, at_frame = f // frames, lax.rem(f, frames)
        for r in range(n_z):
            src = sent.at[f, pl.ds(pl.multiple_of((my_z ^ r) * chunk, 16), chunk)]
            dst = time_in.at[m, r, at_frame]
            if r == 0:
                pltpu.make_async_copy(src, dst, t_send.at[m, 0]).start()
            else:
                pltpu.make_async_remote_copy(
                    src_ref=src, dst_ref=dst, send_sem=t_send.at[m, r],
                    recv_sem=t_recv.at[m, r], device_id=to_z[r], device_id_type=MESH,
                ).start()
        return carry

    lax.fori_loop(0, micros * frames, frame, 0)
    kept = [here(xs, xs_out), here(qkv, qkv_out), here(mixed, mixed_out)]
    gather_last(1)
    arrive(by_core[1])
    standard(1)
    weights_out += [here(std_qkv.at[1], qkv_b), here(std_out.at[1], out_b)]
    for j in (2, 3):
        by_x[j].wait_recv()
        by_y2[j].wait_recv()
    for m in range(micros):
        own_cot[m].wait()
        arrive(cot_in[m])
    for m in range(micros):
        for r in range(n_z):
            src = sent.at[
                pl.ds(m * frames, frames), pl.ds(pl.multiple_of((my_z ^ r) * chunk, 16), chunk)
            ]
            dst = time_in.at[m, r]
            if r == 0:
                pltpu.make_async_copy(src, dst, t_send.at[m, 0]).wait()
            else:
                pltpu.make_async_remote_copy(
                    src_ref=src, dst_ref=dst, send_sem=t_send.at[m, r],
                    recv_sem=t_recv.at[m, r], device_id=to_z[r], device_id_type=MESH,
                ).wait()
    for copy in remote.all:
        copy.wait_send()
    for copy in kept + weights_out:
        copy.wait()


def front(inputs, cot, shard, ln_shard):
    micros, clips, frames, part, width = inputs.shape
    n_tp, n_z = lax.axis_size("tp"), lax.axis_size("fp")
    places = part * n_tp
    total = micros * frames
    chunk = places // n_z
    cols = shard.shape[2]
    groups = width // WIDE
    any_spec = pl.BlockSpec(memory_space=pl.ANY)
    vmem = pl.BlockSpec(memory_space=pltpu.VMEM)
    dma = pltpu.SemaphoreType.DMA
    shape = jax.ShapeDtypeStruct
    weights = [(width, 3 * width), (width, width)] * 2 + [(n_tp, width, cols)] * 2
    return pl.pallas_call(
        front_kernel,
        in_specs=[any_spec] * 4,
        out_specs=[any_spec] * 6 + [vmem] + [any_spec] * 6 + [vmem],
        out_shape=[
            shape((total, places, width), BF),
            shape((micros, n_z, frames, chunk, width), BF),
            shape((frames, places, width), BF),
            shape((frames, places, width), BF),
            shape((total, places, 3 * width), BF),
            shape((total, places, width), BF),
            shape((total, groups, GROUP * places), F32),
        ]
        + [shape(dims, BF) for dims in weights]
        + [shape((8, width), F32)],
        scratch_shapes=[
            pltpu.VMEM((total, places, width), BF),
            pltpu.VMEM((total, places, width), BF),
            pltpu.VMEM((2, n_tp, width, cols), BF),
            pltpu.VMEM((2, width, 3 * width), BF),
            pltpu.VMEM((2, width, width), BF),
            pltpu.VMEM((width, ln_shard.shape[1]), BF),
            pltpu.VMEM((total, places, 3 * width), BF),
            pltpu.VMEM((total, places, width), BF),
            dma((N_REMOTE,)),
            dma((N_REMOTE,)),
            dma((micros, n_z)),
            dma((micros, n_z)),
            dma((N_LOCAL,)),
        ],
        compiler_params=pltpu.CompilerParams(
            vmem_limit_bytes=60 * MIB, collective_id=3, has_side_effects=True
        ),
        cost_estimate=pl.CostEstimate(
            flops=2 * total * places * width * 5 * width,
            bytes_accessed=total * places * width * 16,
            transcendentals=0,
        ),
    )(inputs, cot, shard, ln_shard)


def to_peer(value, axis, step):
    n = lax.axis_size(axis)
    return lax.ppermute(value, axis, [(i, i ^ step) for i in range(n)])


def swap(pieces, axis):
    return [piece if s == 0 else to_peer(piece, axis, s) for s, piece in enumerate(pieces)]


def pick(stack, index):
    return lax.dynamic_index_in_dim(stack, index, 0, keepdims=False)


def shards(
    inputs, cotangent, qkv_weight, out_spatial, out_temporal, mlp_in, mlp_out, ln_gain, ln_bias
):
    micros, clips, frames, local, width = inputs.shape
    n_tp, n_fp = lax.axis_size("tp"), lax.axis_size("fp")
    n_cf = lax.axis_size("clip") * n_fp
    assert clips == n_tp
    my_tp, my_fp = lax.axis_index("tp"), lax.axis_index("fp")
    depth = qkv_weight.shape[2]
    span = qkv_weight.shape[3]
    places = n_tp * local
    chunk = places // n_fp
    at = my_fp.astype(jnp.int32)[None]

    first = jnp.concatenate([qkv_weight[0, i] for i in range(3)] + [out_spatial.T], axis=1)
    second = jnp.concatenate([qkv_weight[1, i] for i in range(3)] + [out_temporal.T], axis=1)
    axes = ("clip", "fp", "tp")
    ln_rows = [v[i] for i in range(3) for v in (ln_gain, ln_bias)]
    whole_rows = depth % 16 == 0 and n_tp == 4 and lax.axis_size("clip") == 2 and micros == 2
    whole_rows = whole_rows and frames * places == width and span * 4 == width

    def from_chunks(chunks):
        stack = jnp.stack(chunks)
        joined = jnp.concatenate([pick(stack, my_fp ^ c) for c in range(n_fp)], axis=1)
        return [joined[:, s * local : (s + 1) * local] for s in range(n_tp)]

    def outward(pieces):
        stack = jnp.stack(swap(pieces, "tp"))
        return jnp.stack([pick(stack, my_tp ^ c) for c in range(n_tp)])

    mine = lax.axis_index("clip") * n_fp + my_fp
    kinds = lambda v: [v[:, i * span : (i + 1) * span] for i in range(4)]

    def arranged(acts, grad_input, late, space, norm_grads):
        norm_grads = norm_grads[:6].reshape(3, 2, n_cf, depth)
        norm_grads = lax.dynamic_index_in_dim(norm_grads, mine, 2, keepdims=False)
        space_g, time_g = kinds(space), kinds(late[2])
        return (
            acts,
            grad_input,
            jnp.stack([jnp.stack(space_g[:3]), jnp.stack(time_g[:3])]),
            space_g[3].T,
            time_g[3].T,
            late[0],
            late[1].T,
            norm_grads[:, 0],
            norm_grads[:, 1],
        )

    if whole_rows:
        ln_shard = jnp.stack(ln_rows + [jnp.zeros_like(ln_rows[0])] * 122, axis=1)
        shard = jnp.stack([first, second, mlp_in, mlp_out.T])
        (
            xs, time_pieces, cot_half, cot_late, qkv, mixed, logsum,
            qkv_space_w, out_space_w, qkv_time_w, out_time_w, in_w, unit_w, norms,
        ) = front(inputs, cotangent, shard, ln_shard)
        results, grads, _, *kept, tail = time_layer(
            [time_pieces], [cot_half, cot_late], qkv_time_w, out_time_w, in_w, unit_w, norms
        )
        sums, norm_grads, acts, input_grad, *_ = back(
            results, grads, xs, qkv, mixed, logsum, qkv_space_w, out_space_w, norms, tail, kept
        )
        return arranged(acts, input_grad.astype(F32), sums, sums[3], norm_grads)

    def gathered(part):
        return lax.all_gather(part, axes).reshape(n_cf, n_tp, depth, part.shape[1])

    def attention_weights(raw):
        raw = raw.reshape(n_cf, n_tp, depth, 4, span).transpose(3, 0, 2, 1, 4)
        raw = raw.reshape(4, n_cf * depth, n_tp * span)
        return jnp.concatenate([raw[0], raw[1], raw[2]], axis=1), raw[3]

    def unit_weights(raw):
        return raw.transpose(1, 0, 2, 3).reshape(n_tp, n_cf * depth, raw.shape[3])

    norms = lax.all_gather(jnp.stack(ln_rows), ("clip", "fp"))
    norms = norms.transpose(1, 0, 2).reshape(6, n_cf * depth).astype(F32)
    qkv_space_w, out_space_w = attention_weights(gathered(first))
    rest = gathered(jnp.concatenate([second, mlp_in, mlp_out.T], axis=1))
    qkv_time_w, out_time_w = attention_weights(rest[..., : 4 * span])
    in_w = unit_weights(rest[..., 4 * span : 4 * span + mlp_in.shape[1]])
    unit_w = unit_weights(rest[..., 4 * span + mlp_in.shape[1] :])

    def inward(array, m):
        return swap([pick(array[m], my_tp ^ s) for s in range(n_tp)], "tp")

    def to_chunks(pieces):
        joined = jnp.concatenate(pieces, axis=1)
        return [
            lax.dynamic_slice_in_dim(joined, (my_fp ^ r) * chunk, chunk, 1)
            for r in range(n_fp)
        ]

    space_kept, time_given = [], []
    for m in range(micros):
        x = inward(inputs, m)
        cots = swap(to_chunks(inward(cotangent, m)), "fp")
        out = space_forward(x, qkv_space_w, out_space_w, norms, at, n_fp)
        time_given.append((swap(out[:n_fp], "fp"), cots))
        space_kept.append((x,) + tuple(out[n_fp:]) + (0,))
    time_kept = []
    results = []
    space_grads = []
    for m in range(micros):
        pieces, cots = time_given[m]
        out = time_layer(pieces, cots, qkv_time_w, out_time_w, in_w, unit_w, norms)
        results.append(outward(from_chunks(swap(out[:n_fp], "fp"))))
        space_grads.append(swap(out[n_fp : 2 * n_fp], "fp"))
        time_kept.append(out[2 * n_fp :])
    space_rows = []
    input_grads = []
    flat = lambda v: v.reshape(-1, v.shape[-1])
    kept = lambda i: [k[i] for k in time_kept]
    time_chunks = [
        ([kept(3)], kept(4), True),
        ([kept(6)], kept(5), False),
        ([kept(0), kept(2)], kept(1), True),
    ]
    for m in range(micros):
        x, qkv, mixed, logsum, skip = space_kept[m]
        out = space_backward(
            x, space_grads[m], qkv, mixed, logsum, qkv_space_w, out_space_w, norms, at, skip, n_tp
        )
        input_grads.append(outward(out[:n_tp]).astype(F32))
        normed, low, columns, norm_grad = out[n_tp:]
        space_rows.append((flat(normed), flat(low), flat(columns), norm_grad))
    rows = lambda i: [k[i] for k in space_rows]
    space_chunk = ([rows(0), rows(1)], rows(2), True)
    early = scatter_grads([space_chunk], n_cf, n_tp)
    late = scatter_grads(time_chunks, n_cf, n_tp)
    norm_grads = lax.psum(jnp.concatenate([sum(rows(3)), sum(kept(7))]), axes)
    return arranged(jnp.stack(results), jnp.stack(input_grads), late, early[0], norm_grads)


def scatter_grads(chunks, n_cf, n_tp):
    tiles = []
    for lefts, rights, _ in chunks:
        cols = rights[0].shape[1] // n_tp
        total = sum(dot(a, b, TN) for a, b in zip(lefts[0], rights))
        total = total.reshape(total.shape[0], n_tp, cols)
        if len(lefts) == 2:
            other = sum(dot(a, b, TN) for a, b in zip(lefts[1], rights))
            other = other.reshape(other.shape[0], n_tp, cols)
            at = 3 * cols // 4
            total = jnp.concatenate([total[..., :at], other[..., at:]], axis=2)
        total = total.reshape(n_cf, total.shape[0] // n_cf, n_tp, cols).transpose(0, 2, 1, 3)
        tiles.append(total.reshape((n_cf * n_tp,) + total.shape[2:]))
    return lax.psum_scatter(jnp.stack(tiles, 1), ("clip", "fp", "tp"), scatter_dimension=0)


def solution(mesh):
    spread = P(None, "clip", "fp", "tp", None)
    return jax.shard_map(
        shards,
        mesh=mesh,
        in_specs=(
            spread,
            spread,
            P(None, None, ("clip", "fp"), "tp"),
            P("tp", ("clip", "fp")),
            P("tp", ("clip", "fp")),
            P(("clip", "fp"), "tp"),
            P("tp", ("clip", "fp")),
            P(None, ("clip", "fp")),
            P(None, ("clip", "fp")),
        ),
        out_specs=(
            spread,
            spread,
            P(None, None, ("clip", "fp"), "tp"),
            P("tp", ("clip", "fp")),
            P("tp", ("clip", "fp")),
            P(("clip", "fp"), "tp"),
            P("tp", ("clip", "fp")),
            P(None, ("clip", "fp")),
            P(None, ("clip", "fp")),
        ),
        check_vma=False,
    )
```
